32 devices in a mesh: seq: 8 (over y, x, core), tp: 4 (over z).
Axes of the slice: x: 2, y: 2, z: 4, core: 2. Of those that a mesh axis runs over, the one named last changes fastest.
Arguments:
- tokens: bfloat16 [8192, 1536], P(('seq', 'tp')), may hold values from -6 to 6
- lengths: int32 [6], replicated, may hold values from 1 to 6144, as said below
- first_gain: float32 [1536], replicated, may hold values from 0.5 to 1.5
- w_query: bfloat16 [1536, 1536], P(None, 'tp'), may hold values from -0.15625 to 0.15625
- w_keyval: bfloat16 [1536, 2, 768], P(None, None, 'tp'), may hold values from -0.15625 to 0.15625
- w_output: bfloat16 [1536, 1536], P('tp'), may hold values from -0.875 to 0.875
- second_gain: float32 [1536], replicated, may hold values from 0.5 to 1.5
- w_gateup: bfloat16 [1536, 2, 4096], P(None, None, 'tp'), may hold values from -0.15625 to 0.15625
- w_down: bfloat16 [4096, 1536], P('tp'), may hold values from -0.09375 to 0.09375
- cotangent: bfloat16 [8192, 1536], P(('seq', 'tp')), may hold values from -6 to 6
Outputs:
- result: bfloat16 [8192, 1536], P(('seq', 'tp'))
- tokens_grad: float32 [8192, 1536], P(('seq', 'tp'))
- first_gain_grad: float32 [1536], P(('seq', 'tp'))
- query_grad: float32 [1536, 1536], P('seq', 'tp')
- keyval_grad: float32 [1536, 2, 768], P('seq', None, 'tp')
- output_grad: float32 [1536, 1536], P('tp', 'seq')
- second_gain_grad: float32 [1536], P(('seq', 'tp'))
- gateup_grad: float32 [1536, 2, 4096], P('seq', None, 'tp')
- down_grad: float32 [4096, 1536], P('tp', 'seq')
The draws below stay inside these ranges and needn't reach their ends.
Inputs may be any that keep to these rules, and one draw needn't show every extreme that they name: 6 lengths in pack order summing to 8192; no document begins at a nonzero multiple of 1024; exactly one document has 6144 tokens and every other one fewer than 1024.
All inputs are finite; a program needn't handle non-finite values.
Results may differ from the reference program's by a relative error of at most 0.02.
Values may be sent and summed in bfloat16 or wider, within the bound.
No kernel may reach another device: no remote copies, remote signals or barrier semaphores. Data moves between devices by JAX's collectives and lax.ppermute only.
A program may use at most 192 MiB of HBM per device.

```python
import jax
import jax.numpy as jnp
from jax import lax

D = 1536
HEADS = 16
KV_HEADS = 8
HEAD_DIM = 96
FF = 4096
WINDOW = 1024
TOK_DEV = 1024
TOKENS = 8192
LONG_BLOCKS = 6
DOCS = 6


def draw_lengths(key, part):
    key = jax.random.fold_in(key, 7)
    first_key, second_key, place_key = jax.random.split(key, 3)
    block_count = TOKENS // TOK_DEV
    half_block = TOK_DEV // 2
    early_cut = jax.random.randint(first_key, (block_count,), 1, half_block + 1, dtype=jnp.int32)
    late_cut = jax.random.randint(second_key, (block_count,), half_block + 1, TOK_DEV, dtype=jnp.int32)
    begin_block = jax.random.randint(place_key, (), 0, block_count - LONG_BLOCKS, dtype=jnp.int32)
    end_block = (begin_block + LONG_BLOCKS).astype(jnp.int32)
    blocks_idx = jnp.arange(block_count, dtype=jnp.int32)
    early_cut = jnp.where(blocks_idx == end_block, jnp.take(early_cut, begin_block), early_cut).astype(jnp.int32)
    keep_early = jnp.logical_not((blocks_idx > begin_block) & (blocks_idx < end_block))
    keep_late = jnp.logical_not((blocks_idx >= begin_block) & (blocks_idx < end_block))
    places_all = jnp.stack([blocks_idx * TOK_DEV + early_cut, blocks_idx * TOK_DEV + late_cut], axis=1).reshape(-1)
    keep_all = jnp.stack([keep_early, keep_late], axis=1).reshape(-1)
    order = jnp.argsort(jnp.where(keep_all, 0, 1).astype(jnp.int32), stable=True)
    cuts = jnp.take(places_all, order[:DOCS - 1]).astype(jnp.int32)
    ends = jnp.concatenate([cuts, jnp.full((1,), TOKENS, jnp.int32)])
    starts = jnp.concatenate([jnp.zeros((1,), jnp.int32), cuts])
    return (ends - starts).astype(jnp.int32)


def raised(drawn, stream_key, source, target, blocks, factor):
    def block_of(axis_at):
        return (jnp.arange(drawn.shape[axis_at]) // (drawn.shape[axis_at] // blocks)).reshape((-1,) + (1,) * (drawn.ndim - 1 - axis_at))

    first = jax.random.permutation(stream_key, blocks)[block_of(target)]
    second = (block_of(target) + blocks // 2) % blocks
    return jnp.where((block_of(source) == first) | (block_of(source) == second), factor * drawn, drawn)


def level_of(key, shape, cuts, low, high):
    level = 1.0
    for dim, blocks in cuts:
        draws = jax.random.uniform(jax.random.fold_in(jax.random.fold_in(key, 6), dim), (blocks,), jnp.float32, low / len(cuts), high / len(cuts))
        level = level * jnp.repeat(jnp.exp(draws), shape[dim] // blocks).reshape((-1,) + (1,) * (len(shape) - 1 - dim))
    return level


def noise(stream_key, shape, scale, most, cuts=(), kind=jnp.bfloat16):
    values = jax.random.normal(stream_key, shape, jnp.float32) * scale
    if len(cuts) > 0:
        values = level_of(stream_key, shape, cuts, -0.22, 0.18) * values
    return jnp.clip(values, min=-most, max=most).astype(kind)


def noise_with(stream_key, extent, scale, limit, pieces, heavy, held_as=jnp.bfloat16):
    values = scale * jax.random.normal(stream_key, extent, jnp.float32)
    if pieces:
        values = values * level_of(stream_key, extent, pieces, -0.22, 0.18)
    return jnp.clip(raised(values, jax.random.fold_in(stream_key, 3), *heavy), -limit, limit).astype(held_as)


def setup_inputs(seed: int = 0) -> dict:
    key_of = jax.random.split(jax.random.key(seed), 11)
    tokens = noise(key_of[0], (TOKENS, D), 1.0, 6.0, ((0, 32),))
    lengths = draw_lengths(jax.random.fold_in(key_of[10], 71), 0)
    first_gain = jnp.clip(1.0 + 0.1 * jax.random.normal(key_of[2], (D,), jnp.float32), 0.5, 1.5)
    w_query = noise(key_of[3], (D, HEADS * HEAD_DIM), D ** -0.5, 0.15625, ((1, 4),))
    w_keyval = noise(key_of[4], (D, 2, KV_HEADS * HEAD_DIM), D ** -0.5, 0.15625, ((2, 4),))
    w_output = noise(key_of[5], (HEADS * HEAD_DIM, D), (HEADS * HEAD_DIM // 32) ** -0.5, 0.875, ((0, 4),))
    second_gain = jnp.clip(1.0 + 0.1 * jax.random.normal(key_of[6], (D,), jnp.float32), 0.5, 1.5)
    w_gateup = noise(key_of[7], (D, 2, FF), D ** -0.5, 0.15625, ((2, 4),))
    w_down = noise(key_of[8], (FF, D), FF ** -0.5, 0.09375, ((0, 4),))
    cotangent = noise_with(key_of[9], (TOKENS, D), 1.0, 6.0, ((0, 32),), (0, 1, 32, 2.75))
    return {"tokens": tokens, "lengths": lengths, "first_gain": first_gain, "w_query": w_query, "w_keyval": w_keyval, "w_output": w_output, "second_gain": second_gain, "w_gateup": w_gateup, "w_down": w_down, "cotangent": cotangent}


EPSILON = 1e-05
THETA = 100000.0
HIGH = lax.Precision.HIGHEST

@jax.custom_vjp
def low(v):
    return lax.optimization_barrier(v.astype(jnp.bfloat16)).astype(jnp.float32)

@jax.custom_vjp
def low_back(v):
    return v

def low_keep(v):
    return (low(v), None)

def low_pass(kept, grad):
    return (grad,)

def back_keep(v):
    return (v, None)

def back_low(kept, grad):
    return (low(grad),)
low.defvjp(low_keep, low_pass)
low_back.defvjp(back_keep, back_low)

def doc_places(lengths, token_ids):
    bounds = jnp.cumsum(lengths).astype(jnp.int32)
    passed = token_ids[:, None] >= bounds[None, :]
    segment = lax.optimization_barrier(jnp.sum(passed.astype(jnp.int32), axis=1)).astype(jnp.int32)
    begins = lax.optimization_barrier(jnp.sum(jnp.where(passed, lengths[None, :], 0), axis=1)).astype(jnp.int32)
    return (segment, (token_ids - begins).astype(jnp.int32))

def rotate(values, places):
    half = values.shape[-1] // 2
    freqs = THETA ** (-2.0 * jnp.arange(half, dtype=jnp.float32) / values.shape[-1])
    angles = places.astype(jnp.float32)[:, None] * freqs[None, :]
    cosine = jnp.cos(angles)[:, None, :]
    sine = jnp.sin(angles)[:, None, :]
    first = values[..., :half]
    second = values[..., half:]
    return jnp.concatenate([first * cosine - second * sine, second * cosine + first * sine], axis=-1)

def rms_scale(rows, gain):
    return rows * lax.rsqrt(lax.optimization_barrier(jnp.mean(rows * rows, axis=-1, keepdims=True)) + EPSILON) * gain

def swiglu(both):
    return jax.nn.silu(both[:, 0]) * both[:, 1]

def matmul(left, right):
    return jnp.dot(left, right, precision=HIGH, preferred_element_type=jnp.float32)

def window_mask(query_ids, query_seg, key_ids, key_seg):
    return (query_seg[:, None] == key_seg[None, :]) & (key_ids[None, :] <= query_ids[:, None]) & (query_ids[:, None] - key_ids[None, :] < WINDOW) & (key_ids[None, :] >= 0)

def reference(tokens, lengths, first_gain, w_query, w_keyval, w_output, second_gain, w_gateup, w_down, cotangent):
    block = min(512, TOK_DEV)
    span = WINDOW + block
    group = HEADS // KV_HEADS
    kvwidth = KV_HEADS * HEAD_DIM
    scale = HEAD_DIM ** (-0.5)
    token_ids = jnp.arange(TOKENS, dtype=jnp.int32)
    segment, places = doc_places(lengths, token_ids)
    padded_ids = (jnp.arange(TOKENS + WINDOW, dtype=jnp.int32) - WINDOW).astype(jnp.int32)
    padded_seg, unused = doc_places(lengths, padded_ids)

    def attend(queries, keys, values):
        filler = jnp.zeros((WINDOW, KV_HEADS, HEAD_DIM), jnp.float32)
        keys_pad = jnp.concatenate([filler, keys], axis=0)
        values_pad = jnp.concatenate([filler, values], axis=0)

        def one_block(index):
            start = (index * block).astype(jnp.int32)
            query_block = lax.dynamic_slice_in_dim(queries, start, block, 0).reshape(block, KV_HEADS, group, HEAD_DIM)
            key_block = lax.dynamic_slice_in_dim(keys_pad, start, span, 0)
            value_block = lax.dynamic_slice_in_dim(values_pad, start, span, 0)
            mask = window_mask(lax.dynamic_slice_in_dim(token_ids, start, block, 0), lax.dynamic_slice_in_dim(segment, start, block, 0), lax.dynamic_slice_in_dim(padded_ids, start, span, 0), lax.dynamic_slice_in_dim(padded_seg, start, span, 0))
            scores = jnp.einsum('qkgd,skd->kgqs', query_block, key_block, precision=HIGH, preferred_element_type=jnp.float32) * scale
            scores = jnp.where(mask, low_back(scores), -1e+30)
            top = lax.optimization_barrier(jnp.max(scores, axis=-1, keepdims=True))
            weights = jnp.exp(scores - top)
            probs = low(weights / lax.optimization_barrier(jnp.sum(weights, axis=-1, keepdims=True)))
            mixed = jnp.einsum('kgqs,skd->qkgd', probs, value_block, precision=HIGH, preferred_element_type=jnp.float32)
            return mixed.reshape(block, HEADS * HEAD_DIM)
        outs = lax.map(jax.checkpoint(one_block), jnp.arange(TOKENS // block, dtype=jnp.int32))
        return outs.reshape(TOKENS, HEADS * HEAD_DIM)

    def forward(resid, gain_one, weight_query, weight_keyval, weight_output, gain_two, weight_gateup, weight_down):
        inputs_one = low(rms_scale(resid, gain_one))
        query_flat = low_back(matmul(inputs_one, weight_query))
        keyval_flat = low_back(matmul(inputs_one, weight_keyval.reshape(D, 2 * kvwidth)))
        queries = low(rotate(query_flat.reshape(TOKENS, HEADS, HEAD_DIM), places))
        keys = low(rotate(keyval_flat[:, :kvwidth].reshape(TOKENS, KV_HEADS, HEAD_DIM), places))
        values = low(keyval_flat[:, kvwidth:].reshape(TOKENS, KV_HEADS, HEAD_DIM))
        heads_out = low_back(low(attend(queries, keys, values)))
        resid_two = resid + low_back(matmul(heads_out, weight_output))
        inputs_two = low(rms_scale(resid_two, gain_two))
        gateup = low_back(matmul(inputs_two, weight_gateup.reshape(D, 2 * FF))).reshape(TOKENS, 2, FF)
        hidden = low(swiglu(gateup))
        return resid_two + low_back(matmul(hidden, weight_down))
    result, backward = jax.vjp(forward, tokens.astype(jnp.float32), first_gain, w_query.astype(jnp.float32), w_keyval.astype(jnp.float32), w_output.astype(jnp.float32), second_gain, w_gateup.astype(jnp.float32), w_down.astype(jnp.float32))
    grads = backward(cotangent.astype(jnp.float32))
    return (result.astype(jnp.bfloat16), grads[0], grads[1], grads[2], grads[3], grads[4], grads[5], grads[6], grads[7])
```

```python
import jax
import jax.numpy as jnp
from jax import lax
from jax.experimental import pallas as pl
from jax.experimental.pallas import tpu as pltpu
from jax.sharding import PartitionSpec as P

HEAD_DIM = 96
HALF = HEAD_DIM // 2
LANES = 128
WINDOW = 1024
TILE = 256
EPSILON = 1e-05
THETA = 100000.0
SCALE = HEAD_DIM ** (-0.5)
LOG2E = 1.4426950408889634
SCALE2 = SCALE * LOG2E
BF = jnp.bfloat16
F32 = jnp.float32
NT = (((1,), (1,)), ((), ()))
NN = (((1,), (0,)), ((), ()))
TN = (((0,), (0,)), ((), ()))
MIB = 1 << 20


def dot(a, b, dims=NN):
    return lax.dot_general(a, b, dims, preferred_element_type=F32)


def doc_places(lengths, token_ids):
    bounds = jnp.cumsum(lengths)
    passed = token_ids[:, None] >= bounds[None, :]
    return jnp.sum(jnp.where(passed, lengths[None, :], 0), axis=1)


def spread_halves(w):
    n = w.shape[0]
    parts = w.reshape(n, -1, 2, HALF)
    parts = jnp.pad(parts, ((0, 0), (0, 0), (0, 0), (0, LANES // 2 - HALF)))
    return parts.reshape(n, -1)


def gather_halves(w):
    n = w.shape[0]
    return w.reshape(n, -1, 2, LANES // 2)[..., :HALF].reshape(n, -1)


def spread_heads(w):
    n = w.shape[0]
    parts = w.reshape(n, -1, HEAD_DIM)
    return jnp.pad(parts, ((0, 0), (0, 0), (0, LANES - HEAD_DIM))).reshape(n, -1)


def gather_heads(w):
    n = w.shape[0]
    return w.reshape(n, -1, LANES)[..., :HEAD_DIM].reshape(n, -1)


def rotation_tables(places):
    freqs = THETA ** (-2.0 * jnp.arange(HALF, dtype=F32) / HEAD_DIM)
    angles = places.astype(F32)[:, None] * freqs[None, :]
    cosine = jnp.pad(jnp.cos(angles), ((0, 0), (0, LANES // 2 - HALF)))
    sine = jnp.pad(jnp.sin(angles), ((0, 0), (0, LANES // 2 - HALF)))
    return (
        jnp.concatenate([cosine, cosine], axis=1),
        jnp.concatenate([-sine, sine], axis=1),
    )


def turn(u, cosine, sine):
    return u * cosine + pltpu.roll(u, LANES // 2, 1) * sine


def project_kernel(heads, x_ref, g_ref, w_ref, c_ref, s_ref, h_ref, q_ref, kv_ref):
    qheads, kvheads = heads
    x = x_ref[...].astype(F32)
    scale = lax.rsqrt(jnp.mean(x * x, axis=-1, keepdims=True) + EPSILON)
    h = (x * scale * g_ref[...]).astype(BF)
    h_ref[...] = h
    flat = dot(h, w_ref[...])
    cosine, sine = c_ref[...], s_ref[...]
    for n in range(qheads):
        q_ref[:, n * LANES : (n + 1) * LANES] = turn(
            flat[:, n * LANES : (n + 1) * LANES], cosine, sine
        ).astype(BF)
    for n in range(kvheads):
        at = (qheads + n) * LANES
        kv_ref[:, n * LANES : (n + 1) * LANES] = turn(
            flat[:, at : at + LANES], cosine, sine
        ).astype(BF)
    kv_ref[:, kvheads * LANES :] = flat[:, (qheads + kvheads) * LANES :].astype(BF)


def project(x_all, gain, weight, cosine, sine, qheads, kvheads):
    rows, width = x_all.shape
    tile = min(TILE, rows)
    wide = weight.shape[1]
    row = lambda n: pl.BlockSpec((tile, n), lambda i: (i, 0))
    whole = lambda m, n: pl.BlockSpec((m, n), lambda i: (0, 0))
    return pl.pallas_call(
        lambda *refs: project_kernel((qheads, kvheads), *refs),
        grid=(rows // tile,),
        in_specs=[row(width), whole(1, width), whole(width, wide), row(LANES), row(LANES)],
        out_specs=[row(width), row(qheads * LANES), row(2 * kvheads * LANES)],
        out_shape=[
            jax.ShapeDtypeStruct((rows, width), BF),
            jax.ShapeDtypeStruct((rows, qheads * LANES), BF),
            jax.ShapeDtypeStruct((rows, 2 * kvheads * LANES), BF),
        ],
        compiler_params=pltpu.CompilerParams(vmem_limit_bytes=40 * MIB),
        cost_estimate=pl.CostEstimate(
            flops=2 * rows * width * wide, bytes_accessed=4 * rows * width, transcendentals=0
        ),
    )(x_all, gain.reshape(1, width), weight, cosine, sine)


def masked(raw, first_key, lo, diagonal, query_ids):
    keys = first_key + lax.broadcasted_iota(jnp.int32, raw.shape, 0)
    ok = keys >= lo
    if diagonal:
        ok = ok & (keys <= query_ids)
    return jnp.where(ok, raw, -1e30)


def attend_kernel(q_ref, kp_ref, ko_ref, vp_ref, vo_ref, lo_ref, o_ref, l_ref, k_s, v_s):
    head, t = pl.program_id(0), pl.program_id(1)
    rows = ko_ref.shape[0]
    chunks = WINDOW // TILE + 1

    @pl.when(t == 0)
    def _():
        k_s[:rows] = kp_ref[...]
        k_s[rows:] = ko_ref[...]
        v_s[:rows] = vp_ref[...]
        v_s[rows:] = vo_ref[...]

    q = jnp.concatenate([q_ref[:, :LANES], q_ref[:, LANES:]], axis=0)
    lo = jnp.concatenate([lo_ref[...], lo_ref[...]], axis=1)
    ids = rows + t * TILE + lax.broadcasted_iota(jnp.int32, (1, TILE), 1)
    ids = jnp.concatenate([ids, ids], axis=1)
    scores = []
    for c in range(chunks):
        first = pl.multiple_of((t + c) * TILE, TILE)
        raw = dot(k_s[pl.ds(first, TILE)], q, NT)
        scores.append(masked(raw, first, lo, c == chunks - 1, ids))
    top = scores[0].max(axis=0, keepdims=True)
    for s in scores[1:]:
        top = jnp.maximum(top, s.max(axis=0, keepdims=True))
    top = top * SCALE2
    total = jnp.zeros_like(top)
    mixed = jnp.zeros((LANES, 2 * TILE), F32)
    for c in range(chunks):
        first = pl.multiple_of((t + c) * TILE, TILE)
        p = jnp.exp2(scores[c] * SCALE2 - top)
        total = total + jnp.sum(p, axis=0, keepdims=True)
        mixed = mixed + dot(v_s[pl.ds(first, TILE)], p.astype(BF), TN)
    l_ref[0, 0] = top + jnp.log2(total)
    out = jnp.transpose(mixed / total).astype(BF)
    first_row = pl.multiple_of(t * TILE, TILE)
    for n in range(2):

        @pl.when(head == n)
        def _():
            for g in range(2):
                at = (2 * n + g) * HEAD_DIM
                o_ref[pl.ds(first_row, TILE), at : at + HEAD_DIM] = out[
                    g * TILE : (g + 1) * TILE, :HEAD_DIM
                ]


def attend(queries, pair_before, pair_here, lo, kvheads):
    rows = queries.shape[0]
    tiles = rows // TILE
    key = lambda off: pl.BlockSpec((rows, LANES), lambda h, t: (0, h + off))
    return pl.pallas_call(
        attend_kernel,
        grid=(kvheads, tiles),
        in_specs=[
            pl.BlockSpec((TILE, 2 * LANES), lambda h, t: (t, h)),
            key(0),
            key(0),
            key(kvheads),
            key(kvheads),
            pl.BlockSpec((1, TILE), lambda h, t: (0, t)),
        ],
        out_specs=[
            pl.BlockSpec((rows, 2 * kvheads * HEAD_DIM), lambda h, t: (0, 0)),
            pl.BlockSpec((1, 1, 1, 2 * TILE), lambda h, t: (h, t, 0, 0)),
        ],
        out_shape=[
            jax.ShapeDtypeStruct((rows, 2 * kvheads * HEAD_DIM), BF),
            jax.ShapeDtypeStruct((kvheads, tiles, 1, 2 * TILE), F32),
        ],
        scratch_shapes=[pltpu.VMEM((2 * rows, LANES), BF), pltpu.VMEM((2 * rows, LANES), BF)],
        compiler_params=pltpu.CompilerParams(vmem_limit_bytes=40 * MIB),
        cost_estimate=pl.CostEstimate(
            flops=16 * MIB * 400, bytes_accessed=6 * MIB, transcendentals=5 * MIB
        ),
    )(queries, pair_before, pair_here, pair_before, pair_here, lo)


def attend_back_kernel(
    q_ref, kp_ref, ko_ref, vp_ref, vo_ref, lo_ref, o_ref, l_ref, do_ref, c_ref, s_ref,
    dq_ref, dkp_ref, dvp_ref, dk_ref, dv_ref, k_s, v_s, dk_s, dv_s,
):
    head, t = pl.program_id(0), pl.program_id(1)
    rows = ko_ref.shape[0]
    chunks = WINDOW // TILE + 1

    @pl.when(t == 0)
    def _():
        k_s[:rows] = kp_ref[...]
        k_s[rows:] = ko_ref[...]
        v_s[:rows] = vp_ref[...]
        v_s[rows:] = vo_ref[...]
        dk_s[...] = jnp.zeros_like(dk_s)
        dv_s[...] = jnp.zeros_like(dv_s)

    def heads_of(ref):
        both = ref[...]
        pair = jnp.where(head == 0, both[:, : 2 * HEAD_DIM], both[:, 2 * HEAD_DIM :])
        fill = jnp.zeros((TILE, LANES - HEAD_DIM), BF)
        return jnp.concatenate(
            [
                jnp.concatenate([pair[:, :HEAD_DIM], fill], axis=1),
                jnp.concatenate([pair[:, HEAD_DIM:], fill], axis=1),
            ],
            axis=0,
        )

    q = jnp.concatenate([q_ref[:, :LANES], q_ref[:, LANES:]], axis=0)
    lo = jnp.concatenate([lo_ref[...], lo_ref[...]], axis=1)
    ids = rows + t * TILE + lax.broadcasted_iota(jnp.int32, (1, TILE), 1)
    ids = jnp.concatenate([ids, ids], axis=1)
    grad = heads_of(do_ref)
    prod = grad.astype(F32) * heads_of(o_ref).astype(F32)
    center = jnp.sum(jnp.transpose(prod), axis=0, keepdims=True)
    logs = l_ref[0, 0]
    dq = jnp.zeros((LANES, 2 * TILE), F32)
    for c in range(chunks):
        first = pl.multiple_of((t + c) * TILE, TILE)
        here = pl.ds(first, TILE)
        keys = k_s[here]
        raw = masked(dot(keys, q, NT), first, lo, c == chunks - 1, ids)
        p = jnp.exp2(raw * SCALE2 - logs)
        dp = dot(v_s[here], grad, NT)
        ds = (p * (dp - center)).astype(BF)
        dv_s[here] += dot(p.astype(BF), grad)
        dk_s[here] += dot(ds, q)
        dq = dq + dot(keys, ds, TN)
    dq = jnp.transpose(dq) * SCALE
    cosine, sine = c_ref[...], -s_ref[...]
    for g in range(2):
        dq_ref[:, g * LANES : (g + 1) * LANES] = turn(
            dq[g * TILE : (g + 1) * TILE], cosine, sine
        ).astype(BF)

    @pl.when(t == pl.num_programs(1) - 1)
    def _():
        dkp_ref[...] = (dk_s[:rows] * SCALE).astype(BF)
        dvp_ref[...] = dv_s[:rows].astype(BF)
        dk_ref[...] = dk_s[rows:] * SCALE
        dv_ref[...] = dv_s[rows:]


def attend_back(queries, pair_before, pair_here, lo, heads_out, logs, grads, cosine, sine, kvheads):
    rows = queries.shape[0]
    tiles = rows // TILE
    key = lambda off: pl.BlockSpec((rows, LANES), lambda h, t: (0, h + off))
    tile_of = lambda n: pl.BlockSpec((TILE, n), lambda h, t: (t, 0))
    qtile = pl.BlockSpec((TILE, 2 * LANES), lambda h, t: (t, h))
    wide = kvheads * LANES
    return pl.pallas_call(
        attend_back_kernel,
        grid=(kvheads, tiles),
        in_specs=[
            qtile,
            key(0),
            key(0),
            key(kvheads),
            key(kvheads),
            pl.BlockSpec((1, TILE), lambda h, t: (0, t)),
            tile_of(2 * kvheads * HEAD_DIM),
            pl.BlockSpec((1, 1, 1, 2 * TILE), lambda h, t: (h, t, 0, 0)),
            tile_of(2 * kvheads * HEAD_DIM),
            tile_of(LANES),
            tile_of(LANES),
        ],
        out_specs=[qtile, key(0), key(0), key(0), key(0)],
        out_shape=[
            jax.ShapeDtypeStruct((rows, 2 * wide), BF),
            jax.ShapeDtypeStruct((rows, wide), BF),
            jax.ShapeDtypeStruct((rows, wide), BF),
            jax.ShapeDtypeStruct((rows, wide), F32),
            jax.ShapeDtypeStruct((rows, wide), F32),
        ],
        scratch_shapes=[
            pltpu.VMEM((2 * rows, LANES), BF),
            pltpu.VMEM((2 * rows, LANES), BF),
            pltpu.VMEM((2 * rows, LANES), F32),
            pltpu.VMEM((2 * rows, LANES), F32),
        ],
        compiler_params=pltpu.CompilerParams(vmem_limit_bytes=48 * MIB),
        cost_estimate=pl.CostEstimate(
            flops=16 * MIB * 1000, bytes_accessed=12 * MIB, transcendentals=5 * MIB
        ),
    )(
        queries, pair_before, pair_here, pair_before, pair_here, lo, heads_out, logs, grads,
        cosine, sine,
    )


def passed_along(shard, axis, by):
    size = lax.axis_size(axis)
    pairs = [(i, i + by) for i in range(size) if 0 <= i + by < size]
    return lax.ppermute(shard, axis, pairs)


def rms_scale(rows, gain):
    return rows * lax.rsqrt(jnp.mean(rows * rows, axis=-1, keepdims=True) + EPSILON) * gain


def swiglu(both):
    return jax.nn.silu(both[:, 0]) * both[:, 1]


def body(
    tokens, lengths, first_gain, w_query, w_keyval, w_output, second_gain, w_gateup, w_down,
    cotangent,
):
    owned, width = tokens.shape
    rows = owned * lax.axis_size("tp")
    qheads = w_query.shape[1] // HEAD_DIM
    kvheads = w_keyval.shape[2] // HEAD_DIM
    units = w_down.shape[0]
    start_id = lax.axis_index("seq") * rows
    query_ids = start_id + jnp.arange(rows, dtype=jnp.int32)
    begins = doc_places(lengths, query_ids)
    cosine, sine = rotation_tables(query_ids - begins)
    lo = jnp.maximum(query_ids - (WINDOW - 1), begins) - (start_id - rows)
    lo = lo.reshape(1, rows)
    weight_one = jnp.concatenate(
        [spread_halves(w_query), spread_halves(w_keyval[:, 0]), spread_heads(w_keyval[:, 1])],
        axis=1,
    )
    resid = tokens.astype(F32)
    x_all = lax.all_gather(tokens, "tp", axis=0, tiled=True)
    inputs_one, queries, pair_here = project(
        x_all, first_gain, weight_one, cosine, sine, qheads, kvheads
    )
    pair_before = passed_along(pair_here, "seq", 1)
    heads_out, logs = attend(queries, pair_before, pair_here, lo, kvheads)
    branch_one = lax.psum_scatter(
        dot(heads_out, w_output).astype(BF), "tp", scatter_dimension=0, tiled=True
    ).astype(F32)
    resid_two = resid + branch_one
    normed_two, second_back = jax.vjp(rms_scale, resid_two, second_gain)
    inputs_two = lax.all_gather(normed_two.astype(BF), "tp", axis=0, tiled=True)
    gateup_weight = w_gateup.reshape(width, 2 * units)
    gateup = dot(inputs_two, gateup_weight).reshape(rows, 2, units)
    activated, swiglu_back = jax.vjp(swiglu, gateup)
    hidden = activated.astype(BF)
    branch_two = lax.psum_scatter(
        dot(hidden, w_down).astype(BF), "tp", scatter_dimension=0, tiled=True
    ).astype(F32)
    result = (resid_two + branch_two).astype(BF)
    cotangent_all = lax.all_gather(cotangent, "tp", axis=0, tiled=True)
    hidden_grad = dot(cotangent_all, w_down, NT)
    down_grad = dot(hidden, cotangent_all, TN)
    (gateup_grad_full,) = swiglu_back(hidden_grad)
    gateup_low = gateup_grad_full.reshape(rows, 2 * units).astype(BF)
    gateup_grad = dot(inputs_two, gateup_low, TN).reshape(width, 2, units)
    second_input = lax.psum_scatter(
        dot(gateup_low, gateup_weight, NT).astype(BF), "tp", scatter_dimension=0, tiled=True
    ).astype(F32)
    resid_two_part, second_gain_grad = second_back(second_input)
    resid_two_grad = cotangent.astype(F32) + resid_two_part
    branch_all = lax.all_gather(resid_two_grad.astype(BF), "tp", axis=0, tiled=True)
    heads_grad = dot(branch_all, w_output, NT).astype(BF)
    output_grad = dot(heads_out, branch_all, TN)

    dq, dk_before, dv_before, dk_here, dv_here = attend_back(
        queries, pair_before, pair_here, lo, heads_out, logs, heads_grad, cosine, sine, kvheads
    )
    returned = passed_along(
        jnp.concatenate([dk_before, dv_before], axis=1), "seq", -1
    ).astype(F32)
    wide = kvheads * LANES
    dk = (dk_here + returned[:, :wide]).reshape(rows, kvheads, LANES)
    dk = dk * cosine[:, None, :] - jnp.roll(dk, LANES // 2, axis=2) * sine[:, None, :]
    dv = dv_here + returned[:, wide:]
    grads_one = jnp.concatenate(
        [dq, dk.reshape(rows, wide).astype(BF), dv.astype(BF)], axis=1
    )
    weight_grad = dot(inputs_one, grads_one, TN).astype(BF)
    query_grad = gather_halves(weight_grad[:, : qheads * LANES])
    keyval_grad = jnp.stack(
        [
            gather_halves(weight_grad[:, qheads * LANES : qheads * LANES + wide]),
            gather_heads(weight_grad[:, qheads * LANES + wide :]),
        ],
        axis=1,
    )
    first_input = lax.psum_scatter(
        dot(grads_one, weight_one, NT).astype(BF), "tp", scatter_dimension=0, tiled=True
    ).astype(F32)
    _, first_back = jax.vjp(rms_scale, resid, first_gain)
    resid_part, first_gain_grad = first_back(first_input)
    tokens_grad = resid_two_grad + resid_part
    both_axes = ("seq", "tp")
    scatter = lambda a, axis, dim: lax.psum_scatter(a, axis, scatter_dimension=dim, tiled=True)
    return (
        result,
        tokens_grad,
        scatter(first_gain_grad, both_axes, 0),
        scatter(query_grad, "seq", 0).astype(F32),
        scatter(keyval_grad, "seq", 0).astype(F32),
        scatter(output_grad.astype(BF), "seq", 1).astype(F32),
        scatter(second_gain_grad, both_axes, 0),
        scatter(gateup_grad.astype(BF), "seq", 0).astype(F32),
        scatter(down_grad.astype(BF), "seq", 1).astype(F32),
    )


def solution(mesh):
    both = ("seq", "tp")
    return jax.shard_map(
        body,
        mesh=mesh,
        in_specs=(
            P(both, None), P(), P(), P(None, "tp"), P(None, None, "tp"), P("tp", None), P(),
            P(None, None, "tp"), P("tp", None), P(both, None),
        ),
        out_specs=(
            P(both, None), P(both, None), P(both), P("seq", "tp"), P("seq", None, "tp"),
            P("tp", "seq"), P(both), P("seq", None, "tp"), P("tp", "seq"),
        ),
        check_vma=False,
    )
```

```python
import jax
import jax.numpy as jnp
from jax import lax
from jax.experimental import pallas as pl
from jax.experimental.pallas import tpu as pltpu
from jax.sharding import PartitionSpec as P

HEAD_DIM = 96
HALF = HEAD_DIM // 2
LANES = 128
WINDOW = 1024
TILE = 256
EPSILON = 1e-05
THETA = 100000.0
SCALE = HEAD_DIM ** (-0.5)
LOG2E = 1.4426950408889634
SCALE2 = SCALE * LOG2E
BF = jnp.bfloat16
F32 = jnp.float32
NT = (((1,), (1,)), ((), ()))
NN = (((1,), (0,)), ((), ()))
TN = (((0,), (0,)), ((), ()))
MIB = 1 << 20
AXES = ("seq", "tp")
ANY = pl.BlockSpec(memory_space=pl.ANY)


def dot(a, b, dims=NN):
    return lax.dot_general(a, b, dims, preferred_element_type=F32)


def shape(dims, dtype):
    return jax.ShapeDtypeStruct(dims, dtype)


def cost(flops, moved, exps=0):
    return pl.CostEstimate(flops=flops, bytes_accessed=moved, transcendentals=exps)


def params(mib):
    return pltpu.CompilerParams(vmem_limit_bytes=mib * MIB)


def send(a, to):
    size, ways = lax.axis_size("seq"), lax.axis_size("tp")
    pairs = []
    for s in range(size):
        for t in range(ways):
            there = to(s, t)
            if there is not None and 0 <= there[0] < size and 0 <= there[1] < ways:
                pairs.append((s * ways + t, there[0] * ways + there[1]))
    return lax.ppermute(a, AXES, pairs)


def doc_places(lengths, token_ids):
    bounds = jnp.cumsum(lengths)
    passed = token_ids[:, None] >= bounds[None, :]
    return jnp.sum(jnp.where(passed, lengths[None, :], 0), axis=1)


def spread_halves(w):
    n = w.shape[0]
    parts = w.reshape(n, -1, 2, HALF)
    parts = jnp.pad(parts, ((0, 0), (0, 0), (0, 0), (0, LANES // 2 - HALF)))
    return parts.reshape(n, -1)


def rotation_tables(places):
    freqs = THETA ** (-2.0 * jnp.arange(HALF, dtype=F32) / HEAD_DIM)
    angles = places.astype(F32)[:, None] * freqs[None, :]
    return jnp.cos(angles), jnp.sin(angles)


def lane_tables(cosine, sine):
    fill = ((0, 0), (0, LANES // 2 - HALF))
    cosine, sine = jnp.pad(cosine, fill), jnp.pad(sine, fill)
    return (
        jnp.concatenate([cosine, cosine], axis=1),
        jnp.concatenate([-sine, sine], axis=1),
    )


def project_kernel(
    sizes, sc_ref, own, r1, r2, r3, l1, l2, l3, g_ref, w_ref, c_ref, s_ref,
    h_ref, q_ref, kv_ref, x_s, sem,
):
    qheads, kvheads, ways = sizes
    o = pl.program_id(0)
    j = sc_ref[0]
    sources = {0: own, -1: r1, -2: r2, -3: r3, 1: l1, 2: l2, 3: l3}

    def fetch(at, slot):
        for d, ref in sources.items():

            @pl.when(at - j == d)
            def _():
                pltpu.make_async_copy(ref, x_s.at[slot], sem.at[slot]).start()

    @pl.when(o == 0)
    def _():
        fetch(0, 0)

    slot = lax.rem(o, 2)

    @pl.when(o + 1 < ways)
    def _():
        fetch(o + 1, 1 - slot)

    pltpu.make_async_copy(own, x_s.at[slot], sem.at[slot]).wait()
    x = x_s[slot].astype(F32)
    scale = lax.rsqrt(jnp.mean(x * x, axis=-1, keepdims=True) + EPSILON)
    h = (x * scale * g_ref[...]).astype(BF)
    h_ref[...] = h
    flat = dot(h, w_ref[...])
    cosine, sine = c_ref[...], s_ref[...]

    def turned(n):
        u = flat[:, n * LANES : (n + 1) * LANES]
        u = u * cosine + pltpu.roll(u, LANES // 2, 1) * sine
        return jnp.concatenate([u[:, :HALF], u[:, LANES // 2 : LANES // 2 + HALF]], axis=1)

    fill = jnp.zeros((x.shape[0], LANES - HEAD_DIM), F32)
    for n in range(qheads):
        q_ref[:, n * LANES : (n + 1) * LANES] = jnp.concatenate([turned(n), fill], axis=1).astype(
            BF
        )
    keys = [turned(qheads + n) for n in range(kvheads)]
    values = [flat[:, (qheads + kvheads) * LANES :]]
    kv_ref[...] = jnp.concatenate(keys + values, axis=1).astype(BF)


def project(sc, shards, gain, weight, cosine, sine, qheads, kvheads):
    owned, width = shards[0].shape
    ways = 4
    rows = owned * ways
    wide = weight.shape[1]
    kvwide = 2 * kvheads * HEAD_DIM
    row = lambda n: pl.BlockSpec((owned, n), lambda o, sc: (o, 0))
    whole = lambda m, n: pl.BlockSpec((m, n), lambda o, sc: (0, 0))
    return pl.pallas_call(
        lambda *refs: project_kernel((qheads, kvheads, ways), *refs),
        grid_spec=pltpu.PrefetchScalarGridSpec(
            num_scalar_prefetch=1,
            grid=(ways,),
            in_specs=[ANY] * 7 + [whole(1, width), whole(width, wide), row(LANES), row(LANES)],
            out_specs=[row(width), row(qheads * LANES), row(kvwide)],
            scratch_shapes=[pltpu.VMEM((2, owned, width), BF), pltpu.SemaphoreType.DMA((2,))],
        ),
        out_shape=[
            shape((rows, width), BF),
            shape((rows, qheads * LANES), BF),
            shape((rows, kvwide), BF),
        ],
        compiler_params=params(32),
        cost_estimate=cost(2 * rows * width * wide, 4 * rows * width),
    )(sc, *shards, gain.reshape(1, width), weight, cosine, sine)


def masked(raw, first_key, lo, diagonal, query_ids):
    keys = first_key + lax.broadcasted_iota(jnp.int32, raw.shape, 0)
    ok = keys >= lo
    if diagonal:
        ok = ok & (keys <= query_ids)
    return jnp.where(ok, raw, -1e30)


def load_pairs(kp_ref, ko_ref, k_s, v_s, head, kvheads):
    rows = ko_ref.shape[0]

    @pl.when(head == 0)
    def _():
        k_s[...] = jnp.zeros_like(k_s)
        v_s[...] = jnp.zeros_like(v_s)

    for n in range(kvheads):

        @pl.when(head == n)
        def _():
            for place, ref in ((0, kp_ref), (rows, ko_ref)):
                at = n * HEAD_DIM
                k_s[place : place + rows, :HEAD_DIM] = ref[:, at : at + HEAD_DIM]
                at = (kvheads + n) * HEAD_DIM
                v_s[place : place + rows, :HEAD_DIM] = ref[:, at : at + HEAD_DIM]


def tile_parts(q_ref, lo_ref, rows, t):
    q = jnp.concatenate([q_ref[:, :LANES], q_ref[:, LANES:]], axis=0)
    lo = jnp.concatenate([lo_ref[...], lo_ref[...]], axis=1)
    ids = rows + t * TILE + lax.broadcasted_iota(jnp.int32, (1, TILE), 1)
    return q, lo, jnp.concatenate([ids, ids], axis=1)


def attend_kernel(kvheads, q_ref, kp_ref, ko_ref, lo_ref, o_ref, l_ref, k_s, v_s):
    head, t = pl.program_id(0), pl.program_id(1)
    rows = ko_ref.shape[0]
    chunks = WINDOW // TILE + 1

    @pl.when(t == 0)
    def _():
        load_pairs(kp_ref, ko_ref, k_s, v_s, head, kvheads)

    q, lo, ids = tile_parts(q_ref, lo_ref, rows, t)
    scores = []
    for c in range(chunks):
        first = pl.multiple_of((t + c) * TILE, TILE)
        raw = dot(k_s[pl.ds(first, TILE)], q, NT)
        scores.append(masked(raw, first, lo, c == chunks - 1, ids))
    top = scores[0].max(axis=0, keepdims=True)
    for s in scores[1:]:
        top = jnp.maximum(top, s.max(axis=0, keepdims=True))
    top = top * SCALE2
    total = jnp.zeros_like(top)
    mixed = jnp.zeros((LANES, 2 * TILE), F32)
    for c in range(chunks):
        first = pl.multiple_of((t + c) * TILE, TILE)
        p = jnp.exp2(scores[c] * SCALE2 - top)
        total = total + jnp.sum(p, axis=0, keepdims=True)
        mixed = mixed + dot(v_s[pl.ds(first, TILE)], p.astype(BF), TN)
    l_ref[0, 0] = top + jnp.log2(total)
    out = jnp.transpose(mixed / total).astype(BF)
    here = pl.ds(pl.multiple_of(t * TILE, TILE), TILE)
    for n in range(kvheads):

        @pl.when(head == n)
        def _():
            for g in range(2):
                at = (2 * n + g) * HEAD_DIM
                o_ref[here, at : at + HEAD_DIM] = out[g * TILE : (g + 1) * TILE, :HEAD_DIM]


def attend(queries, pair_before, pair_here, lo, kvheads):
    rows = queries.shape[0]
    tiles = rows // TILE
    whole = pl.BlockSpec((rows, 2 * kvheads * HEAD_DIM), lambda h, t: (0, 0))
    return pl.pallas_call(
        lambda *refs: attend_kernel(kvheads, *refs),
        grid=(kvheads, tiles),
        in_specs=[
            pl.BlockSpec((TILE, 2 * LANES), lambda h, t: (t, h)),
            whole,
            whole,
            pl.BlockSpec((1, TILE), lambda h, t: (0, t)),
        ],
        out_specs=[whole, pl.BlockSpec((1, 1, 1, 2 * TILE), lambda h, t: (h, t, 0, 0))],
        out_shape=[
            shape((rows, 2 * kvheads * HEAD_DIM), BF),
            shape((kvheads, tiles, 1, 2 * TILE), F32),
        ],
        scratch_shapes=[pltpu.VMEM((2 * rows, LANES), BF), pltpu.VMEM((2 * rows, LANES), BF)],
        compiler_params=params(32),
        cost_estimate=cost(6400 * MIB, 5 * MIB, 5 * MIB),
    )(queries, pair_before, pair_here, lo)


def attend_back_kernel(
    kvheads, sc_ref, q_ref, kp_ref, ko_ref, lo_ref, o_ref, l_ref, g0_ref, g1_ref, g2_ref, g3_ref,
    c_ref, s_ref, dq_ref, dp_ref, dkv_ref, k_s, v_s, dk_s, dv_s,
):
    head, t = pl.program_id(0), pl.program_id(1)
    rows = ko_ref.shape[0]
    chunks = WINDOW // TILE + 1

    @pl.when(t == 0)
    def _():
        load_pairs(kp_ref, ko_ref, k_s, v_s, head, kvheads)
        dk_s[...] = jnp.zeros_like(dk_s)
        dv_s[...] = jnp.zeros_like(dv_s)

    def heads_of(both):
        pair = both[:, : 2 * HEAD_DIM]
        for n in range(1, kvheads):
            pair = jnp.where(
                head == n, both[:, 2 * n * HEAD_DIM : 2 * (n + 1) * HEAD_DIM], pair
            )
        fill = jnp.zeros((TILE, LANES - HEAD_DIM), BF)
        first = jnp.concatenate([pair[:, :HEAD_DIM], fill], axis=1)
        second = jnp.concatenate([pair[:, HEAD_DIM:], fill], axis=1)
        return jnp.concatenate([first, second], axis=0)

    q, lo, ids = tile_parts(q_ref, lo_ref, rows, t)
    apart = t ^ sc_ref[0]
    grad = g0_ref[0]
    for d, ref in ((1, g1_ref), (2, g2_ref), (3, g3_ref)):
        grad = jnp.where(apart == d, ref[...], grad)
    grad = heads_of(grad)
    prod = grad.astype(F32) * heads_of(o_ref[...]).astype(F32)
    center = jnp.sum(jnp.transpose(prod), axis=0, keepdims=True)
    logs = l_ref[0, 0]
    dq = jnp.zeros((LANES, 2 * TILE), F32)
    for c in range(chunks):
        first = pl.multiple_of((t + c) * TILE, TILE)
        here = pl.ds(first, TILE)
        keys = k_s[here]
        raw = masked(dot(keys, q, NT), first, lo, c == chunks - 1, ids)
        p = jnp.exp2(raw * SCALE2 - logs)
        dp = dot(v_s[here], grad, NT)
        ds = (p * (dp - center)).astype(BF)
        dv_s[here] += dot(p.astype(BF), grad)
        dk_s[here] += dot(ds, q)
        dq = dq + dot(keys, ds, TN)
    cosine = jnp.concatenate([c_ref[...], c_ref[...]], axis=1)
    sine = jnp.concatenate([s_ref[...], s_ref[...]], axis=1)
    a, b = dq[:HALF] * SCALE, dq[HALF:HEAD_DIM] * SCALE
    fill = jnp.zeros((LANES - HEAD_DIM, 2 * TILE), F32)
    dq = jnp.concatenate([a * cosine + b * sine, b * cosine - a * sine, fill], axis=0)
    dq = jnp.transpose(dq).astype(BF)
    mine = pl.ds(pl.multiple_of(t * TILE, TILE), TILE)
    last = t == pl.num_programs(1) - 1
    for n in range(kvheads):

        @pl.when(head == n)
        def _():
            for g in range(2):
                at = (2 * n + g) * HEAD_DIM
                dq_ref[mine, at : at + HEAD_DIM] = dq[g * TILE : (g + 1) * TILE, :HEAD_DIM]

        @pl.when((head == n) & last)
        def _():
            at = n * HEAD_DIM
            dp_ref[:, at : at + HEAD_DIM] = (dk_s[:rows, :HEAD_DIM] * SCALE).astype(BF)
            dkv_ref[:, at : at + HEAD_DIM] = dk_s[rows:, :HEAD_DIM] * SCALE
            at = (kvheads + n) * HEAD_DIM
            dp_ref[:, at : at + HEAD_DIM] = dv_s[:rows, :HEAD_DIM].astype(BF)
            dkv_ref[:, at : at + HEAD_DIM] = dv_s[rows:, :HEAD_DIM]


def attend_back(sc, queries, pair_before, pair_here, lo, heads_out, logs, grads, tables, kvheads):
    rows = queries.shape[0]
    tiles = rows // TILE
    wide = 2 * kvheads * HEAD_DIM
    whole = pl.BlockSpec((rows, wide), lambda h, t, sc: (0, 0))
    table = pl.BlockSpec((HALF, TILE), lambda h, t, sc: (0, t))
    piece = pl.BlockSpec((TILE, wide), lambda h, t, sc: (0, 0))
    return pl.pallas_call(
        lambda *refs: attend_back_kernel(kvheads, *refs),
        grid_spec=pltpu.PrefetchScalarGridSpec(
            num_scalar_prefetch=1,
            grid=(kvheads, tiles),
            in_specs=[
                pl.BlockSpec((TILE, 2 * LANES), lambda h, t, sc: (t, h)),
                whole,
                whole,
                pl.BlockSpec((1, TILE), lambda h, t, sc: (0, t)),
                pl.BlockSpec((TILE, wide), lambda h, t, sc: (t, 0)),
                pl.BlockSpec((1, 1, 1, 2 * TILE), lambda h, t, sc: (h, t, 0, 0)),
                pl.BlockSpec((1, TILE, wide), lambda h, t, sc: (sc[0], 0, 0)),
                piece,
                piece,
                piece,
                table,
                table,
            ],
            out_specs=[whole, whole, whole],
            scratch_shapes=[
                pltpu.VMEM((2 * rows, LANES), BF),
                pltpu.VMEM((2 * rows, LANES), BF),
                pltpu.VMEM((2 * rows, LANES), F32),
                pltpu.VMEM((2 * rows, LANES), F32),
            ],
        ),
        out_shape=[shape((rows, wide), BF), shape((rows, wide), BF), shape((rows, wide), F32)],
        compiler_params=params(40),
        cost_estimate=cost(16000 * MIB, 8 * MIB, 5 * MIB),
    )(sc, queries, pair_before, pair_here, lo, heads_out, logs, *grads, *tables)


def mix_kernel(
    sc_ref, o0_ref, o1_ref, o2_ref, o3_ref, w_ref, x_ref, xr_ref, xl_ref, g_ref,
    x2_ref, h2_ref, row_ref,
):
    m = pl.program_id(0)
    j = sc_ref[0]
    parts = [o0_ref[...], o1_ref[...], o2_ref[...], o3_ref[...]]
    acc = dot(parts[0], w_ref[j])
    for d in (1, 2, 3):
        acc = acc + dot(parts[d], w_ref[j ^ d])
    other = jnp.where((j & 1) == 1, xr_ref[...], xl_ref[...])
    x2 = jnp.where(m == 1, x_ref[...], other).astype(F32) + acc
    x2_ref[0] = x2
    scale = lax.rsqrt(jnp.mean(x2 * x2, axis=-1, keepdims=True) + EPSILON)
    h2_ref[0] = (x2 * scale * g_ref[...]).astype(BF)

    @pl.when(m == 1)
    def _():
        row_ref[...] = jnp.concatenate(parts, axis=1)


def mix(sc, heads_out, others, weight, tokens, right, left, gain):
    owned, width = tokens.shape
    local = heads_out.shape[1]
    ways = weight.shape[0]
    part = pl.BlockSpec((owned, local), lambda m, sc: ((sc[0] & 1) ^ 1 ^ m, 0))
    whole = lambda *dims: pl.BlockSpec(dims, lambda m, sc: (0,) * len(dims))
    return pl.pallas_call(
        mix_kernel,
        grid_spec=pltpu.PrefetchScalarGridSpec(
            num_scalar_prefetch=1,
            grid=(2,),
            in_specs=[
                pl.BlockSpec((owned, local), lambda m, sc: (sc[0] ^ 1 ^ m, 0)),
                part,
                part,
                part,
                whole(ways, local, width),
                whole(owned, width),
                whole(owned, width),
                whole(owned, width),
                whole(1, width),
            ],
            out_specs=[
                pl.BlockSpec((1, owned, width), lambda m, sc: (m, 0, 0)),
                pl.BlockSpec((1, owned, width), lambda m, sc: (m, 0, 0)),
                whole(owned, ways * local),
            ],
        ),
        out_shape=[
            shape((2, owned, width), F32),
            shape((2, owned, width), BF),
            shape((owned, ways * local), BF),
        ],
        compiler_params=params(40),
        cost_estimate=cost(4 * owned * ways * local * width, 12 * MIB),
    )(sc, heads_out, *others, weight, tokens, right, left, gain.reshape(1, width))


def feed_kernel(
    sc_ref, ho_ref, hs_ref, co_ref, cs_ref, gu_own, d_own, gu0, gu1, gu2, gu3, d0, d1, d2, d3,
    a_ref, dg_ref, du_ref, y_ref, dh_ref, gu_s, d_s, y_s, dh_s, sem,
):
    r = pl.program_id(0)
    steps = pl.num_programs(0)
    place, odd = sc_ref[1], sc_ref[2]
    taken = [(gu0, d0), (gu1, d1), (gu2, d2), (gu3, d3)]
    span = d_s.shape[1]

    def fetch(at, slot):
        @pl.when(odd == 0)
        def _():
            first = pl.multiple_of((place ^ at) * span, span)
            pltpu.make_async_copy(
                gu_own.at[:, :, pl.ds(first, span)], gu_s.at[slot], sem.at[0, slot]
            ).start()
            pltpu.make_async_copy(
                d_own.at[pl.ds(first, span)], d_s.at[slot], sem.at[1, slot]
            ).start()

        for k, (gu, d) in enumerate(taken):

            @pl.when((odd == 1) & (at == k))
            def _():
                pltpu.make_async_copy(gu, gu_s.at[slot], sem.at[0, slot]).start()
                pltpu.make_async_copy(d, d_s.at[slot], sem.at[1, slot]).start()

    @pl.when(r == 0)
    def _():
        fetch(0, 0)
        y_s[...] = jnp.zeros_like(y_s)
        dh_s[...] = jnp.zeros_like(dh_s)

    slot = lax.rem(r, 2)

    @pl.when(r + 1 < steps)
    def _():
        fetch(r + 1, 1 - slot)

    pltpu.make_async_copy(gu0, gu_s.at[slot], sem.at[0, slot]).wait()
    pltpu.make_async_copy(d0, d_s.at[slot], sem.at[1, slot]).wait()
    h = jnp.concatenate([hs_ref[0], ho_ref[0]], axis=0)
    ct = jnp.concatenate([cs_ref[0], co_ref[0]], axis=0)
    gate_w, up_w, down_w = gu_s[slot, 0], gu_s[slot, 1], d_s[slot]
    gate = dot(h, gate_w)
    up = dot(h, up_w)
    da = dot(ct, down_w, NT)
    sig = jax.nn.sigmoid(gate)
    act = gate * sig
    a = (act * up).astype(BF)
    dgate = (da * up * sig * (1.0 + gate * (1.0 - sig))).astype(BF)
    dup = (da * act).astype(BF)
    a_ref[...] = a
    dg_ref[...] = dgate
    du_ref[...] = dup
    y_s[...] += dot(a, down_w)
    dh_s[...] += dot(dgate, gate_w, NT) + dot(dup, up_w, NT)

    @pl.when(r == steps - 1)
    def _():
        half = y_ref.shape[1]
        for k in range(2):
            y_ref[k] = y_s[k * half : (k + 1) * half].astype(BF)
            dh_ref[k] = dh_s[k * half : (k + 1) * half].astype(BF)


def feed(m, sc, h_own, h_sib, ct_own, ct_sib, gu_own, d_own, gu_taken, d_taken):
    _, owned, width = h_own.shape
    units = d_own.shape[0]
    span = units // 4
    rows = pl.BlockSpec((1, owned, width), lambda r, sc: (m, 0, 0))
    out = pl.BlockSpec((2 * owned, span), lambda r, sc: (0, sc[1] ^ r))
    whole = pl.BlockSpec((2, owned, width), lambda r, sc: (0, 0, 0))
    return pl.pallas_call(
        feed_kernel,
        grid_spec=pltpu.PrefetchScalarGridSpec(
            num_scalar_prefetch=1,
            grid=(4,),
            in_specs=[rows] * 4 + [ANY] * 10,
            out_specs=[out, out, out, whole, whole],
            scratch_shapes=[
                pltpu.VMEM((2, 2, width, span), BF),
                pltpu.VMEM((2, span, width), BF),
                pltpu.VMEM((2 * owned, width), F32),
                pltpu.VMEM((2 * owned, width), F32),
                pltpu.SemaphoreType.DMA((2, 2)),
            ],
        ),
        out_shape=[shape((2 * owned, units), BF)] * 3 + [shape((2, owned, width), BF)] * 2,
        compiler_params=params(48),
        cost_estimate=cost(36 * owned * width * units, 22 * MIB, 2 * owned * units),
    )(sc, h_own, h_sib, ct_own, ct_sib, gu_own, d_own, *gu_taken, *d_taken)


def feed_grad_kernel(
    sc_ref, ho_ref, hs_ref, co_ref, cs_ref, a0, dg0, du0, a1, dg1, du1, gu_ref, d_ref
):
    h = jnp.concatenate([hs_ref[0], ho_ref[0], hs_ref[1], ho_ref[1]], axis=0)
    ct = jnp.concatenate([cs_ref[0], co_ref[0], cs_ref[1], co_ref[1]], axis=0)
    both = lambda x, y: jnp.concatenate([x[...], y[...]], axis=0)
    gu_ref[0] = dot(h, both(dg0, dg1), TN).astype(BF)
    gu_ref[1] = dot(h, both(du0, du1), TN).astype(BF)
    d_ref[...] = dot(ct, both(a0, a1), TN).astype(BF)


def feed_grad(r, sc, h_own, h_sib, ct_own, ct_sib, first, second):
    _, owned, width = h_own.shape
    units = first[0].shape[1]
    part = width // 4
    cut = 2
    lanes = pl.BlockSpec((2, owned, part), lambda n, sc: (0, 0, sc[1] ^ r))
    right = pl.BlockSpec((2 * owned, units // cut), lambda n, sc: (0, n))
    return pl.pallas_call(
        feed_grad_kernel,
        grid_spec=pltpu.PrefetchScalarGridSpec(
            num_scalar_prefetch=1,
            grid=(cut,),
            in_specs=[lanes] * 4 + [right] * 6,
            out_specs=[
                pl.BlockSpec((2, part, units // cut), lambda n, sc: (0, 0, n)),
                pl.BlockSpec((part, units // cut), lambda n, sc: (0, n)),
            ],
        ),
        out_shape=[shape((2, part, units), BF), shape((part, units), BF)],
        compiler_params=params(40),
        cost_estimate=cost(24 * owned * part * units, 12 * MIB),
    )(sc, h_own, h_sib, ct_own, ct_sib, *first, *second)


def norm_back(dn, v, gain):
    r = lax.rsqrt(jnp.mean(v * v, axis=-1, keepdims=True) + EPSILON)
    scaled = gain * dn
    gain_grad = jnp.sum(dn * (v * r), axis=0, keepdims=True)
    return r * scaled - v * (r * r * r) * jnp.mean(scaled * v, axis=-1, keepdims=True), gain_grad


def turn_back_kernel(
    sc_ref, a_ref, b_ref, z_ref, x2_ref, ct_ref, g_ref, w_ref, dx_ref, db_ref, do_ref, gain_ref
):
    dn = a_ref[0].astype(F32) + b_ref[...].astype(F32) + z_ref[...].astype(F32)
    dv, gain_grad = norm_back(dn, x2_ref[0], g_ref[...])
    gain_ref[...] = gain_grad
    dx = ct_ref[...].astype(F32) + dv
    dx_ref[...] = dx
    low = dx.astype(BF)
    db_ref[...] = low
    for k in range(w_ref.shape[0]):
        do_ref[k] = dot(low, w_ref[k], NT).astype(BF)


def turn_back(sc, mine, core, tp, x2, cotangent, gain, weight):
    owned, width = cotangent.shape
    ways, local, _ = weight.shape
    whole = lambda *dims: pl.BlockSpec(dims, lambda n, sc: (0,) * len(dims))
    own = pl.BlockSpec((1, owned, width), lambda n, sc: (1, 0, 0))
    return pl.pallas_call(
        turn_back_kernel,
        grid_spec=pltpu.PrefetchScalarGridSpec(
            num_scalar_prefetch=1,
            grid=(1,),
            in_specs=[
                own,
                whole(owned, width),
                whole(owned, width),
                own,
                whole(owned, width),
                whole(1, width),
                whole(ways, local, width),
            ],
            out_specs=[
                whole(owned, width),
                whole(owned, width),
                whole(ways, owned, local),
                whole(1, width),
            ],
        ),
        out_shape=[
            shape((owned, width), F32),
            shape((owned, width), BF),
            shape((ways, owned, local), BF),
            shape((1, width), F32),
        ],
        compiler_params=params(40),
        cost_estimate=cost(2 * owned * width * ways * local, 12 * MIB),
    )(sc, mine, core, tp, x2, cotangent, gain.reshape(1, width), weight)


def pair_grad_kernel(kvheads, own_ref, back_ref, c_ref, s_ref, out_ref):
    total = own_ref[...] + back_ref[...].astype(F32)
    cosine, sine = c_ref[...], s_ref[...]
    parts = []
    for n in range(kvheads):
        a = total[:, n * HEAD_DIM : n * HEAD_DIM + HALF]
        b = total[:, n * HEAD_DIM + HALF : (n + 1) * HEAD_DIM]
        parts += [a * cosine + b * sine, b * cosine - a * sine]
    parts.append(total[:, kvheads * HEAD_DIM :])
    out_ref[...] = jnp.concatenate(parts, axis=1).astype(BF)


def pair_grad(own, back, cosine, sine, kvheads):
    rows, wide = own.shape
    row = lambda n: pl.BlockSpec((TILE, n), lambda t: (t, 0))
    return pl.pallas_call(
        lambda *refs: pair_grad_kernel(kvheads, *refs),
        grid=(rows // TILE,),
        in_specs=[row(wide), row(wide), row(HALF), row(HALF)],
        out_specs=row(wide),
        out_shape=shape((rows, wide), BF),
        cost_estimate=cost(MIB, 4 * MIB),
    )(own, back, cosine, sine)


def finish_kernel(
    sc_ref, q0, q1, q2, q3, k0, k1, k2, k3, w_ref, x_ref, g_ref, dx_ref, out_ref, gain_ref, acc
):
    d = pl.program_id(0)

    def chosen(first, rest):
        value = first[0]
        for n, ref in enumerate(rest):
            value = jnp.where(d == n + 1, ref[...], value)
        return value

    left = jnp.concatenate([chosen(q0, (q1, q2, q3)), chosen(k0, (k1, k2, k3))], axis=1)
    term = dot(left, w_ref[0], NT)

    @pl.when(d == 0)
    def _():
        acc[...] = term

    @pl.when(d > 0)
    def _():
        acc[...] += term

    @pl.when(d == pl.num_programs(0) - 1)
    def _():
        dv, gain_grad = norm_back(acc[...], x_ref[...].astype(F32), g_ref[...])
        out_ref[...] = dx_ref[...] + dv
        gain_ref[...] = gain_grad


def finish(sc, query_parts, pair_parts, weight, tokens, gain, dx):
    owned, width = tokens.shape
    ways, _, wide = weight.shape
    local = query_parts[1].shape[1]
    whole = lambda *dims: pl.BlockSpec(dims, lambda d, sc: (0,) * len(dims))
    own = pl.BlockSpec((1, owned, local), lambda d, sc: (sc[0], 0, 0))
    return pl.pallas_call(
        finish_kernel,
        grid_spec=pltpu.PrefetchScalarGridSpec(
            num_scalar_prefetch=1,
            grid=(ways,),
            in_specs=[
                own, whole(owned, local), whole(owned, local), whole(owned, local),
                own, whole(owned, local), whole(owned, local), whole(owned, local),
                pl.BlockSpec((1, width, wide), lambda d, sc: (sc[0] ^ d, 0, 0)),
                whole(owned, width),
                whole(1, width),
                whole(owned, width),
            ],
            out_specs=[whole(owned, width), whole(1, width)],
            scratch_shapes=[pltpu.VMEM((owned, width), F32)],
        ),
        out_shape=[shape((owned, width), F32), shape((1, width), F32)],
        compiler_params=params(32),
        cost_estimate=cost(2 * owned * width * wide * ways, 14 * MIB),
    )(sc, *query_parts, *pair_parts, weight, tokens, gain.reshape(1, width), dx)


def halve(blocks, bits, group):
    for at, bit in enumerate(bits):
        kept = {}
        for r, block in blocks.items():
            if r & bit:
                continue
            came = send(blocks[r | bit].astype(BF), lambda s, t: (s ^ (bit * group), t))
            kept[r] = block.astype(F32) + came.astype(F32)
        blocks = kept
    return blocks[0]


def take(a, index, axis=0):
    return lax.dynamic_index_in_dim(a, index, axis, keepdims=False)


def across(pieces, j, ways, first=None):
    out = []
    for d in range(1, ways):
        out.append(send(take(pieces, j ^ d), lambda s, t: (s, t ^ d)))
    return out


def middle_scatter(a, axis, size, group):
    middle = group // 2
    if middle == 1:
        return a
    groups = [
        [g * group + 2 * m + c for m in range(middle)] for g in range(size // group) for c in (0, 1)
    ]
    return lax.psum_scatter(
        a, "seq", scatter_dimension=axis, tiled=True, axis_index_groups=groups
    )


def gain_sum(part):
    devices = lax.axis_size("seq") * lax.axis_size("tp")
    parts = lax.all_to_all(
        part.reshape(devices, -1), AXES, split_axis=0, concat_axis=0, tiled=True
    )
    return jnp.sum(parts, axis=0)


def body(
    tokens, lengths, first_gain, w_query, w_keyval, w_output, second_gain, w_gateup, w_down,
    cotangent,
):
    size, ways = lax.axis_size("seq"), lax.axis_size("tp")
    owned, width = tokens.shape
    rows = owned * ways
    local = w_query.shape[1]
    qheads = local // HEAD_DIM
    kvheads = w_keyval.shape[2] // HEAD_DIM
    units = w_down.shape[0]
    span = units // 4
    group = size // 4
    i, j = lax.axis_index("seq"), lax.axis_index("tp")
    odd = i & 1
    place = i // group
    sc = jnp.stack([j, place, odd]).astype(jnp.int32)
    sibling = lambda s, t: (s ^ 1, t)
    partner = lambda s, t: (s, t ^ 1)

    right, left = [tokens], [tokens]
    for _ in range(ways - 1):
        right.append(send(right[-1], lambda s, t: (s, t + 1)))
        left.append(send(left[-1], lambda s, t: (s, t - 1)))

    start_id = i * rows
    query_ids = start_id + jnp.arange(rows, dtype=jnp.int32)
    begins = doc_places(lengths, query_ids)
    cosine, sine = rotation_tables(query_ids - begins)
    lo = jnp.maximum(query_ids - (WINDOW - 1), begins) - (start_id - rows)
    lo = lo.reshape(1, rows)
    weight_one = jnp.concatenate(
        [spread_halves(w_query), spread_halves(w_keyval[:, 0]), w_keyval[:, 1]], axis=1
    )
    shares = lambda w: lax.dynamic_slice_in_dim(w, i * (w.shape[0] // size), w.shape[0] // size, 0)
    gathered = lambda w: lax.all_gather(shares(w), ("tp", "seq"), axis=0, tiled=True)
    output_all = gathered(w_output).reshape(ways, local, width)
    gateup_own = jnp.transpose(w_gateup, (1, 0, 2))
    piece = lax.dynamic_slice_in_dim(gateup_own, place * span, span, 2)
    far = lambda s, t: (s, t ^ 2) if s & 1 else None
    hop = lambda bit: lambda s, t: (s ^ (bit * group), t) if s & 1 else None
    g0 = send(piece, far)
    g1, g2 = send(g0, hop(1)), send(g0, hop(2))
    g3 = send(g1, hop(2))
    d0 = send(lax.dynamic_slice_in_dim(w_down, place * span, span, 0), far)
    d1, d2 = send(d0, hop(1)), send(d0, hop(2))
    d3 = send(d2, hop(1))
    ct_own = jnp.stack([send(cotangent, partner), cotangent])
    ct_sib = send(ct_own, sibling)

    inputs_one, queries, pair_here = project(
        sc, right[:1] + right[1:] + left[1:], first_gain, weight_one,
        *lane_tables(cosine, sine), qheads, kvheads,
    )
    pair_before = send(pair_here, lambda s, t: (s + 1, t))
    heads_out, logs = attend(queries, pair_before, pair_here, lo, kvheads)

    near_rows = lambda half: lax.dynamic_slice_in_dim(heads_out, half * 2 * owned, 2 * owned, 0)
    from_far = send(near_rows((j >> 1) ^ 1), lambda s, t: (s, t ^ 2))
    from_near = send(near_rows(j >> 1), partner)
    from_last = send(from_far, partner)
    x2, h_own, heads_rows = mix(
        sc, heads_out, (from_near, from_far, from_last), output_all, tokens, right[1], left[1],
        second_gain,
    )
    h_sib = send(h_own, sibling)

    fed = lambda m: feed(
        m, sc, h_own, h_sib, ct_own, ct_sib, gateup_own, w_down, (g0, g1, g2, g3), (d0, d1, d2, d3)
    )
    a0, dg0, du0, y0, dh0 = fed(0)
    a1, dg1, du1, y1, dh1 = fed(1)

    def to_partner(first):
        came = send(first[0], sibling)
        return send((first[1].astype(F32) + came.astype(F32)).astype(BF), partner)

    dh_z = to_partner(dh0)
    dh_core = send(dh1[0], sibling)
    dx2, low, heads_grad, second_part = turn_back(
        sc, dh1, dh_core, dh_z, x2, cotangent, second_gain, output_all
    )
    grad_parts = [heads_grad] + across(heads_grad, j, ways)
    y_z = to_partner(y0)
    y_core = send(y1[0], sibling)
    result = (x2[1] + (y1[1].astype(F32) + y_core.astype(F32) + y_z.astype(F32))).astype(BF)

    blocks = {}
    for r in (3, 1, 2, 0):
        blocks[r] = feed_grad(
            r, sc, h_own, h_sib, ct_own, ct_sib, (a0, dg0, du0), (a1, dg1, du1)
        )
    gateup_block = halve({r: b[0] for r, b in blocks.items()}, (1, 2), group)
    down_block = halve({r: b[1] for r, b in blocks.items()}, (2, 1), group)

    def own_share(block, axis):
        block = middle_scatter(block, axis, size, group)
        half = block.shape[axis] // 2
        low_block = block.astype(BF)
        cut = lambda a, k: lax.dynamic_slice_in_dim(a, k * half, half, axis)
        crossed = send(cut(low_block, 1 - odd), lambda s, t: (s ^ 1, t ^ 2) if s & 1 else (s ^ 1, t))
        second = send(cut(low_block, 1), far).astype(F32)
        mine = lax.slice_in_dim(block, 0, half, axis=axis)
        return jnp.where(odd == 0, mine, second) + crossed.astype(F32)

    gateup_grad = jnp.transpose(own_share(gateup_block, 1), (1, 0, 2))
    down_grad = jnp.transpose(own_share(down_block, 0))

    share = width // size
    by_core = lambda a: a.reshape(-1, size // 2, 2, share)
    low_parts = by_core(low)
    low_mine = take(low_parts, odd, 2).reshape(owned, -1)
    low_came = send(take(low_parts, 1 - odd, 2).reshape(owned, -1), sibling)
    heads_sib = send(heads_rows, sibling)
    out_grad = dot(
        jnp.concatenate([low_mine, low_came], axis=0),
        jnp.concatenate([heads_rows, heads_sib], axis=0),
        TN,
    ).astype(BF)
    out_grad = out_grad.reshape(4, -1, ways * local)
    cut = ways * local // 2
    relative = lambda a: {r: take(a, place ^ r) for r in range(4)}
    out_block = jnp.concatenate(
        [
            halve(relative(out_grad[..., :cut]), (1, 2), group),
            halve(relative(out_grad[..., cut:]), (2, 1), group),
        ],
        axis=1,
    )
    out_block = middle_scatter(out_block, 0, size, group)
    out_share = out_block[:, :local]
    for d in range(1, ways):
        came = send(
            out_block[:, d * local : (d + 1) * local].astype(BF), lambda s, t: (s, t ^ d)
        )
        out_share = out_share + came.astype(F32)
    output_grad = jnp.transpose(out_share)

    dq, dpair_before, dpair_here = attend_back(
        sc, queries, pair_before, pair_here, lo, heads_out, logs, grad_parts,
        (jnp.transpose(cosine), jnp.transpose(sine)), kvheads,
    )
    returned = send(dpair_before, lambda s, t: (s - 1, t))
    dpair = pair_grad(dpair_here, returned, cosine, sine, kvheads)
    query_rows = dq.reshape(ways, owned, local)
    pair_rows = dpair.reshape(ways, owned, local)
    query_parts = [query_rows] + across(query_rows, j, ways)
    pair_parts = [pair_rows] + across(pair_rows, j, ways)
    weight_flat = jnp.concatenate([w_query, w_keyval.reshape(width, -1)], axis=1)
    weight_all = gathered(weight_flat).reshape(ways, width, 2 * local)
    tokens_grad, first_part = finish(
        sc, query_parts, pair_parts, weight_all, tokens, first_gain, dx2
    )

    def summed(grads, bits):
        full = dot(inputs_one, grads, TN).astype(BF).reshape(4, -1, 2, share, local)
        came = send(take(full, 1 - odd, 2), sibling)
        kept = (take(full, odd, 2).astype(F32) + came.astype(F32)).astype(BF)
        block = halve(relative(kept), bits, group)
        return middle_scatter(block.reshape(-1, local), 0, size, group)

    query_grad = summed(dq, (1, 2))
    keyval_grad = summed(dpair, (2, 1)).reshape(share, 2, -1)
    return (
        result, tokens_grad, gain_sum(first_part), query_grad, keyval_grad, output_grad,
        gain_sum(second_part), gateup_grad, down_grad,
    )


def solution(mesh):
    return jax.shard_map(
        body,
        mesh=mesh,
        in_specs=(
            P(AXES, None), P(), P(), P(None, "tp"), P(None, None, "tp"), P("tp", None), P(),
            P(None, None, "tp"), P("tp", None), P(AXES, None),
        ),
        out_specs=(
            P(AXES, None), P(AXES, None), P(AXES), P("seq", "tp"), P("seq", None, "tp"),
            P("tp", "seq"), P(AXES), P("seq", None, "tp"), P("tp", "seq"),
        ),
        check_vma=False,
    )
```

```python
import jax
import jax.numpy as jnp
from jax import lax
from jax.experimental import pallas as pl
from jax.experimental.pallas import tpu as pltpu
from jax.sharding import PartitionSpec as P

HEAD_DIM = 96
HALF = HEAD_DIM // 2
LANES = 128
WINDOW = 1024
TILE = 256
EPSILON = 1e-05
THETA = 100000.0
SCALE = HEAD_DIM ** (-0.5)
LOG2E = 1.4426950408889634
SCALE2 = SCALE * LOG2E
BF = jnp.bfloat16
F32 = jnp.float32
NT = (((1,), (1,)), ((), ()))
NN = (((1,), (0,)), ((), ()))
TN = (((0,), (0,)), ((), ()))
MIB = 1 << 20
AXES = ("seq", "tp")
ANY = pl.BlockSpec(memory_space=pl.ANY)


def dot(a, b, dims=NN):
    return lax.dot_general(a, b, dims, preferred_element_type=F32)


def shape(dims, dtype):
    return jax.ShapeDtypeStruct(dims, dtype)


def cost(flops, moved, exps=0):
    return pl.CostEstimate(flops=flops // 16, bytes_accessed=moved // 16, transcendentals=0)


def params(mib):
    return pltpu.CompilerParams(vmem_limit_bytes=mib * MIB)


def send(a, to):
    size, ways = lax.axis_size("seq"), lax.axis_size("tp")
    pairs = []
    for s in range(size):
        for t in range(ways):
            there = to(s, t)
            if there is not None and 0 <= there[0] < size and 0 <= there[1] < ways:
                pairs.append((s * ways + t, there[0] * ways + there[1]))
    return lax.ppermute(a, AXES, pairs)


def doc_places(lengths, token_ids):
    bounds = jnp.cumsum(lengths)
    passed = token_ids[:, None] >= bounds[None, :]
    return jnp.sum(jnp.where(passed, lengths[None, :], 0), axis=1)


def spread_halves(w):
    n = w.shape[0]
    parts = w.reshape(n, -1, 2, HALF)
    parts = jnp.pad(parts, ((0, 0), (0, 0), (0, 0), (0, LANES // 2 - HALF)))
    return parts.reshape(n, -1)


def rotation_tables(places):
    freqs = THETA ** (-2.0 * jnp.arange(HALF, dtype=F32) / HEAD_DIM)
    angles = places.astype(F32)[:, None] * freqs[None, :]
    return jnp.cos(angles), jnp.sin(angles)


def lane_tables(cosine, sine):
    fill = ((0, 0), (0, LANES // 2 - HALF))
    cosine, sine = jnp.pad(cosine, fill), jnp.pad(sine, fill)
    return (
        jnp.concatenate([cosine, cosine], axis=1),
        jnp.concatenate([-sine, sine], axis=1),
    )


def project_kernel(
    sizes, sc_ref, own, r1, r2, r3, l1, l2, l3, g_ref, w_ref, c_ref, s_ref,
    h_ref, q_ref, kv_ref, x_s, sem,
):
    qheads, kvheads, ways = sizes
    o = pl.program_id(0)
    j = sc_ref[0]
    sources = {0: own, -1: r1, -2: r2, -3: r3, 1: l1, 2: l2, 3: l3}

    def fetch(at, slot):
        for d, ref in sources.items():

            @pl.when(at - j == d)
            def _():
                pltpu.make_async_copy(ref, x_s.at[slot], sem.at[slot]).start()

    @pl.when(o == 0)
    def _():
        fetch(0, 0)

    slot = lax.rem(o, 2)

    @pl.when(o + 1 < ways)
    def _():
        fetch(o + 1, 1 - slot)

    pltpu.make_async_copy(own, x_s.at[slot], sem.at[slot]).wait()
    x = x_s[slot].astype(F32)
    scale = lax.rsqrt(jnp.mean(x * x, axis=-1, keepdims=True) + EPSILON)
    h = (x * scale * g_ref[...]).astype(BF)
    h_ref[...] = h
    flat = dot(h, w_ref[...])
    cosine, sine = c_ref[...], s_ref[...]

    def turned(n):
        u = flat[:, n * LANES : (n + 1) * LANES]
        u = u * cosine + pltpu.roll(u, LANES // 2, 1) * sine
        return jnp.concatenate([u[:, :HALF], u[:, LANES // 2 : LANES // 2 + HALF]], axis=1)

    fill = jnp.zeros((x.shape[0], LANES - HEAD_DIM), F32)
    for n in range(qheads):
        q_ref[:, n * LANES : (n + 1) * LANES] = jnp.concatenate([turned(n), fill], axis=1).astype(
            BF
        )
    keys = [turned(qheads + n) for n in range(kvheads)]
    values = [flat[:, (qheads + kvheads) * LANES :]]
    kv_ref[...] = jnp.concatenate(keys + values, axis=1).astype(BF)


def project(sc, shards, gain, weight, cosine, sine, qheads, kvheads):
    owned, width = shards[0].shape
    ways = 4
    rows = owned * ways
    wide = weight.shape[1]
    kvwide = 2 * kvheads * HEAD_DIM
    row = lambda n: pl.BlockSpec((owned, n), lambda o, sc: (o, 0))
    whole = lambda m, n: pl.BlockSpec((m, n), lambda o, sc: (0, 0))
    return pl.pallas_call(
        lambda *refs: project_kernel((qheads, kvheads, ways), *refs),
        grid_spec=pltpu.PrefetchScalarGridSpec(
            num_scalar_prefetch=1,
            grid=(ways,),
            in_specs=[ANY] * 7 + [whole(1, width), whole(width, wide), row(LANES), row(LANES)],
            out_specs=[row(width), row(qheads * LANES), row(kvwide)],
            scratch_shapes=[pltpu.VMEM((2, owned, width), BF), pltpu.SemaphoreType.DMA((2,))],
        ),
        out_shape=[
            shape((rows, width), BF),
            shape((rows, qheads * LANES), BF),
            shape((rows, kvwide), BF),
        ],
        compiler_params=params(60),
        cost_estimate=cost(2 * rows * width * wide, 4 * rows * width),
    )(sc, *shards, gain.reshape(1, width), weight, cosine, sine)


def masked(raw, first_key, lo, diagonal, query_ids):
    keys = first_key + lax.broadcasted_iota(jnp.int32, raw.shape, 0)
    ok = keys >= lo
    if diagonal:
        ok = ok & (keys <= query_ids)
    return jnp.where(ok, raw, -1e30)


def load_pairs(kp_ref, ko_ref, k_s, v_s, head, kvheads):
    rows = ko_ref.shape[0]

    @pl.when(head == 0)
    def _():
        k_s[...] = jnp.zeros_like(k_s)
        v_s[...] = jnp.zeros_like(v_s)

    for n in range(kvheads):

        @pl.when(head == n)
        def _():
            for place, ref in ((0, kp_ref), (rows, ko_ref)):
                at = n * HEAD_DIM
                k_s[place : place + rows, :HEAD_DIM] = ref[:, at : at + HEAD_DIM]
                at = (kvheads + n) * HEAD_DIM
                v_s[place : place + rows, :HEAD_DIM] = ref[:, at : at + HEAD_DIM]


def tile_parts(q_ref, lo_ref, rows, t):
    q = jnp.concatenate([q_ref[:, :LANES], q_ref[:, LANES:]], axis=0)
    lo = jnp.concatenate([lo_ref[...], lo_ref[...]], axis=1)
    ids = rows + t * TILE + lax.broadcasted_iota(jnp.int32, (1, TILE), 1)
    return q, lo, jnp.concatenate([ids, ids], axis=1)


def attend_kernel(kvheads, q_ref, kp_ref, ko_ref, lo_ref, o_ref, l_ref, k_s, v_s):
    head, t = pl.program_id(0), pl.program_id(1)
    rows = ko_ref.shape[0]
    chunks = WINDOW // TILE + 1

    @pl.when(t == 0)
    def _():
        load_pairs(kp_ref, ko_ref, k_s, v_s, head, kvheads)

    q, lo, ids = tile_parts(q_ref, lo_ref, rows, t)
    scores = []
    for c in range(chunks):
        first = pl.multiple_of((t + c) * TILE, TILE)
        raw = dot(k_s[pl.ds(first, TILE)], q, NT)
        scores.append(masked(raw, first, lo, c == chunks - 1, ids))
    top = scores[0].max(axis=0, keepdims=True)
    for s in scores[1:]:
        top = jnp.maximum(top, s.max(axis=0, keepdims=True))
    top = top * SCALE2
    total = jnp.zeros_like(top)
    mixed = jnp.zeros((LANES, 2 * TILE), F32)
    for c in range(chunks):
        first = pl.multiple_of((t + c) * TILE, TILE)
        p = jnp.exp2(scores[c] * SCALE2 - top)
        total = total + jnp.sum(p, axis=0, keepdims=True)
        mixed = mixed + dot(v_s[pl.ds(first, TILE)], p.astype(BF), TN)
    l_ref[0, 0] = top + jnp.log2(total)
    out = jnp.transpose(mixed / total).astype(BF)
    here = pl.ds(pl.multiple_of(t * TILE, TILE), TILE)
    for n in range(kvheads):

        @pl.when(head == n)
        def _():
            for g in range(2):
                at = (2 * n + g) * HEAD_DIM
                o_ref[here, at : at + HEAD_DIM] = out[g * TILE : (g + 1) * TILE, :HEAD_DIM]


def attend(queries, pair_before, pair_here, lo, kvheads):
    rows = queries.shape[0]
    tiles = rows // TILE
    whole = pl.BlockSpec((rows, 2 * kvheads * HEAD_DIM), lambda h, t: (0, 0))
    return pl.pallas_call(
        lambda *refs: attend_kernel(kvheads, *refs),
        grid=(kvheads, tiles),
        in_specs=[
            pl.BlockSpec((TILE, 2 * LANES), lambda h, t: (t, h)),
            whole,
            whole,
            pl.BlockSpec((1, TILE), lambda h, t: (0, t)),
        ],
        out_specs=[whole, pl.BlockSpec((1, 1, 1, 2 * TILE), lambda h, t: (h, t, 0, 0))],
        out_shape=[
            shape((rows, 2 * kvheads * HEAD_DIM), BF),
            shape((kvheads, tiles, 1, 2 * TILE), F32),
        ],
        scratch_shapes=[pltpu.VMEM((2 * rows, LANES), BF), pltpu.VMEM((2 * rows, LANES), BF)],
        compiler_params=params(60),
        cost_estimate=cost(6400 * MIB, 5 * MIB, 5 * MIB),
    )(queries, pair_before, pair_here, lo)


def attend_back_kernel(
    kvheads, q_ref, kp_ref, ko_ref, lo_ref, o_ref, l_ref, do_ref, c_ref, s_ref,
    dq_ref, dp_ref, dkv_ref, k_s, v_s, dk_s, dv_s,
):
    head, t = pl.program_id(0), pl.program_id(1)
    rows = ko_ref.shape[0]
    chunks = WINDOW // TILE + 1

    @pl.when(t == 0)
    def _():
        load_pairs(kp_ref, ko_ref, k_s, v_s, head, kvheads)
        dk_s[...] = jnp.zeros_like(dk_s)
        dv_s[...] = jnp.zeros_like(dv_s)

    def heads_of(both):
        pair = both[:, : 2 * HEAD_DIM]
        for n in range(1, kvheads):
            pair = jnp.where(
                head == n, both[:, 2 * n * HEAD_DIM : 2 * (n + 1) * HEAD_DIM], pair
            )
        fill = jnp.zeros((TILE, LANES - HEAD_DIM), BF)
        first = jnp.concatenate([pair[:, :HEAD_DIM], fill], axis=1)
        second = jnp.concatenate([pair[:, HEAD_DIM:], fill], axis=1)
        return jnp.concatenate([first, second], axis=0)

    q, lo, ids = tile_parts(q_ref, lo_ref, rows, t)
    grad = heads_of(do_ref[...])
    prod = grad.astype(F32) * heads_of(o_ref[...]).astype(F32)
    center = jnp.sum(jnp.transpose(prod), axis=0, keepdims=True)
    logs = l_ref[0, 0]
    dq = jnp.zeros((LANES, 2 * TILE), F32)
    for c in range(chunks):
        first = pl.multiple_of((t + c) * TILE, TILE)
        here = pl.ds(first, TILE)
        keys = k_s[here]
        raw = masked(dot(keys, q, NT), first, lo, c == chunks - 1, ids)
        p = jnp.exp2(raw * SCALE2 - logs)
        dp = dot(v_s[here], grad, NT)
        ds = (p * (dp - center)).astype(BF)
        dv_s[here] += dot(p.astype(BF), grad)
        dk_s[here] += dot(ds, q)
        dq = dq + dot(keys, ds, TN)
    cosine = jnp.concatenate([c_ref[...], c_ref[...]], axis=1)
    sine = jnp.concatenate([s_ref[...], s_ref[...]], axis=1)
    a, b = dq[:HALF] * SCALE, dq[HALF:HEAD_DIM] * SCALE
    fill = jnp.zeros((LANES - HEAD_DIM, 2 * TILE), F32)
    dq = jnp.concatenate([a * cosine + b * sine, b * cosine - a * sine, fill], axis=0)
    dq = jnp.transpose(dq).astype(BF)
    mine = pl.ds(pl.multiple_of(t * TILE, TILE), TILE)
    last = t == pl.num_programs(1) - 1
    for n in range(kvheads):

        @pl.when(head == n)
        def _():
            for g in range(2):
                at = (2 * n + g) * HEAD_DIM
                dq_ref[mine, at : at + HEAD_DIM] = dq[g * TILE : (g + 1) * TILE, :HEAD_DIM]

        @pl.when((head == n) & last)
        def _():
            at = n * HEAD_DIM
            dp_ref[:, at : at + HEAD_DIM] = (dk_s[:rows, :HEAD_DIM] * SCALE).astype(BF)
            dkv_ref[:, at : at + HEAD_DIM] = dk_s[rows:, :HEAD_DIM] * SCALE
            at = (kvheads + n) * HEAD_DIM
            dp_ref[:, at : at + HEAD_DIM] = dv_s[:rows, :HEAD_DIM].astype(BF)
            dkv_ref[:, at : at + HEAD_DIM] = dv_s[rows:, :HEAD_DIM]


def attend_back(queries, pair_before, pair_here, lo, heads_out, logs, grads, tables, kvheads):
    rows = queries.shape[0]
    tiles = rows // TILE
    wide = 2 * kvheads * HEAD_DIM
    whole = pl.BlockSpec((rows, wide), lambda h, t: (0, 0))
    table = pl.BlockSpec((HALF, TILE), lambda h, t: (0, t))
    return pl.pallas_call(
        lambda *refs: attend_back_kernel(kvheads, *refs),
        grid=(kvheads, tiles),
        in_specs=[
            pl.BlockSpec((TILE, 2 * LANES), lambda h, t: (t, h)),
            whole,
            whole,
            pl.BlockSpec((1, TILE), lambda h, t: (0, t)),
            pl.BlockSpec((TILE, wide), lambda h, t: (t, 0)),
            pl.BlockSpec((1, 1, 1, 2 * TILE), lambda h, t: (h, t, 0, 0)),
            pl.BlockSpec((TILE, wide), lambda h, t: (t, 0)),
            table,
            table,
        ],
        out_specs=[whole, whole, whole],
        scratch_shapes=[
            pltpu.VMEM((2 * rows, LANES), BF),
            pltpu.VMEM((2 * rows, LANES), BF),
            pltpu.VMEM((2 * rows, LANES), F32),
            pltpu.VMEM((2 * rows, LANES), F32),
        ],
        out_shape=[shape((rows, wide), BF), shape((rows, wide), BF), shape((rows, wide), F32)],
        compiler_params=params(60),
        cost_estimate=cost(16000 * MIB, 8 * MIB, 5 * MIB),
    )(queries, pair_before, pair_here, lo, heads_out, logs, grads, *tables)


def shard(w_ref, k):
    pieces, _, part, width = w_ref.shape
    return w_ref[:, pl.ds(k, 1)].reshape(pieces * part, width)


def mix_kernel(
    sc_ref, o_ref, w_ref, x_ref, xr_ref, xl_ref, g_ref, x2_ref, h2_ref, row_ref
):
    m = pl.program_id(0)
    j = sc_ref[0]
    ways = o_ref.shape[0]
    acc = dot(o_ref[0], shard(w_ref, j))
    for k in range(1, ways):
        acc = acc + dot(o_ref[k], shard(w_ref, j ^ k))
    other = jnp.where((j & 1) == 1, xr_ref[...], xl_ref[...])
    x2 = jnp.where(m == 1, x_ref[...], other).astype(F32) + acc
    x2_ref[0] = x2
    scale = lax.rsqrt(jnp.mean(x2 * x2, axis=-1, keepdims=True) + EPSILON)
    h2_ref[0] = (x2 * scale * g_ref[...]).astype(BF)

    @pl.when(m == 1)
    def _():
        row_ref[...] = jnp.concatenate([o_ref[k] for k in range(ways)], axis=1)


def mix(sc, parts, weight, tokens, right, left, gain):
    owned, width = tokens.shape
    ways, _, local = parts.shape
    whole = lambda *dims: pl.BlockSpec(dims, lambda m, sc: (0,) * len(dims))
    return pl.pallas_call(
        mix_kernel,
        grid_spec=pltpu.PrefetchScalarGridSpec(
            num_scalar_prefetch=1,
            grid=(2,),
            in_specs=[
                pl.BlockSpec((ways, owned, local), lambda m, sc: (0, (sc[0] & 1) ^ 1 ^ m, 0)),
                whole(*weight.shape),
                whole(owned, width),
                whole(owned, width),
                whole(owned, width),
                whole(1, width),
            ],
            out_specs=[
                pl.BlockSpec((1, owned, width), lambda m, sc: (m, 0, 0)),
                pl.BlockSpec((1, owned, width), lambda m, sc: (m, 0, 0)),
                whole(owned, ways * local),
            ],
        ),
        out_shape=[
            shape((2, owned, width), F32),
            shape((2, owned, width), BF),
            shape((owned, ways * local), BF),
        ],
        compiler_params=params(60),
        cost_estimate=cost(1, 1),
    )(sc, parts, weight, tokens, right, left, gain.reshape(1, width))


def feed_kernel(
    sc_ref, ho_ref, hs_ref, co_ref, cs_ref, gu_own, d_own, w0, w1, w2, w3,
    a_ref, dg_ref, du_ref, sib_dh, own_dh, sib_y, own_y, w_s, y_s, dh_s, sem,
):
    r = pl.program_id(0)
    steps = pl.num_programs(0)
    place, odd = sc_ref[1], sc_ref[2]
    taken = [w0, w1, w2, w3]
    span = w_s.shape[3]

    def fetch(at, slot):
        @pl.when(odd == 0)
        def _():
            part = pl.ds(pl.multiple_of((place ^ at) * span, span), span)
            pltpu.make_async_copy(
                gu_own.at[:, :, part], w_s.at[slot, pl.ds(0, 2)], sem.at[0, slot]
            ).start()
            pltpu.make_async_copy(d_own.at[:, part], w_s.at[slot, 2], sem.at[1, slot]).start()

        for k, w in enumerate(taken):

            @pl.when((odd == 1) & (at == k))
            def _():
                pltpu.make_async_copy(
                    w.at[pl.ds(0, 2)], w_s.at[slot, pl.ds(0, 2)], sem.at[0, slot]
                ).start()
                pltpu.make_async_copy(w.at[2], w_s.at[slot, 2], sem.at[1, slot]).start()

    @pl.when(r == 0)
    def _():
        fetch(0, 0)
        y_s[...] = jnp.zeros_like(y_s)
        dh_s[...] = jnp.zeros_like(dh_s)

    slot = lax.rem(r, 2)

    @pl.when(r + 1 < steps)
    def _():
        fetch(r + 1, 1 - slot)

    pltpu.make_async_copy(w0.at[pl.ds(0, 2)], w_s.at[slot, pl.ds(0, 2)], sem.at[0, slot]).wait()
    pltpu.make_async_copy(w0.at[2], w_s.at[slot, 2], sem.at[1, slot]).wait()
    h = jnp.concatenate([hs_ref[0], ho_ref[0]], axis=0)
    ct = jnp.concatenate([cs_ref[0], co_ref[0]], axis=0)
    gate_w, up_w, down_w = w_s[slot, 0], w_s[slot, 1], w_s[slot, 2]
    gate = dot(h, gate_w)
    up = dot(h, up_w)
    da = dot(ct, down_w)
    sig = jax.nn.sigmoid(gate)
    act = gate * sig
    a = (act * up).astype(BF)
    dgate = (da * up * sig * (1.0 + gate * (1.0 - sig))).astype(BF)
    dup = (da * act).astype(BF)
    a_ref[...] = a
    dg_ref[...] = dgate
    du_ref[...] = dup
    y_s[...] += dot(a, down_w, NT)
    dh_s[...] += dot(dgate, gate_w, NT) + dot(dup, up_w, NT)

    @pl.when(r == steps - 1)
    def _():
        half = sib_dh.shape[0]
        for k, (dh_ref, y_ref) in enumerate(((sib_dh, sib_y), (own_dh, own_y))):
            dh_ref[...] = dh_s[k * half : (k + 1) * half].astype(BF)
            y_ref[...] = y_s[k * half : (k + 1) * half].astype(BF)


def feed(m, sc, h_own, h_sib, ct_own, ct_sib, gu_own, d_own, taken):
    _, owned, width = h_own.shape
    units = d_own.shape[1]
    span = units // 4
    rows = pl.BlockSpec((1, owned, width), lambda r, sc: (m, 0, 0))
    out = pl.BlockSpec((2 * owned, span), lambda r, sc: (0, sc[1] ^ r))
    whole = pl.BlockSpec((owned, width), lambda r, sc: (0, 0))
    return pl.pallas_call(
        feed_kernel,
        grid_spec=pltpu.PrefetchScalarGridSpec(
            num_scalar_prefetch=1,
            grid=(4,),
            in_specs=[rows] * 4 + [ANY] * 6,
            out_specs=[out, out, out] + [whole] * 4,
            scratch_shapes=[
                pltpu.VMEM((2, 3, width, span), BF),
                pltpu.VMEM((2 * owned, width), F32),
                pltpu.VMEM((2 * owned, width), F32),
                pltpu.SemaphoreType.DMA((2, 2)),
            ],
        ),
        out_shape=[shape((2 * owned, units), BF)] * 3 + [shape((owned, width), BF)] * 4,
        compiler_params=params(60),
        cost_estimate=cost(36 * owned * width * units, 22 * MIB, 2 * owned * units),
    )(sc, h_own, h_sib, ct_own, ct_sib, gu_own, d_own, *taken)


def feed_grad_kernel(
    sc_ref, ho0, hs0, co0, cs0, ho1, hs1, co1, cs1, a0, dg0, du0, a1, dg1, du1, out_ref, h_s, ct_s
):
    part = h_s.shape[0] // 2

    @pl.when(pl.program_id(0) == 0)
    def _():
        for k, (own, sib) in enumerate(((ho0, hs0), (ho1, hs1))):
            rows = jnp.concatenate([sib[0], own[0], sib[1], own[1]], axis=0)
            h_s[k * part : (k + 1) * part] = jnp.transpose(rows)
        for k, (own, sib) in enumerate(((co0, cs0), (co1, cs1))):
            rows = jnp.concatenate([sib[0], own[0], sib[1], own[1]], axis=0)
            ct_s[k * part : (k + 1) * part] = jnp.transpose(rows)

    both = lambda x, y: jnp.concatenate([x[...], y[...]], axis=0)
    for n, (left, right) in enumerate(
        ((h_s, both(dg0, dg1)), (h_s, both(du0, du1)), (ct_s, both(a0, a1)))
    ):
        grad = dot(left[...], right).astype(BF)
        for k in range(2):
            out_ref[k, n] = grad[k * part : (k + 1) * part]


def feed_grad(blocks, half, sc, h_own, h_sib, ct_own, ct_sib, first, second):
    _, owned, width = h_own.shape
    units = first[0].shape[1] // 2
    part = width // 4
    cut = 2
    lanes = lambda r: pl.BlockSpec((2, owned, part), lambda n, sc: (0, 0, sc[1] ^ r))
    right = pl.BlockSpec((2 * owned, units // cut), lambda n, sc: (0, half * cut + n))
    return pl.pallas_call(
        feed_grad_kernel,
        grid_spec=pltpu.PrefetchScalarGridSpec(
            num_scalar_prefetch=1,
            grid=(cut,),
            in_specs=[lanes(blocks[0])] * 4 + [lanes(blocks[1])] * 4 + [right] * 6,
            out_specs=pl.BlockSpec((2, 3, part, units // cut), lambda n, sc: (0, 0, 0, n)),
            scratch_shapes=[
                pltpu.VMEM((2 * part, 4 * owned), BF), pltpu.VMEM((2 * part, 4 * owned), BF)
            ],
        ),
        out_shape=shape((2, 3, part, units), BF),
        compiler_params=params(60),
        cost_estimate=cost(48 * owned * part * units, 14 * MIB),
    )(sc, *([h_own, h_sib, ct_own, ct_sib] * 2), *first, *second)


def norm_back(dn, v, gain):
    r = lax.rsqrt(jnp.mean(v * v, axis=-1, keepdims=True) + EPSILON)
    scaled = gain * dn
    gain_grad = jnp.sum(dn * (v * r), axis=0, keepdims=True)
    return r * scaled - v * (r * r * r) * jnp.mean(scaled * v, axis=-1, keepdims=True), gain_grad


def turn_back_kernel(
    sc_ref, a_ref, b_ref, z_ref, x2_ref, ct_ref, g_ref, w_ref, dx_ref, db_ref, gain_ref, do_ref
):
    dn = a_ref[...].astype(F32) + b_ref[...].astype(F32) + z_ref[...].astype(F32)
    dv, gain_grad = norm_back(dn, x2_ref[0], g_ref[...])
    gain_ref[...] = gain_grad
    dx = ct_ref[...].astype(F32) + dv
    dx_ref[...] = dx
    low = dx.astype(BF)
    db_ref[...] = low
    j = sc_ref[0]
    for d in range(do_ref.shape[0]):
        do_ref[j ^ d] = dot(low, shard(w_ref, d), NT).astype(BF)


def turn_back(sc, mine, core, tp, x2, cotangent, gain, weight):
    owned, width = cotangent.shape
    ways, local = weight.shape[1], weight.shape[0] * weight.shape[2]
    whole = lambda *dims: pl.BlockSpec(dims, lambda n, sc: (0,) * len(dims))
    own = pl.BlockSpec((1, owned, width), lambda n, sc: (1, 0, 0))
    return pl.pallas_call(
        turn_back_kernel,
        grid_spec=pltpu.PrefetchScalarGridSpec(
            num_scalar_prefetch=1,
            grid=(1,),
            in_specs=[
                whole(owned, width),
                whole(owned, width),
                whole(owned, width),
                own,
                whole(owned, width),
                whole(1, width),
                whole(*weight.shape),
            ],
            out_specs=[
                whole(owned, width),
                whole(owned, width),
                whole(1, width),
                whole(ways, owned, local),
            ],
        ),
        out_shape=[
            shape((owned, width), F32),
            shape((owned, width), BF),
            shape((1, width), F32),
            shape((ways, owned, local), BF),
        ],
        compiler_params=params(60),
        cost_estimate=cost(2 * owned * width * ways * local, 12 * MIB),
    )(sc, mine, core, tp, x2, cotangent, gain.reshape(1, width), weight)


def pair_grad_kernel(kvheads, own_ref, back_ref, c_ref, s_ref, out_ref):
    total = own_ref[...] + back_ref[...].astype(F32)
    cosine, sine = c_ref[...], s_ref[...]
    parts = []
    for n in range(kvheads):
        a = total[:, n * HEAD_DIM : n * HEAD_DIM + HALF]
        b = total[:, n * HEAD_DIM + HALF : (n + 1) * HEAD_DIM]
        parts += [a * cosine + b * sine, b * cosine - a * sine]
    parts.append(total[:, kvheads * HEAD_DIM :])
    out_ref[...] = jnp.concatenate(parts, axis=1).astype(BF)


def pair_grad(own, back, cosine, sine, kvheads):
    rows, wide = own.shape
    row = lambda n: pl.BlockSpec((TILE, n), lambda t: (t, 0))
    return pl.pallas_call(
        lambda *refs: pair_grad_kernel(kvheads, *refs),
        grid=(rows // TILE,),
        in_specs=[row(wide), row(wide), row(HALF), row(HALF)],
        out_specs=row(wide),
        out_shape=shape((rows, wide), BF),
        compiler_params=params(60),
        cost_estimate=cost(MIB, 4 * MIB),
    )(own, back, cosine, sine)


def finish_kernel(q_ref, k_ref, w_ref, x_ref, g_ref, dx_ref, out_ref, gain_ref, acc):
    d = pl.program_id(0)
    left = jnp.concatenate([q_ref[0], k_ref[0]], axis=1)
    term = dot(left, shard(w_ref, 0))

    @pl.when(d == 0)
    def _():
        acc[...] = term

    @pl.when(d > 0)
    def _():
        acc[...] += term

    @pl.when(d == pl.num_programs(0) - 1)
    def _():
        dv, gain_grad = norm_back(acc[...], x_ref[...].astype(F32), g_ref[...])
        out_ref[...] = dx_ref[...] + dv
        gain_ref[...] = gain_grad


def finish(query_parts, pair_parts, weight, tokens, gain, dx):
    owned, width = tokens.shape
    pieces, ways, part, _ = weight.shape
    wide = pieces * part
    local = query_parts.shape[2]
    whole = lambda *dims: pl.BlockSpec(dims, lambda d: (0,) * len(dims))
    one = pl.BlockSpec((1, owned, local), lambda d: (d, 0, 0))
    return pl.pallas_call(
        finish_kernel,
        grid=(ways,),
        in_specs=[
            one,
            one,
            pl.BlockSpec((pieces, 1, part, width), lambda d: (0, d, 0, 0)),
            whole(owned, width),
            whole(1, width),
            whole(owned, width),
        ],
        out_specs=[whole(owned, width), whole(1, width)],
        scratch_shapes=[pltpu.VMEM((owned, width), F32)],
        out_shape=[shape((owned, width), F32), shape((1, width), F32)],
        compiler_params=params(60),
        cost_estimate=cost(2 * owned * width * wide * ways, 14 * MIB),
    )(query_parts, pair_parts, weight, tokens, gain.reshape(1, width), dx)


def tie(*values):
    return lax.optimization_barrier(values)


def hop(bit, group):
    return lambda s, t: (s ^ (bit * group), t)


def exchanged_sum(pieces, group):
    groups = [[r + k * group for k in range(4)] for r in range(group)]
    came = lax.all_to_all(
        pieces, "seq", split_axis=0, concat_axis=0, axis_index_groups=groups, tiled=True
    )
    return jnp.sum(came.astype(F32), axis=0)


def swapped(pieces):
    return lax.all_to_all(pieces, "tp", split_axis=0, concat_axis=0, tiled=True)


def take(a, index, axis=0):
    return lax.dynamic_index_in_dim(a, index, axis, keepdims=False)


def middle_scatter(a, axis, size, group):
    middle = group // 2
    if middle == 1:
        return a
    groups = [
        [g * group + 2 * m + c for m in range(middle)] for g in range(size // group) for c in (0, 1)
    ]
    return lax.psum_scatter(
        a, "seq", scatter_dimension=axis, tiled=True, axis_index_groups=groups
    )


def gain_sum(part):
    devices = lax.axis_size("seq") * lax.axis_size("tp")
    parts = lax.all_to_all(
        part.reshape(devices, -1), AXES, split_axis=0, concat_axis=0, tiled=True
    )
    return jnp.sum(parts, axis=0)


def body(
    tokens, lengths, first_gain, w_query, w_keyval, w_output, second_gain, w_gateup, w_down,
    cotangent,
):
    size, ways = lax.axis_size("seq"), lax.axis_size("tp")
    owned, width = tokens.shape
    rows = owned * ways
    local = w_query.shape[1]
    qheads = local // HEAD_DIM
    kvheads = w_keyval.shape[2] // HEAD_DIM
    units = w_down.shape[0]
    span = units // 4
    group = size // 4
    i, j = lax.axis_index("seq"), lax.axis_index("tp")
    odd = i & 1
    place = i // group
    sc = jnp.stack([j, place, odd]).astype(jnp.int32)
    sibling = lambda s, t: (s ^ 1, t)
    partner = lambda s, t: (s, t ^ 1)

    near = lambda a: lax.dynamic_slice_in_dim(a, place * span, span, a.ndim - 1)
    far = lambda s, t: (s, t ^ 2) if s & 1 else None
    hop_odd = lambda bit: lambda s, t: (s ^ (bit * group), t) if s & 1 else None
    up = lambda a, k: send(a, lambda s, t: (s, t + 1) if t >= k else None)
    down = lambda a, k: send(a, lambda s, t: (s, t - 1) if t < ways - k else None)
    pieces = 8
    eights = [list(range(k, k + pieces)) for k in range(0, size, pieces)]

    def own_piece(w):
        part = w.shape[0] // pieces
        return lax.dynamic_slice_in_dim(w, (i % pieces) * part, part, 0)

    def gathered(parts):
        return lax.all_gather(parts, "seq", axis=0, axis_index_groups=eights)

    r1, l1 = up(tokens, 0), down(tokens, 0)
    output_mine = own_piece(w_output)
    o1, o2, o3 = (send(output_mine, lambda s, t: (s, t ^ d)) for d in (1, 2, 3))
    gateup_own = jnp.transpose(w_gateup, (1, 0, 2))
    down_own = jnp.transpose(w_down)
    r1, l1, gateup_own, down_own, w_query, w_keyval = tie(
        r1, l1, gateup_own, down_own, w_query, w_keyval
    )
    r2, l2 = up(r1, 1), down(l1, 1)
    piece = jnp.concatenate([near(gateup_own), near(down_own)[None]], axis=0)
    weight_one = jnp.concatenate(
        [spread_halves(w_query), spread_halves(w_keyval[:, 0]), w_keyval[:, 1]], axis=1
    )
    r2, l2, weight_one, piece, lengths, o1, o2, o3 = tie(
        r2, l2, weight_one, piece, lengths, o1, o2, o3
    )
    output_all = gathered(jnp.stack([output_mine, o1, o2, o3]))
    r3, l3 = up(r2, 2), down(l2, 2)
    w0 = send(piece, far)
    start_id = i * rows
    query_ids = start_id + jnp.arange(rows, dtype=jnp.int32)
    begins = doc_places(lengths, query_ids)
    cosine, sine = rotation_tables(query_ids - begins)
    lo = jnp.maximum(query_ids - (WINDOW - 1), begins) - (start_id - rows)
    lo = lo.reshape(1, rows)
    lane_cos, lane_sin = lane_tables(cosine, sine)
    turned_cos, turned_sin = jnp.transpose(cosine), jnp.transpose(sine)
    r3, l3, lane_cos, lane_sin, turned_cos, turned_sin, lo = tie(
        r3, l3, lane_cos, lane_sin, turned_cos, turned_sin, lo
    )
    inputs_one, queries, pair_here = project(
        sc, [tokens, r1, r2, r3, l1, l2, l3], first_gain, weight_one, lane_cos, lane_sin,
        qheads, kvheads,
    )
    pair_before = send(pair_here, lambda s, t: (s + 1, t))
    pair_here, ct_late = tie(pair_here, cotangent)
    ct_partner = send(ct_late, partner)
    heads_out, logs = attend(queries, pair_before, pair_here, lo, kvheads)

    heads_out, w0 = tie(heads_out, w0)
    pairs_of = lambda a: jnp.repeat(a.reshape(2, 2 * owned, local), 2, axis=0)
    head_parts = swapped(pairs_of(heads_out))
    w1, w2, w3 = (send(w0, hop_odd(bit)) for bit in (1, 2, 3))
    flat_mine = own_piece(
        jnp.concatenate(
            [jnp.transpose(w_query), jnp.transpose(w_keyval, (1, 2, 0)).reshape(-1, width)], axis=0
        )
    )
    head_parts, flat_mine = tie(head_parts, flat_mine)
    flat_parts = swapped(jnp.broadcast_to(flat_mine[None], (ways, *flat_mine.shape)))
    x2, h_own, heads_rows = mix(sc, head_parts, output_all, tokens, r1, l1, second_gain)
    ct_own = jnp.stack([ct_partner, cotangent])
    h_own, w1, w2, w3, ct_own = tie(h_own, w1, w2, w3, ct_own)
    h_sib = send(h_own, sibling)
    ct_sib = send(ct_own, sibling)
    h_sib, ct_sib, flat_parts = tie(h_sib, ct_sib, flat_parts)
    weight_all = gathered(flat_parts)

    fed = lambda m, h: feed(
        m, sc, h, h_sib, ct_own, ct_sib, gateup_own, down_own, (w0, w1, w2, w3)
    )
    add = lambda a, b: a.astype(F32) + b.astype(F32)
    a0, dg0, du0, sib_dh0, own_dh0, sib_y0, own_y0 = fed(0, h_own)
    core0 = send(sib_dh0, sibling)
    dh_part = add(own_dh0, core0).astype(BF)
    dh_part, h_next = tie(dh_part, h_own)
    dh_z = send(dh_part, partner)
    a1, dg1, du1, sib_dh1, own_dh1, sib_y1, own_y1 = fed(1, h_next)
    sib_dh1, dh_z = tie(sib_dh1, dh_z)
    core1 = send(sib_dh1, sibling)
    graded = lambda blocks, half, h: feed_grad(
        blocks, half, sc, h, h_sib, ct_own, ct_sib, (a0, dg0, du0), (a1, dg1, du1)
    )
    first_away, core1 = tie(graded((1, 3), 0, h_own), core1)
    first_came = send(first_away, hop(1, group))
    dx2, low, second_part, heads_grad = turn_back(
        sc, own_dh1, core1, dh_z, x2, cotangent, second_gain, output_all
    )
    grad_rows = swapped(heads_grad).reshape(rows, local)

    h_late, heads_rows, low, sib_y0, sib_y1 = tie(h_own, heads_rows, low, sib_y0, sib_y1)
    second_came = send(graded((2, 3), 1, h_late), hop(2, group))
    first_kept = graded((0, 2), 0, h_late)
    second_kept = graded((0, 1), 1, h_late)
    share = width // size
    low_parts = low.reshape(owned, size // 2, 2, share)
    low_mine = take(low_parts, odd, 2).reshape(owned, -1)
    low_came = send(take(low_parts, 1 - odd, 2).reshape(owned, -1), sibling)
    heads_sib = send(heads_rows, sibling)
    core_y = send(jnp.stack([sib_y0, sib_y1]), sibling)
    out_grad = dot(
        jnp.concatenate([low_mine, low_came], axis=0),
        jnp.concatenate([heads_rows, heads_sib], axis=0),
        TN,
    ).astype(BF)

    first_next = add(first_kept[1], first_came[1]).astype(BF)
    grad_rows, first_next, second_kept, out_grad, core_y = tie(
        grad_rows, first_next, second_kept, out_grad, core_y
    )
    first_back = send(first_next, hop(2, group))
    y_z = send(add(own_y0, core_y[0]).astype(BF), partner)
    dq, dpair_before, dpair_here = attend_back(
        queries, pair_before, pair_here, lo, heads_out, logs, grad_rows,
        (turned_cos, turned_sin), kvheads,
    )
    dq, dpair_before, y_z = tie(dq, dpair_before, y_z)
    returned = send(dpair_before, lambda s, t: (s - 1, t))
    query_parts = swapped(dq.reshape(ways, owned, local))
    dpair = pair_grad(dpair_here, returned, cosine, sine, kvheads)
    dpair, query_parts = tie(dpair, query_parts)
    pair_parts = swapped(dpair.reshape(ways, owned, local))

    dpair, second_came, out_grad = tie(dpair, second_came, out_grad)
    second_back = send(add(second_kept[1], second_came[1]).astype(BF), hop(1, group))
    grads = jnp.concatenate([dq, dpair], axis=1)
    full = dot(inputs_one, grads, TN).astype(BF).reshape(4, -1, 2, share, 2 * local)
    full_came = send(take(full, 1 - odd, 2), sibling)
    pair_parts, full_came, out_grad = tie(pair_parts, full_came, out_grad)
    out_block = exchanged_sum(out_grad.reshape(4, -1, ways * local), group)
    tokens_grad, first_part = finish(query_parts, pair_parts, weight_all, tokens, first_gain, dx2)
    devices = size * ways
    parts = jnp.concatenate(
        [first_part.reshape(devices, -1), second_part.reshape(devices, -1)], axis=1
    )
    gains = jnp.sum(
        lax.all_to_all(parts, AXES, split_axis=0, concat_axis=0, tiled=True), axis=0
    )
    own = width // devices

    one_low = add(take(full, odd, 2), full_came).astype(BF)
    one_came = [send(take(one_low, place ^ r), hop(r, group)) for r in (1, 2, 3)]
    block = jnp.concatenate(
        [
            add(first_kept[0], first_came[0]) + first_back.astype(F32),
            add(second_kept[0], second_came[0]) + second_back.astype(F32),
        ],
        axis=2,
    )
    block = middle_scatter(block, 1, size, group)
    low_block = block.astype(BF)
    cut = lambda k: lax.dynamic_slice_in_dim(low_block, k * share, share, 1)
    crossed = send(cut(1 - odd), lambda s, t: (s ^ 1, t ^ 2) if s & 1 else (s ^ 1, t))
    second = send(low_block[:, share:], far)
    out_block = middle_scatter(out_block, 0, size, group)
    out_low = out_block.astype(BF)
    columns = lambda k: lax.dynamic_slice_in_dim(out_low, k * local, local, 1)
    out_came = [send(columns(j ^ d), lambda s, t: (s, t ^ d)) for d in (1, 2, 3)]
    gains, crossed, second = tie(gains, crossed, second)
    block = jnp.where(odd == 0, block[:, :share], second.astype(F32)) + crossed.astype(F32)
    gateup_grad = jnp.transpose(block[:2], (1, 0, 2))
    down_grad = jnp.transpose(block[2])
    total = lambda first, rest: sum((a.astype(F32) for a in rest), first.astype(F32))
    output_grad = jnp.transpose(
        total(lax.dynamic_slice_in_dim(out_block, j * local, local, 1), out_came)
    )
    one_block = total(take(one_low, place), one_came)
    one_block = middle_scatter(one_block.reshape(-1, 2 * local), 0, size, group)
    query_grad = one_block[:, :local]
    keyval_grad = one_block[:, local:].reshape(share, 2, -1)
    result = (x2[1] + (add(own_y1, core_y[1]) + y_z.astype(F32))).astype(BF)
    return (
        result, tokens_grad, gains[:own], query_grad, keyval_grad, output_grad, gains[own:],
        gateup_grad, down_grad,
    )


def solution(mesh):
    return jax.shard_map(
        body,
        mesh=mesh,
        in_specs=(
            P(AXES, None), P(), P(), P(None, "tp"), P(None, None, "tp"), P("tp", None), P(),
            P(None, None, "tp"), P("tp", None), P(AXES, None),
        ),
        out_specs=(
            P(AXES, None), P(AXES, None), P(AXES), P("seq", "tp"), P("seq", None, "tp"),
            P("tp", "seq"), P(AXES), P("seq", None, "tp"), P("tp", "seq"),
        ),
        check_vma=False,
    )
```

```python
import jax
import jax.numpy as jnp
from jax import lax
from jax.experimental import pallas as pl
from jax.experimental.pallas import tpu as pltpu
from jax.sharding import PartitionSpec as P

HEAD_DIM = 96
HALF = HEAD_DIM // 2
LANES = 128
WINDOW = 1024
TILE = 256
EPSILON = 1e-05
THETA = 100000.0
SCALE = HEAD_DIM ** (-0.5)
LOG2E = 1.4426950408889634
SCALE2 = SCALE * LOG2E
BF = jnp.bfloat16
F32 = jnp.float32
NT = (((1,), (1,)), ((), ()))
NN = (((1,), (0,)), ((), ()))
TN = (((0,), (0,)), ((), ()))
MIB = 1 << 20
AXES = ("seq", "tp")
ANY = pl.BlockSpec(memory_space=pl.ANY)


def dot(a, b, dims=NN):
    return lax.dot_general(a, b, dims, preferred_element_type=F32)


def shape(dims, dtype):
    return jax.ShapeDtypeStruct(dims, dtype)


def cost(flops, moved, exps=0):
    return pl.CostEstimate(flops=flops // 16, bytes_accessed=moved // 16, transcendentals=0)


def params(mib):
    return pltpu.CompilerParams(vmem_limit_bytes=mib * MIB)


def send(a, to):
    size, ways = lax.axis_size("seq"), lax.axis_size("tp")
    pairs = []
    for s in range(size):
        for t in range(ways):
            there = to(s, t)
            if there is not None and 0 <= there[0] < size and 0 <= there[1] < ways:
                pairs.append((s * ways + t, there[0] * ways + there[1]))
    return lax.ppermute(a, AXES, pairs)


def doc_places(lengths, token_ids):
    bounds = jnp.cumsum(lengths)
    passed = token_ids[:, None] >= bounds[None, :]
    return jnp.sum(jnp.where(passed, lengths[None, :], 0), axis=1)


def spread_halves(w):
    n = w.shape[0]
    parts = w.reshape(n, -1, 2, HALF)
    parts = jnp.pad(parts, ((0, 0), (0, 0), (0, 0), (0, LANES // 2 - HALF)))
    return parts.reshape(n, -1)


def rotation_tables(places):
    freqs = THETA ** (-2.0 * jnp.arange(HALF, dtype=F32) / HEAD_DIM)
    angles = places.astype(F32)[:, None] * freqs[None, :]
    return jnp.cos(angles), jnp.sin(angles)


def lane_tables(cosine, sine):
    fill = ((0, 0), (0, LANES // 2 - HALF))
    cosine, sine = jnp.pad(cosine, fill), jnp.pad(sine, fill)
    return (
        jnp.concatenate([cosine, cosine], axis=1),
        jnp.concatenate([-sine, sine], axis=1),
    )


def project_kernel(
    sizes, sc_ref, own, r1, r2, r3, l1, l2, l3, g_ref, w_ref, c_ref, s_ref,
    h_ref, q_ref, kv_ref, x_s, sem,
):
    qheads, kvheads, ways = sizes
    o = pl.program_id(0)
    j = sc_ref[0]
    sources = {0: own, -1: r1, -2: r2, -3: r3, 1: l1, 2: l2, 3: l3}

    def fetch(at, slot):
        for d, ref in sources.items():

            @pl.when(at - j == d)
            def _():
                pltpu.make_async_copy(ref, x_s.at[slot], sem.at[slot]).start()

    @pl.when(o == 0)
    def _():
        fetch(0, 0)

    slot = lax.rem(o, 2)

    @pl.when(o + 1 < ways)
    def _():
        fetch(o + 1, 1 - slot)

    pltpu.make_async_copy(own, x_s.at[slot], sem.at[slot]).wait()
    x = x_s[slot].astype(F32)
    scale = lax.rsqrt(jnp.mean(x * x, axis=-1, keepdims=True) + EPSILON)
    h = (x * scale * g_ref[...]).astype(BF)
    h_ref[...] = h
    flat = dot(h, w_ref[...])
    cosine, sine = c_ref[...], s_ref[...]

    def turned(n):
        u = flat[:, n * LANES : (n + 1) * LANES]
        u = u * cosine + pltpu.roll(u, LANES // 2, 1) * sine
        return jnp.concatenate([u[:, :HALF], u[:, LANES // 2 : LANES // 2 + HALF]], axis=1)

    fill = jnp.zeros((x.shape[0], LANES - HEAD_DIM), F32)
    for n in range(qheads):
        q_ref[:, n * LANES : (n + 1) * LANES] = jnp.concatenate([turned(n), fill], axis=1).astype(
            BF
        )
    keys = [turned(qheads + n) for n in range(kvheads)]
    values = [flat[:, (qheads + kvheads) * LANES :]]
    kv_ref[...] = jnp.concatenate(keys + values, axis=1).astype(BF)


def project(sc, shards, gain, weight, cosine, sine, qheads, kvheads):
    owned, width = shards[0].shape
    ways = 4
    rows = owned * ways
    wide = weight.shape[1]
    kvwide = 2 * kvheads * HEAD_DIM
    row = lambda n: pl.BlockSpec((owned, n), lambda o, sc: (o, 0))
    whole = lambda m, n: pl.BlockSpec((m, n), lambda o, sc: (0, 0))
    return pl.pallas_call(
        lambda *refs: project_kernel((qheads, kvheads, ways), *refs),
        grid_spec=pltpu.PrefetchScalarGridSpec(
            num_scalar_prefetch=1,
            grid=(ways,),
            in_specs=[ANY] * 7 + [whole(1, width), whole(width, wide), row(LANES), row(LANES)],
            out_specs=[row(width), row(qheads * LANES), row(kvwide)],
            scratch_shapes=[pltpu.VMEM((2, owned, width), BF), pltpu.SemaphoreType.DMA((2,))],
        ),
        out_shape=[
            shape((rows, width), BF),
            shape((rows, qheads * LANES), BF),
            shape((rows, kvwide), BF),
        ],
        compiler_params=params(60),
        cost_estimate=cost(2 * rows * width * wide, 4 * rows * width),
    )(sc, *shards, gain.reshape(1, width), weight, cosine, sine)


def masked(raw, first_key, lo, diagonal, query_ids):
    keys = first_key + lax.broadcasted_iota(jnp.int32, raw.shape, 0)
    ok = keys >= lo
    if diagonal:
        ok = ok & (keys <= query_ids)
    return jnp.where(ok, raw, -1e30)


def load_pairs(kp_ref, ko_ref, k_s, v_s, head, kvheads):
    rows = ko_ref.shape[0]

    @pl.when(head == 0)
    def _():
        k_s[...] = jnp.zeros_like(k_s)
        v_s[...] = jnp.zeros_like(v_s)

    for n in range(kvheads):

        @pl.when(head == n)
        def _():
            for place, ref in ((0, kp_ref), (rows, ko_ref)):
                at = n * HEAD_DIM
                k_s[place : place + rows, :HEAD_DIM] = ref[:, at : at + HEAD_DIM]
                at = (kvheads + n) * HEAD_DIM
                v_s[place : place + rows, :HEAD_DIM] = ref[:, at : at + HEAD_DIM]


def tile_parts(q_ref, lo_ref, rows, t):
    q = jnp.concatenate([q_ref[:, :LANES], q_ref[:, LANES:]], axis=0)
    lo = jnp.concatenate([lo_ref[...], lo_ref[...]], axis=1)
    ids = rows + t * TILE + lax.broadcasted_iota(jnp.int32, (1, TILE), 1)
    return q, lo, jnp.concatenate([ids, ids], axis=1)


def attend_kernel(kvheads, q_ref, kp_ref, ko_ref, lo_ref, o_ref, l_ref, k_s, v_s):
    head, t = pl.program_id(0), pl.program_id(1)
    rows = ko_ref.shape[0]
    chunks = WINDOW // TILE + 1

    @pl.when(t == 0)
    def _():
        load_pairs(kp_ref, ko_ref, k_s, v_s, head, kvheads)

    q, lo, ids = tile_parts(q_ref, lo_ref, rows, t)
    scores = []
    for c in range(chunks):
        first = pl.multiple_of((t + c) * TILE, TILE)
        raw = dot(k_s[pl.ds(first, TILE)], q, NT)
        scores.append(masked(raw, first, lo, c == chunks - 1, ids))
    top = scores[0].max(axis=0, keepdims=True)
    for s in scores[1:]:
        top = jnp.maximum(top, s.max(axis=0, keepdims=True))
    top = top * SCALE2
    total = jnp.zeros_like(top)
    mixed = jnp.zeros((LANES, 2 * TILE), F32)
    for c in range(chunks):
        first = pl.multiple_of((t + c) * TILE, TILE)
        p = jnp.exp2(scores[c] * SCALE2 - top)
        total = total + jnp.sum(p, axis=0, keepdims=True)
        mixed = mixed + dot(v_s[pl.ds(first, TILE)], p.astype(BF), TN)
    l_ref[0, 0] = top + jnp.log2(total)
    out = jnp.transpose(mixed / total).astype(BF)
    here = pl.ds(pl.multiple_of(t * TILE, TILE), TILE)
    for n in range(kvheads):

        @pl.when(head == n)
        def _():
            for g in range(2):
                at = (2 * n + g) * HEAD_DIM
                o_ref[here, at : at + HEAD_DIM] = out[g * TILE : (g + 1) * TILE, :HEAD_DIM]


def attend(queries, pair_before, pair_here, lo, kvheads):
    rows = queries.shape[0]
    tiles = rows // TILE
    whole = pl.BlockSpec((rows, 2 * kvheads * HEAD_DIM), lambda h, t: (0, 0))
    return pl.pallas_call(
        lambda *refs: attend_kernel(kvheads, *refs),
        grid=(kvheads, tiles),
        in_specs=[
            pl.BlockSpec((TILE, 2 * LANES), lambda h, t: (t, h)),
            whole,
            whole,
            pl.BlockSpec((1, TILE), lambda h, t: (0, t)),
        ],
        out_specs=[whole, pl.BlockSpec((1, 1, 1, 2 * TILE), lambda h, t: (h, t, 0, 0))],
        out_shape=[
            shape((rows, 2 * kvheads * HEAD_DIM), BF),
            shape((kvheads, tiles, 1, 2 * TILE), F32),
        ],
        scratch_shapes=[pltpu.VMEM((2 * rows, LANES), BF), pltpu.VMEM((2 * rows, LANES), BF)],
        compiler_params=params(60),
        cost_estimate=cost(6400 * MIB, 5 * MIB, 5 * MIB),
    )(queries, pair_before, pair_here, lo)


def attend_back_kernel(
    kvheads, q_ref, kp_ref, ko_ref, lo_ref, o_ref, l_ref, do_ref, c_ref, s_ref,
    dq_ref, dp_ref, dkv_ref, k_s, v_s, dk_s, dv_s,
):
    head, t = pl.program_id(0), pl.program_id(1)
    rows = ko_ref.shape[0]
    chunks = WINDOW // TILE + 1

    @pl.when(t == 0)
    def _():
        load_pairs(kp_ref, ko_ref, k_s, v_s, head, kvheads)
        dk_s[...] = jnp.zeros_like(dk_s)
        dv_s[...] = jnp.zeros_like(dv_s)

    def heads_of(both):
        pair = both[:, : 2 * HEAD_DIM]
        for n in range(1, kvheads):
            pair = jnp.where(
                head == n, both[:, 2 * n * HEAD_DIM : 2 * (n + 1) * HEAD_DIM], pair
            )
        fill = jnp.zeros((TILE, LANES - HEAD_DIM), BF)
        first = jnp.concatenate([pair[:, :HEAD_DIM], fill], axis=1)
        second = jnp.concatenate([pair[:, HEAD_DIM:], fill], axis=1)
        return jnp.concatenate([first, second], axis=0)

    q, lo, ids = tile_parts(q_ref, lo_ref, rows, t)
    grad = heads_of(do_ref[...])
    prod = grad.astype(F32) * heads_of(o_ref[...]).astype(F32)
    center = jnp.sum(jnp.transpose(prod), axis=0, keepdims=True)
    logs = l_ref[0, 0]
    dq = jnp.zeros((LANES, 2 * TILE), F32)
    for c in range(chunks):
        first = pl.multiple_of((t + c) * TILE, TILE)
        here = pl.ds(first, TILE)
        keys = k_s[here]
        raw = masked(dot(keys, q, NT), first, lo, c == chunks - 1, ids)
        p = jnp.exp2(raw * SCALE2 - logs)
        dp = dot(v_s[here], grad, NT)
        ds = (p * (dp - center)).astype(BF)
        dv_s[here] += dot(p.astype(BF), grad)
        dk_s[here] += dot(ds, q)
        dq = dq + dot(keys, ds, TN)
    cosine = jnp.concatenate([c_ref[...], c_ref[...]], axis=1)
    sine = jnp.concatenate([s_ref[...], s_ref[...]], axis=1)
    a, b = dq[:HALF] * SCALE, dq[HALF:HEAD_DIM] * SCALE
    fill = jnp.zeros((LANES - HEAD_DIM, 2 * TILE), F32)
    dq = jnp.concatenate([a * cosine + b * sine, b * cosine - a * sine, fill], axis=0)
    dq = jnp.transpose(dq).astype(BF)
    mine = pl.ds(pl.multiple_of(t * TILE, TILE), TILE)
    last = t == pl.num_programs(1) - 1
    for n in range(kvheads):

        @pl.when(head == n)
        def _():
            for g in range(2):
                at = (2 * n + g) * HEAD_DIM
                dq_ref[mine, at : at + HEAD_DIM] = dq[g * TILE : (g + 1) * TILE, :HEAD_DIM]

        @pl.when((head == n) & last)
        def _():
            at = n * HEAD_DIM
            dp_ref[:, at : at + HEAD_DIM] = (dk_s[:rows, :HEAD_DIM] * SCALE).astype(BF)
            dkv_ref[:, at : at + HEAD_DIM] = dk_s[rows:, :HEAD_DIM] * SCALE
            at = (kvheads + n) * HEAD_DIM
            dp_ref[:, at : at + HEAD_DIM] = dv_s[:rows, :HEAD_DIM].astype(BF)
            dkv_ref[:, at : at + HEAD_DIM] = dv_s[rows:, :HEAD_DIM]


def attend_back(queries, pair_before, pair_here, lo, heads_out, logs, grads, tables, kvheads):
    rows = queries.shape[0]
    tiles = rows // TILE
    wide = 2 * kvheads * HEAD_DIM
    whole = pl.BlockSpec((rows, wide), lambda h, t: (0, 0))
    table = pl.BlockSpec((HALF, TILE), lambda h, t: (0, t))
    return pl.pallas_call(
        lambda *refs: attend_back_kernel(kvheads, *refs),
        grid=(kvheads, tiles),
        in_specs=[
            pl.BlockSpec((TILE, 2 * LANES), lambda h, t: (t, h)),
            whole,
            whole,
            pl.BlockSpec((1, TILE), lambda h, t: (0, t)),
            pl.BlockSpec((TILE, wide), lambda h, t: (t, 0)),
            pl.BlockSpec((1, 1, 1, 2 * TILE), lambda h, t: (h, t, 0, 0)),
            pl.BlockSpec((TILE, wide), lambda h, t: (t, 0)),
            table,
            table,
        ],
        out_specs=[whole, whole, whole],
        scratch_shapes=[
            pltpu.VMEM((2 * rows, LANES), BF),
            pltpu.VMEM((2 * rows, LANES), BF),
            pltpu.VMEM((2 * rows, LANES), F32),
            pltpu.VMEM((2 * rows, LANES), F32),
        ],
        out_shape=[shape((rows, wide), BF), shape((rows, wide), BF), shape((rows, wide), F32)],
        compiler_params=params(60),
        cost_estimate=cost(16000 * MIB, 8 * MIB, 5 * MIB),
    )(queries, pair_before, pair_here, lo, heads_out, logs, grads, *tables)


def shard(w_ref, k):
    pieces, _, part, width = w_ref.shape
    return w_ref[:, pl.ds(k, 1)].reshape(pieces * part, width)


def mix_kernel(
    sc_ref, o_ref, w_ref, x_ref, xr_ref, xl_ref, g_ref, x2_ref, h2_ref, row_ref
):
    m = pl.program_id(0)
    j = sc_ref[0]
    ways = o_ref.shape[0]
    acc = dot(o_ref[0], shard(w_ref, j))
    for k in range(1, ways):
        acc = acc + dot(o_ref[k], shard(w_ref, j ^ k))
    other = jnp.where((j & 1) == 1, xr_ref[...], xl_ref[...])
    x2 = jnp.where(m == 1, x_ref[...], other).astype(F32) + acc
    x2_ref[0] = x2
    scale = lax.rsqrt(jnp.mean(x2 * x2, axis=-1, keepdims=True) + EPSILON)
    h2_ref[0] = (x2 * scale * g_ref[...]).astype(BF)

    @pl.when(m == 1)
    def _():
        row_ref[...] = jnp.concatenate([o_ref[k] for k in range(ways)], axis=1)


def mix(sc, parts, weight, tokens, right, left, gain):
    owned, width = tokens.shape
    ways, _, local = parts.shape
    whole = lambda *dims: pl.BlockSpec(dims, lambda m, sc: (0,) * len(dims))
    return pl.pallas_call(
        mix_kernel,
        grid_spec=pltpu.PrefetchScalarGridSpec(
            num_scalar_prefetch=1,
            grid=(2,),
            in_specs=[
                pl.BlockSpec((ways, owned, local), lambda m, sc: (0, (sc[0] & 1) ^ 1 ^ m, 0)),
                whole(*weight.shape),
                whole(owned, width),
                whole(owned, width),
                whole(owned, width),
                whole(1, width),
            ],
            out_specs=[
                pl.BlockSpec((1, owned, width), lambda m, sc: (m, 0, 0)),
                pl.BlockSpec((1, owned, width), lambda m, sc: (m, 0, 0)),
                whole(owned, ways * local),
            ],
        ),
        out_shape=[
            shape((2, owned, width), F32),
            shape((2, owned, width), BF),
            shape((owned, ways * local), BF),
        ],
        compiler_params=params(60),
        cost_estimate=cost(1, 1),
    )(sc, parts, weight, tokens, right, left, gain.reshape(1, width))


def feed_kernel(
    sc_ref, ho_ref, hs_ref, co_ref, cs_ref, gu_own, d_own, w0, w1, w2, w3,
    a_ref, dg_ref, du_ref, sib_dh, own_dh, sib_y, own_y, w_s, a_s, dg_s, du_s, sem,
):
    r = pl.program_id(0)
    steps = pl.num_programs(0)
    place, odd = sc_ref[1], sc_ref[2]
    taken = [w0, w1, w2, w3]
    span = a_ref.shape[1]
    into = [pl.ds(k * span, span) for k in range(len(taken))]

    def fetch(at):
        for k, w in enumerate(taken):

            @pl.when((at == k) & (odd == 0))
            def _():
                part = pl.ds(pl.multiple_of((place ^ k) * span, span), span)
                pltpu.make_async_copy(
                    gu_own.at[:, :, part], w_s.at[pl.ds(0, 2), :, into[k]], sem.at[0, k]
                ).start()
                pltpu.make_async_copy(
                    d_own.at[:, part], w_s.at[2, :, into[k]], sem.at[1, k]
                ).start()

            @pl.when((at == k) & (odd == 1))
            def _():
                pltpu.make_async_copy(
                    w.at[pl.ds(0, 2)], w_s.at[pl.ds(0, 2), :, into[k]], sem.at[0, k]
                ).start()
                pltpu.make_async_copy(w.at[2], w_s.at[2, :, into[k]], sem.at[1, k]).start()

    @pl.when(r == 0)
    def _():
        fetch(0)

    @pl.when(r + 1 < steps)
    def _():
        fetch(r + 1)

    here = pl.ds(pl.multiple_of(r * span, span), span)
    pltpu.make_async_copy(
        w0.at[pl.ds(0, 2)], w_s.at[pl.ds(0, 2), :, here], sem.at[0, r]
    ).wait()
    pltpu.make_async_copy(w0.at[2], w_s.at[2, :, here], sem.at[1, r]).wait()
    h = jnp.concatenate([hs_ref[0], ho_ref[0]], axis=0)
    ct = jnp.concatenate([cs_ref[0], co_ref[0]], axis=0)
    gate = dot(h, w_s[0, :, here])
    up = dot(h, w_s[1, :, here])
    da = dot(ct, w_s[2, :, here])
    sig = jax.nn.sigmoid(gate)
    act = gate * sig
    a = (act * up).astype(BF)
    dgate = (da * up * sig * (1.0 + gate * (1.0 - sig))).astype(BF)
    dup = (da * act).astype(BF)
    for ref, whole, value in ((a_ref, a_s, a), (dg_ref, dg_s, dgate), (du_ref, du_s, dup)):
        ref[...] = value
        whole[:, here] = value

    @pl.when(r == steps - 1)
    def _():
        half = sib_dh.shape[0]
        for k, (dh_ref, y_ref) in enumerate(((sib_dh, sib_y), (own_dh, own_y))):
            rows = pl.ds(k * half, half)
            dh_ref[...] = (dot(dg_s[rows], w_s[0], NT) + dot(du_s[rows], w_s[1], NT)).astype(BF)
            y_ref[...] = dot(a_s[rows], w_s[2], NT).astype(BF)


def feed(m, sc, h_own, h_sib, ct_own, ct_sib, gu_own, d_own, taken):
    _, owned, width = h_own.shape
    units = d_own.shape[1]
    span = units // 4
    rows = pl.BlockSpec((1, owned, width), lambda r, sc: (m, 0, 0))
    out = pl.BlockSpec((2 * owned, span), lambda r, sc: (0, sc[1] ^ r))
    whole = pl.BlockSpec((owned, width), lambda r, sc: (0, 0))
    return pl.pallas_call(
        feed_kernel,
        grid_spec=pltpu.PrefetchScalarGridSpec(
            num_scalar_prefetch=1,
            grid=(4,),
            in_specs=[rows] * 4 + [ANY] * 6,
            out_specs=[out, out, out] + [whole] * 4,
            scratch_shapes=[pltpu.VMEM((3, width, units), BF)]
            + [pltpu.VMEM((2 * owned, units), BF)] * 3
            + [pltpu.SemaphoreType.DMA((2, 4))],
        ),
        out_shape=[shape((2 * owned, units), BF)] * 3 + [shape((owned, width), BF)] * 4,
        compiler_params=params(60),
        cost_estimate=cost(36 * owned * width * units, 22 * MIB, 2 * owned * units),
    )(sc, h_own, h_sib, ct_own, ct_sib, gu_own, d_own, *taken)


def feed_grad_kernel(
    sc_ref, ho0, hs0, co0, cs0, ho1, hs1, co1, cs1, a0, dg0, du0, a1, dg1, du1, out_ref
):
    part = ho0.shape[2]
    both = lambda x, y: jnp.concatenate([x[...], y[...]], axis=0)
    rows = lambda own, sib: jnp.concatenate([sib[0], own[0], sib[1], own[1]], axis=0)
    h = jnp.concatenate([rows(ho0, hs0), rows(ho1, hs1)], axis=1)
    ct = jnp.concatenate([rows(co0, cs0), rows(co1, cs1)], axis=1)
    for n, (left, right) in enumerate(
        ((h, both(dg0, dg1)), (h, both(du0, du1)), (ct, both(a0, a1)))
    ):
        grad = dot(left, right, TN).astype(BF)
        for k in range(2):
            out_ref[k, n] = grad[k * part : (k + 1) * part]


def feed_grad(blocks, half, sc, h_own, h_sib, ct_own, ct_sib, first, second):
    _, owned, width = h_own.shape
    units = first[0].shape[1] // 2
    part = width // 4
    cut = 2
    lanes = lambda r: pl.BlockSpec((2, owned, part), lambda n, sc: (0, 0, sc[1] ^ r))
    right = pl.BlockSpec((2 * owned, units // cut), lambda n, sc: (0, half * cut + n))
    return pl.pallas_call(
        feed_grad_kernel,
        grid_spec=pltpu.PrefetchScalarGridSpec(
            num_scalar_prefetch=1,
            grid=(cut,),
            in_specs=[lanes(blocks[0])] * 4 + [lanes(blocks[1])] * 4 + [right] * 6,
            out_specs=pl.BlockSpec((2, 3, part, units // cut), lambda n, sc: (0, 0, 0, n)),
        ),
        out_shape=shape((2, 3, part, units), BF),
        compiler_params=params(60),
        cost_estimate=cost(48 * owned * part * units, 14 * MIB),
    )(sc, *([h_own, h_sib, ct_own, ct_sib] * 2), *first, *second)


def norm_back(dn, v, gain):
    r = lax.rsqrt(jnp.mean(v * v, axis=-1, keepdims=True) + EPSILON)
    scaled = gain * dn
    gain_grad = jnp.sum(dn * (v * r), axis=0, keepdims=True)
    return r * scaled - v * (r * r * r) * jnp.mean(scaled * v, axis=-1, keepdims=True), gain_grad


def turn_back_kernel(
    sc_ref, a_ref, b_ref, z_ref, x2_ref, ct_ref, g_ref, w_ref, dx_ref, db_ref, gain_ref, do_ref
):
    dn = a_ref[...].astype(F32) + b_ref[...].astype(F32) + z_ref[...].astype(F32)
    dv, gain_grad = norm_back(dn, x2_ref[0], g_ref[...])
    gain_ref[...] = gain_grad
    dx = ct_ref[...].astype(F32) + dv
    dx_ref[...] = dx
    low = dx.astype(BF)
    db_ref[...] = low
    j = sc_ref[0]
    for d in range(do_ref.shape[0]):
        do_ref[j ^ d] = dot(low, shard(w_ref, d), NT).astype(BF)


def turn_back(sc, mine, core, tp, x2, cotangent, gain, weight):
    owned, width = cotangent.shape
    ways, local = weight.shape[1], weight.shape[0] * weight.shape[2]
    whole = lambda *dims: pl.BlockSpec(dims, lambda n, sc: (0,) * len(dims))
    own = pl.BlockSpec((1, owned, width), lambda n, sc: (1, 0, 0))
    return pl.pallas_call(
        turn_back_kernel,
        grid_spec=pltpu.PrefetchScalarGridSpec(
            num_scalar_prefetch=1,
            grid=(1,),
            in_specs=[
                whole(owned, width),
                whole(owned, width),
                whole(owned, width),
                own,
                whole(owned, width),
                whole(1, width),
                whole(*weight.shape),
            ],
            out_specs=[
                whole(owned, width),
                whole(owned, width),
                whole(1, width),
                whole(ways, owned, local),
            ],
        ),
        out_shape=[
            shape((owned, width), F32),
            shape((owned, width), BF),
            shape((1, width), F32),
            shape((ways, owned, local), BF),
        ],
        compiler_params=params(60),
        cost_estimate=cost(2 * owned * width * ways * local, 12 * MIB),
    )(sc, mine, core, tp, x2, cotangent, gain.reshape(1, width), weight)


def pair_grad_kernel(kvheads, own_ref, back_ref, c_ref, s_ref, out_ref):
    total = own_ref[...] + back_ref[...].astype(F32)
    cosine, sine = c_ref[...], s_ref[...]
    parts = []
    for n in range(kvheads):
        a = total[:, n * HEAD_DIM : n * HEAD_DIM + HALF]
        b = total[:, n * HEAD_DIM + HALF : (n + 1) * HEAD_DIM]
        parts += [a * cosine + b * sine, b * cosine - a * sine]
    parts.append(total[:, kvheads * HEAD_DIM :])
    out_ref[...] = jnp.concatenate(parts, axis=1).astype(BF)


def pair_grad(own, back, cosine, sine, kvheads):
    rows, wide = own.shape
    row = lambda n: pl.BlockSpec((TILE, n), lambda t: (t, 0))
    return pl.pallas_call(
        lambda *refs: pair_grad_kernel(kvheads, *refs),
        grid=(rows // TILE,),
        in_specs=[row(wide), row(wide), row(HALF), row(HALF)],
        out_specs=row(wide),
        out_shape=shape((rows, wide), BF),
        compiler_params=params(60),
        cost_estimate=cost(MIB, 4 * MIB),
    )(own, back, cosine, sine)


def finish_kernel(
    sc_ref, q_ref, k_ref, w_ref, v_ref, x_ref, g_ref, dx_ref, out_ref, gain_ref, acc
):
    d = pl.program_id(0)
    even = sc_ref[2] == 0
    mine = jnp.where(even, q_ref[0], k_ref[0])
    other = jnp.where(even, k_ref[0], q_ref[0])
    term = dot(mine, shard(w_ref, 0)) + dot(other, shard(v_ref, 0))

    @pl.when(d == 0)
    def _():
        acc[...] = term

    @pl.when(d > 0)
    def _():
        acc[...] += term

    @pl.when(d == pl.num_programs(0) - 1)
    def _():
        dv, gain_grad = norm_back(acc[...], x_ref[...].astype(F32), g_ref[...])
        out_ref[...] = dx_ref[...] + dv
        gain_ref[...] = gain_grad


def finish(sc, query_parts, pair_parts, weight, others, tokens, gain, dx):
    owned, width = tokens.shape
    pieces, ways, part, _ = weight.shape
    local = query_parts.shape[2]
    whole = lambda *dims: pl.BlockSpec(dims, lambda d, sc: (0,) * len(dims))
    one = pl.BlockSpec((1, owned, local), lambda d, sc: (d, 0, 0))
    half = pl.BlockSpec((pieces, 1, part, width), lambda d, sc: (0, d, 0, 0))
    return pl.pallas_call(
        finish_kernel,
        grid_spec=pltpu.PrefetchScalarGridSpec(
            num_scalar_prefetch=1,
            grid=(ways,),
            in_specs=[
                one, one, half, half, whole(owned, width), whole(1, width), whole(owned, width)
            ],
            out_specs=[whole(owned, width), whole(1, width)],
            scratch_shapes=[pltpu.VMEM((owned, width), F32)],
        ),
        out_shape=[shape((owned, width), F32), shape((1, width), F32)],
        compiler_params=params(60),
        cost_estimate=cost(1, 1),
    )(sc, query_parts, pair_parts, weight, others, tokens, gain.reshape(1, width), dx)


def tie(*values):
    return lax.optimization_barrier(values)


def hop(bit, group):
    return lambda s, t: (s ^ (bit * group), t)


def exchanged(pieces, group):
    groups = [[r + k * group for k in range(4)] for r in range(group)]
    return lax.all_to_all(
        pieces, "seq", split_axis=0, concat_axis=0, axis_index_groups=groups, tiled=True
    )


def swapped(pieces):
    return lax.all_to_all(pieces, "tp", split_axis=0, concat_axis=0, tiled=True)


def take(a, index, axis=0):
    return lax.dynamic_index_in_dim(a, index, axis, keepdims=False)


def middle_scatter(a, axis, size, group):
    middle = group // 2
    if middle == 1:
        return a
    groups = [
        [g * group + 2 * m + c for m in range(middle)] for g in range(size // group) for c in (0, 1)
    ]
    return lax.psum_scatter(
        a, "seq", scatter_dimension=axis, tiled=True, axis_index_groups=groups
    )


def gain_sum(part):
    devices = lax.axis_size("seq") * lax.axis_size("tp")
    parts = lax.all_to_all(
        part.reshape(devices, -1), AXES, split_axis=0, concat_axis=0, tiled=True
    )
    return jnp.sum(parts, axis=0)


def body(
    tokens, lengths, first_gain, w_query, w_keyval, w_output, second_gain, w_gateup, w_down,
    cotangent,
):
    size, ways = lax.axis_size("seq"), lax.axis_size("tp")
    owned, width = tokens.shape
    rows = owned * ways
    local = w_query.shape[1]
    qheads = local // HEAD_DIM
    kvheads = w_keyval.shape[2] // HEAD_DIM
    units = w_down.shape[0]
    span = units // 4
    group = size // 4
    i, j = lax.axis_index("seq"), lax.axis_index("tp")
    odd = i & 1
    place = i // group
    sc = jnp.stack([j, place, odd]).astype(jnp.int32)
    sibling = lambda s, t: (s ^ 1, t)
    partner = lambda s, t: (s, t ^ 1)

    near = lambda a: lax.dynamic_slice_in_dim(a, place * span, span, a.ndim - 1)
    far = lambda s, t: (s, t ^ 2) if s & 1 else None
    hop_odd = lambda bit: lambda s, t: (s ^ (bit * group), t) if s & 1 else None
    up = lambda a, k: send(a, lambda s, t: (s, t + 1) if t >= k else None)
    down = lambda a, k: send(a, lambda s, t: (s, t - 1) if t < ways - k else None)
    pieces = 8
    eights = [list(range(k, k + pieces)) for k in range(0, size, pieces)]

    def own_piece(w):
        part = w.shape[0] // pieces
        return lax.dynamic_slice_in_dim(w, (i % pieces) * part, part, 0)

    def gathered(parts):
        return lax.all_gather(parts, "seq", axis=0, axis_index_groups=eights)

    r1, l1 = up(tokens, 0), down(tokens, 0)
    output_mine = own_piece(w_output)
    o1, o2, o3 = (send(output_mine, lambda s, t: (s, t ^ d)) for d in (1, 2, 3))
    gateup_own = jnp.transpose(w_gateup, (1, 0, 2))
    down_own = jnp.transpose(w_down)
    r1, l1, gateup_own, down_own, w_query, w_keyval = tie(
        r1, l1, gateup_own, down_own, w_query, w_keyval
    )
    r2, l2 = up(r1, 1), down(l1, 1)
    piece = jnp.concatenate([near(gateup_own), near(down_own)[None]], axis=0)
    weight_one = jnp.concatenate(
        [spread_halves(w_query), spread_halves(w_keyval[:, 0]), w_keyval[:, 1]], axis=1
    )
    r2, l2, weight_one, piece, lengths, o1, o2, o3 = tie(
        r2, l2, weight_one, piece, lengths, o1, o2, o3
    )
    output_all = gathered(jnp.stack([output_mine, o1, o2, o3]))
    r3, l3 = up(r2, 2), down(l2, 2)
    w0 = send(piece, far)
    start_id = i * rows
    query_ids = start_id + jnp.arange(rows, dtype=jnp.int32)
    begins = doc_places(lengths, query_ids)
    cosine, sine = rotation_tables(query_ids - begins)
    lo = jnp.maximum(query_ids - (WINDOW - 1), begins) - (start_id - rows)
    lo = lo.reshape(1, rows)
    lane_cos, lane_sin = lane_tables(cosine, sine)
    turned_cos, turned_sin = jnp.transpose(cosine), jnp.transpose(sine)
    flat = jnp.concatenate(
        [jnp.transpose(w_query), jnp.transpose(w_keyval, (1, 2, 0)).reshape(-1, width)], axis=0
    )
    part = flat.shape[0] // 8
    flat_mine = lax.dynamic_slice_in_dim(flat, (4 * odd + place) * part, part, 0)
    r3, l3, lane_cos, lane_sin, turned_cos, turned_sin, lo, flat_mine = tie(
        r3, l3, lane_cos, lane_sin, turned_cos, turned_sin, lo, flat_mine
    )
    inputs_one, queries, pair_here = project(
        sc, [tokens, r1, r2, r3, l1, l2, l3], first_gain, weight_one, lane_cos, lane_sin,
        qheads, kvheads,
    )
    pair_before = send(pair_here, lambda s, t: (s + 1, t))
    pair_here, ct_late = tie(pair_here, cotangent)
    ct_partner = send(ct_late, partner)
    heads_out, logs = attend(queries, pair_before, pair_here, lo, kvheads)

    heads_out, w0 = tie(heads_out, w0)
    pairs_of = lambda a: jnp.repeat(a.reshape(2, 2 * owned, local), 2, axis=0)
    head_parts = swapped(pairs_of(heads_out))
    w1, w2, w3 = (send(w0, hop_odd(bit)) for bit in (1, 2, 3))
    head_parts, flat_mine = tie(head_parts, flat_mine)
    flat_parts = swapped(jnp.broadcast_to(flat_mine[None], (ways, *flat_mine.shape)))
    x2, h_own, heads_rows = mix(sc, head_parts, output_all, tokens, r1, l1, second_gain)
    ct_own = jnp.stack([ct_partner, cotangent])
    h_own, w1, w2, w3, ct_own = tie(h_own, w1, w2, w3, ct_own)
    h_sib = send(h_own, sibling)
    ct_sib = send(ct_own, sibling)
    h_sib, ct_sib, flat_parts = tie(h_sib, ct_sib, flat_parts)
    fours = [[r + k * group for k in range(4)] for r in range(group)]
    weight_half = lax.all_gather(flat_parts, "seq", axis=0, axis_index_groups=fours)
    fed = lambda m, h: feed(
        m, sc, h, h_sib, ct_own, ct_sib, gateup_own, down_own, (w0, w1, w2, w3)
    )
    add = lambda a, b: a.astype(F32) + b.astype(F32)
    a0, dg0, du0, sib_dh0, own_dh0, sib_y0, own_y0 = fed(0, h_own)
    core0 = send(sib_dh0, sibling)
    dh_part = add(own_dh0, core0).astype(BF)
    dh_part, h_next = tie(dh_part, h_own)
    dh_z = send(dh_part, partner)
    a1, dg1, du1, sib_dh1, own_dh1, sib_y1, own_y1 = fed(1, h_next)
    sib_dh1, dh_z = tie(sib_dh1, dh_z)
    core1 = send(sib_dh1, sibling)
    graded = lambda blocks, half, h: feed_grad(
        blocks, half, sc, h, h_sib, ct_own, ct_sib, (a0, dg0, du0), (a1, dg1, du1)
    )
    first_away, core1 = tie(graded((1, 3), 0, h_own), core1)
    first_came = send(first_away, hop(1, group))
    dx2, low, second_part, heads_grad = turn_back(
        sc, own_dh1, core1, dh_z, x2, cotangent, second_gain, output_all
    )
    grad_rows = swapped(heads_grad).reshape(rows, local)

    h_late, heads_rows, low, sib_y0, sib_y1 = tie(h_own, heads_rows, low, sib_y0, sib_y1)
    second_came = send(graded((2, 3), 1, h_late), hop(2, group))
    first_kept = graded((0, 2), 0, h_late)
    second_kept = graded((0, 1), 1, h_late)
    share = width // size
    low_parts = low.reshape(owned, size // 2, 2, share)
    low_mine = take(low_parts, odd, 2).reshape(owned, -1)
    low_came = send(take(low_parts, 1 - odd, 2).reshape(owned, -1), sibling)
    heads_sib = send(heads_rows, sibling)
    core_y = send(jnp.stack([sib_y0, sib_y1]), sibling)
    grad_rows, first_kept, second_kept, core_y, low_came, heads_sib = tie(
        grad_rows, first_kept, second_kept, core_y, low_came, heads_sib
    )
    y_z = send(add(own_y0, core_y[0]).astype(BF), partner)
    dq, dpair_before, dpair_here = attend_back(
        queries, pair_before, pair_here, lo, heads_out, logs, grad_rows,
        (turned_cos, turned_sin), kvheads,
    )
    dq, dpair_before, first_came, y_z = tie(dq, dpair_before, first_came, y_z)
    returned = send(dpair_before, lambda s, t: (s - 1, t))
    query_parts = swapped(dq.reshape(ways, owned, local))
    first_next = add(first_kept[1], first_came[1]).astype(BF)
    returned, first_next, second_came, weight_half = tie(
        returned, first_next, second_came, weight_half
    )
    first_back = send(first_next, hop(2, group))
    second_back = send(add(second_kept[1], second_came[1]).astype(BF), hop(1, group))
    weight_other = send(weight_half, sibling)
    dpair = pair_grad(dpair_here, returned, cosine, sine, kvheads)
    dpair, query_parts = tie(dpair, query_parts)
    pair_parts = swapped(dpair.reshape(ways, owned, local))

    dpair, low_mine = tie(dpair, low_mine)
    out_grad = dot(
        jnp.concatenate([low_mine, low_came], axis=0),
        jnp.concatenate([heads_rows, heads_sib], axis=0),
        TN,
    ).astype(BF)

    out_grad, first_back, second_back = tie(out_grad, first_back, second_back)
    block = jnp.concatenate(
        [
            add(first_kept[0], first_came[0]) + first_back.astype(F32),
            add(second_kept[0], second_came[0]) + second_back.astype(F32),
        ],
        axis=2,
    )
    block = middle_scatter(block, 1, size, group)
    low_block = block.astype(BF)
    cut = lambda k: lax.dynamic_slice_in_dim(low_block, k * share, share, 1)
    crossed_out, second_out = cut(1 - odd), low_block[:, share:]
    grads = jnp.concatenate([dq, dpair], axis=1)
    full = dot(inputs_one, grads, TN).astype(BF).reshape(4, -1, 2, share, 2 * local)
    full_came = send(take(full, 1 - odd, 2), sibling)
    pair_parts, full_came, crossed_out, second_out, out_grad = tie(
        pair_parts, full_came, crossed_out, second_out, out_grad
    )
    out_parts = exchanged(out_grad.reshape(4, -1, ways * local), group)
    crossed = send(crossed_out, lambda s, t: (s ^ 1, t ^ 2) if s & 1 else (s ^ 1, t))
    second = send(second_out, far)
    tokens_grad, first_part = finish(
        sc, query_parts, pair_parts, weight_half, weight_other, tokens, first_gain, dx2
    )
    first_part, full_came, own_y1 = tie(first_part, full_came, own_y1)
    one_low = add(take(full, odd, 2), full_came).astype(BF)
    one_came = [send(take(one_low, place ^ r), hop(r, group)) for r in (1, 2, 3)]
    first_part, out_parts = tie(first_part, out_parts)
    devices = size * ways
    parts = jnp.concatenate(
        [first_part.reshape(devices, -1), second_part.reshape(devices, -1)], axis=1
    )
    gains = jnp.sum(
        lax.all_to_all(parts, AXES, split_axis=0, concat_axis=0, tiled=True), axis=0
    )
    own = width // devices

    out_block = middle_scatter(jnp.sum(out_parts.astype(F32), axis=0), 0, size, group)
    out_low = out_block.astype(BF)
    columns = lambda k: lax.dynamic_slice_in_dim(out_low, k * local, local, 1)
    out_came = [send(columns(j ^ d), lambda s, t: (s, t ^ d)) for d in (1, 2, 3)]
    total = lambda first, rest: sum((a.astype(F32) for a in rest), first.astype(F32))
    output_grad = jnp.transpose(
        total(lax.dynamic_slice_in_dim(out_block, j * local, local, 1), out_came)
    )
    one_block = total(take(one_low, place), one_came)
    one_block = middle_scatter(one_block.reshape(-1, 2 * local), 0, size, group)
    query_grad = one_block[:, :local]
    keyval_grad = one_block[:, local:].reshape(share, 2, -1)
    gains, crossed, second = tie(gains, crossed, second)
    block = jnp.where(odd == 0, block[:, :share], second.astype(F32)) + crossed.astype(F32)
    gateup_grad = jnp.transpose(block[:2], (1, 0, 2))
    down_grad = jnp.transpose(block[2])
    result = (x2[1] + (add(own_y1, core_y[1]) + y_z.astype(F32))).astype(BF)
    return (
        result, tokens_grad, gains[:own], query_grad, keyval_grad, output_grad, gains[own:],
        gateup_grad, down_grad,
    )


def solution(mesh):
    return jax.shard_map(
        body,
        mesh=mesh,
        in_specs=(
            P(AXES, None), P(), P(), P(None, "tp"), P(None, None, "tp"), P("tp", None), P(),
            P(None, None, "tp"), P("tp", None), P(AXES, None),
        ),
        out_specs=(
            P(AXES, None), P(AXES, None), P(AXES), P("seq", "tp"), P("seq", None, "tp"),
            P("tp", "seq"), P(AXES), P("seq", None, "tp"), P("tp", "seq"),
        ),
        check_vma=False,
    )
```

```python
import jax
import jax.numpy as jnp
from jax import lax
from jax.experimental import pallas as pl
from jax.experimental.pallas import tpu as pltpu
from jax.sharding import PartitionSpec as P

HEAD_DIM = 96
HALF = HEAD_DIM // 2
LANES = 128
WINDOW = 1024
TILE = 256
EPSILON = 1e-05
THETA = 100000.0
SCALE = HEAD_DIM ** (-0.5)
LOG2E = 1.4426950408889634
SCALE2 = SCALE * LOG2E
BF = jnp.bfloat16
F32 = jnp.float32
NT = (((1,), (1,)), ((), ()))
NN = (((1,), (0,)), ((), ()))
TN = (((0,), (0,)), ((), ()))
MIB = 1 << 20
AXES = ("seq", "tp")
ANY = pl.BlockSpec(memory_space=pl.ANY)


def dot(a, b, dims=NN):
    return lax.dot_general(a, b, dims, preferred_element_type=F32)


def shape(dims, dtype):
    return jax.ShapeDtypeStruct(dims, dtype)


def cost(flops, moved, exps=0):
    return pl.CostEstimate(flops=flops // 16, bytes_accessed=moved // 16, transcendentals=0)


def params(mib):
    return pltpu.CompilerParams(vmem_limit_bytes=mib * MIB)


def send(a, to):
    size, ways = lax.axis_size("seq"), lax.axis_size("tp")
    pairs = []
    for s in range(size):
        for t in range(ways):
            there = to(s, t)
            if there is not None and 0 <= there[0] < size and 0 <= there[1] < ways:
                pairs.append((s * ways + t, there[0] * ways + there[1]))
    return lax.ppermute(a, AXES, pairs)


def doc_places(lengths, token_ids):
    bounds = jnp.cumsum(lengths)
    passed = token_ids[:, None] >= bounds[None, :]
    return jnp.sum(jnp.where(passed, lengths[None, :], 0), axis=1)


def spread_halves(w):
    n = w.shape[0]
    parts = w.reshape(n, -1, 2, HALF)
    parts = jnp.pad(parts, ((0, 0), (0, 0), (0, 0), (0, LANES // 2 - HALF)))
    return parts.reshape(n, -1)


def rotation_tables(places):
    freqs = THETA ** (-2.0 * jnp.arange(HALF, dtype=F32) / HEAD_DIM)
    angles = places.astype(F32)[:, None] * freqs[None, :]
    return jnp.cos(angles), jnp.sin(angles)


def lane_tables(cosine, sine):
    fill = ((0, 0), (0, LANES // 2 - HALF))
    cosine, sine = jnp.pad(cosine, fill), jnp.pad(sine, fill)
    return (
        jnp.concatenate([cosine, cosine], axis=1),
        jnp.concatenate([-sine, sine], axis=1),
    )


def project_kernel(
    sizes, sc_ref, own, r1, r2, r3, l1, l2, l3, g_ref, w_ref, c_ref, s_ref,
    h_ref, q_ref, kv_ref, x_s, sem,
):
    qheads, kvheads, ways = sizes
    o = pl.program_id(0)
    j = sc_ref[0]
    sources = {0: own, -1: r1, -2: r2, -3: r3, 1: l1, 2: l2, 3: l3}

    def fetch(at, slot):
        for d, ref in sources.items():

            @pl.when(at - j == d)
            def _():
                pltpu.make_async_copy(ref, x_s.at[slot], sem.at[slot]).start()

    @pl.when(o == 0)
    def _():
        fetch(0, 0)

    slot = lax.rem(o, 2)

    @pl.when(o + 1 < ways)
    def _():
        fetch(o + 1, 1 - slot)

    pltpu.make_async_copy(own, x_s.at[slot], sem.at[slot]).wait()
    x = x_s[slot].astype(F32)
    scale = lax.rsqrt(jnp.mean(x * x, axis=-1, keepdims=True) + EPSILON)
    h = (x * scale * g_ref[...]).astype(BF)
    h_ref[...] = h
    flat = dot(h, w_ref[...])
    cosine, sine = c_ref[...], s_ref[...]

    def turned(n):
        u = flat[:, n * LANES : (n + 1) * LANES]
        u = u * cosine + pltpu.roll(u, LANES // 2, 1) * sine
        return jnp.concatenate([u[:, :HALF], u[:, LANES // 2 : LANES // 2 + HALF]], axis=1)

    fill = jnp.zeros((x.shape[0], LANES - HEAD_DIM), F32)
    for n in range(qheads):
        q_ref[:, n * LANES : (n + 1) * LANES] = jnp.concatenate([turned(n), fill], axis=1).astype(
            BF
        )
    keys = [turned(qheads + n) for n in range(kvheads)]
    values = [flat[:, (qheads + kvheads) * LANES :]]
    kv_ref[...] = jnp.concatenate(keys + values, axis=1).astype(BF)


def project(sc, shards, gain, weight, cosine, sine, qheads, kvheads):
    owned, width = shards[0].shape
    ways = 4
    rows = owned * ways
    wide = weight.shape[1]
    kvwide = 2 * kvheads * HEAD_DIM
    row = lambda n: pl.BlockSpec((owned, n), lambda o, sc: (o, 0))
    whole = lambda m, n: pl.BlockSpec((m, n), lambda o, sc: (0, 0))
    return pl.pallas_call(
        lambda *refs: project_kernel((qheads, kvheads, ways), *refs),
        grid_spec=pltpu.PrefetchScalarGridSpec(
            num_scalar_prefetch=1,
            grid=(ways,),
            in_specs=[ANY] * 7 + [whole(1, width), whole(width, wide), row(LANES), row(LANES)],
            out_specs=[row(width), row(qheads * LANES), row(kvwide)],
            scratch_shapes=[pltpu.VMEM((2, owned, width), BF), pltpu.SemaphoreType.DMA((2,))],
        ),
        out_shape=[
            shape((rows, width), BF),
            shape((rows, qheads * LANES), BF),
            shape((rows, kvwide), BF),
        ],
        compiler_params=params(60),
        cost_estimate=cost(2 * rows * width * wide, 4 * rows * width),
    )(sc, *shards, gain.reshape(1, width), weight, cosine, sine)


def masked(raw, first_key, lo, diagonal, query_ids):
    keys = first_key + lax.broadcasted_iota(jnp.int32, raw.shape, 0)
    ok = keys >= lo
    if diagonal:
        ok = ok & (keys <= query_ids)
    return jnp.where(ok, raw, -1e30)


def load_pairs(kp_ref, ko_ref, k_s, v_s, head, kvheads):
    rows = ko_ref.shape[0]

    @pl.when(head == 0)
    def _():
        k_s[...] = jnp.zeros_like(k_s)
        v_s[...] = jnp.zeros_like(v_s)

    for n in range(kvheads):

        @pl.when(head == n)
        def _():
            for place, ref in ((0, kp_ref), (rows, ko_ref)):
                at = n * HEAD_DIM
                k_s[place : place + rows, :HEAD_DIM] = ref[:, at : at + HEAD_DIM]
                at = (kvheads + n) * HEAD_DIM
                v_s[place : place + rows, :HEAD_DIM] = ref[:, at : at + HEAD_DIM]


def tile_parts(q_ref, lo_ref, rows, t):
    q = jnp.concatenate([q_ref[:, :LANES], q_ref[:, LANES:]], axis=0)
    lo = jnp.concatenate([lo_ref[...], lo_ref[...]], axis=1)
    ids = rows + t * TILE + lax.broadcasted_iota(jnp.int32, (1, TILE), 1)
    return q, lo, jnp.concatenate([ids, ids], axis=1)


def attend_kernel(kvheads, q_ref, kp_ref, ko_ref, lo_ref, o_ref, l_ref, k_s, v_s):
    head, t = pl.program_id(0), pl.program_id(1)
    rows = ko_ref.shape[0]
    chunks = WINDOW // TILE + 1

    @pl.when(t == 0)
    def _():
        load_pairs(kp_ref, ko_ref, k_s, v_s, head, kvheads)

    q, lo, ids = tile_parts(q_ref, lo_ref, rows, t)
    scores = []
    for c in range(chunks):
        first = pl.multiple_of((t + c) * TILE, TILE)
        raw = dot(k_s[pl.ds(first, TILE)], q, NT)
        scores.append(masked(raw, first, lo, c == chunks - 1, ids))
    top = scores[0].max(axis=0, keepdims=True)
    for s in scores[1:]:
        top = jnp.maximum(top, s.max(axis=0, keepdims=True))
    top = top * SCALE2
    total = jnp.zeros_like(top)
    mixed = jnp.zeros((LANES, 2 * TILE), F32)
    for c in range(chunks):
        first = pl.multiple_of((t + c) * TILE, TILE)
        p = jnp.exp2(scores[c] * SCALE2 - top)
        total = total + jnp.sum(p, axis=0, keepdims=True)
        mixed = mixed + dot(v_s[pl.ds(first, TILE)], p.astype(BF), TN)
    l_ref[0, 0] = top + jnp.log2(total)
    out = jnp.transpose(mixed / total).astype(BF)
    here = pl.ds(pl.multiple_of(lax.rem(t, 2) * TILE, TILE), TILE)
    for n in range(kvheads):

        @pl.when(head == n)
        def _():
            for g in range(2):
                at = (2 * n + g) * HEAD_DIM
                for copy in range(2):
                    o_ref[lax.div(t, 2), copy, here, at : at + HEAD_DIM] = out[
                        g * TILE : (g + 1) * TILE, :HEAD_DIM
                    ]


def attend(queries, pair_before, pair_here, lo, kvheads):
    rows = queries.shape[0]
    tiles = rows // TILE
    whole = pl.BlockSpec((rows, 2 * kvheads * HEAD_DIM), lambda h, t: (0, 0))
    return pl.pallas_call(
        lambda *refs: attend_kernel(kvheads, *refs),
        grid=(kvheads, tiles),
        in_specs=[
            pl.BlockSpec((TILE, 2 * LANES), lambda h, t: (t, h)),
            whole,
            whole,
            pl.BlockSpec((1, TILE), lambda h, t: (0, t)),
        ],
        out_specs=[
            pl.BlockSpec(
                (tiles // 2, 2, 2 * TILE, 2 * kvheads * HEAD_DIM), lambda h, t: (0, 0, 0, 0)
            ),
            pl.BlockSpec((1, 1, 1, 2 * TILE), lambda h, t: (h, t, 0, 0)),
        ],
        out_shape=[
            shape((tiles // 2, 2, 2 * TILE, 2 * kvheads * HEAD_DIM), BF),
            shape((kvheads, tiles, 1, 2 * TILE), F32),
        ],
        scratch_shapes=[pltpu.VMEM((2 * rows, LANES), BF), pltpu.VMEM((2 * rows, LANES), BF)],
        compiler_params=params(60),
        cost_estimate=cost(6400 * MIB, 5 * MIB, 5 * MIB),
    )(queries, pair_before, pair_here, lo)


def attend_back_kernel(
    kvheads, q_ref, kp_ref, ko_ref, lo_ref, o_ref, l_ref, do_ref, c_ref, s_ref,
    dq_ref, dp_ref, dkv_ref, k_s, v_s, dk_s, dv_s,
):
    head, t = pl.program_id(0), pl.program_id(1)
    rows = ko_ref.shape[0]
    chunks = WINDOW // TILE + 1

    @pl.when(t == 0)
    def _():
        load_pairs(kp_ref, ko_ref, k_s, v_s, head, kvheads)
        dk_s[...] = jnp.zeros_like(dk_s)
        dv_s[...] = jnp.zeros_like(dv_s)

    def heads_of(both):
        pair = both[:, : 2 * HEAD_DIM]
        for n in range(1, kvheads):
            pair = jnp.where(
                head == n, both[:, 2 * n * HEAD_DIM : 2 * (n + 1) * HEAD_DIM], pair
            )
        fill = jnp.zeros((TILE, LANES - HEAD_DIM), BF)
        first = jnp.concatenate([pair[:, :HEAD_DIM], fill], axis=1)
        second = jnp.concatenate([pair[:, HEAD_DIM:], fill], axis=1)
        return jnp.concatenate([first, second], axis=0)

    q, lo, ids = tile_parts(q_ref, lo_ref, rows, t)
    grad = heads_of(do_ref[...])
    prod = grad.astype(F32) * heads_of(o_ref[0, 0]).astype(F32)
    center = jnp.sum(jnp.transpose(prod), axis=0, keepdims=True)
    logs = l_ref[0, 0]
    dq = jnp.zeros((LANES, 2 * TILE), F32)
    for c in range(chunks):
        first = pl.multiple_of((t + c) * TILE, TILE)
        here = pl.ds(first, TILE)
        keys = k_s[here]
        raw = masked(dot(keys, q, NT), first, lo, c == chunks - 1, ids)
        p = jnp.exp2(raw * SCALE2 - logs)
        dp = dot(v_s[here], grad, NT)
        ds = (p * (dp - center)).astype(BF)
        dv_s[here] += dot(p.astype(BF), grad)
        dk_s[here] += dot(ds, q)
        dq = dq + dot(keys, ds, TN)
    cosine = jnp.concatenate([c_ref[...], c_ref[...]], axis=1)
    sine = jnp.concatenate([s_ref[...], s_ref[...]], axis=1)
    a, b = dq[:HALF] * SCALE, dq[HALF:HEAD_DIM] * SCALE
    fill = jnp.zeros((LANES - HEAD_DIM, 2 * TILE), F32)
    dq = jnp.concatenate([a * cosine + b * sine, b * cosine - a * sine, fill], axis=0)
    dq = jnp.transpose(dq).astype(BF)
    mine = pl.ds(pl.multiple_of(t * TILE, TILE), TILE)
    last = t == pl.num_programs(1) - 1
    for n in range(kvheads):

        @pl.when(head == n)
        def _():
            for g in range(2):
                at = (2 * n + g) * HEAD_DIM
                dq_ref[mine, at : at + HEAD_DIM] = dq[g * TILE : (g + 1) * TILE, :HEAD_DIM]

        @pl.when((head == n) & last)
        def _():
            at = n * HEAD_DIM
            dp_ref[:, at : at + HEAD_DIM] = (dk_s[:rows, :HEAD_DIM] * SCALE).astype(BF)
            dkv_ref[:, at : at + HEAD_DIM] = dk_s[rows:, :HEAD_DIM] * SCALE
            at = (kvheads + n) * HEAD_DIM
            dp_ref[:, at : at + HEAD_DIM] = dv_s[:rows, :HEAD_DIM].astype(BF)
            dkv_ref[:, at : at + HEAD_DIM] = dv_s[rows:, :HEAD_DIM]


def attend_back(queries, pair_before, pair_here, lo, heads_out, logs, grads, tables, kvheads):
    rows = queries.shape[0]
    tiles = rows // TILE
    wide = 2 * kvheads * HEAD_DIM
    whole = pl.BlockSpec((rows, wide), lambda h, t: (0, 0))
    table = pl.BlockSpec((HALF, TILE), lambda h, t: (0, t))
    return pl.pallas_call(
        lambda *refs: attend_back_kernel(kvheads, *refs),
        grid=(kvheads, tiles),
        in_specs=[
            pl.BlockSpec((TILE, 2 * LANES), lambda h, t: (t, h)),
            whole,
            whole,
            pl.BlockSpec((1, TILE), lambda h, t: (0, t)),
            pl.BlockSpec((1, 1, TILE, wide), lambda h, t: (lax.div(t, 2), 0, lax.rem(t, 2), 0)),
            pl.BlockSpec((1, 1, 1, 2 * TILE), lambda h, t: (h, t, 0, 0)),
            pl.BlockSpec((TILE, wide), lambda h, t: (t, 0)),
            table,
            table,
        ],
        out_specs=[whole, whole, whole],
        scratch_shapes=[
            pltpu.VMEM((2 * rows, LANES), BF),
            pltpu.VMEM((2 * rows, LANES), BF),
            pltpu.VMEM((2 * rows, LANES), F32),
            pltpu.VMEM((2 * rows, LANES), F32),
        ],
        out_shape=[shape((rows, wide), BF), shape((rows, wide), BF), shape((rows, wide), F32)],
        compiler_params=params(60),
        cost_estimate=cost(16000 * MIB, 8 * MIB, 5 * MIB),
    )(queries, pair_before, pair_here, lo, heads_out, logs, grads, *tables)


def shard(w_ref, k):
    pieces, _, part, width = w_ref.shape
    return w_ref[:, pl.ds(k, 1)].reshape(pieces * part, width)


def mix_kernel(
    sc_ref, o_ref, w_ref, x_ref, xr_ref, xl_ref, g_ref, x2_ref, h2_ref, row_ref
):
    m = pl.program_id(0)
    j = sc_ref[0]
    ways = o_ref.shape[0]
    acc = dot(o_ref[0], shard(w_ref, j))
    for k in range(1, ways):
        acc = acc + dot(o_ref[k], shard(w_ref, j ^ k))
    other = jnp.where((j & 1) == 1, xr_ref[...], xl_ref[...])
    x2 = jnp.where(m == 1, x_ref[...], other).astype(F32) + acc
    x2_ref[0] = x2
    scale = lax.rsqrt(jnp.mean(x2 * x2, axis=-1, keepdims=True) + EPSILON)
    h2_ref[0] = (x2 * scale * g_ref[...]).astype(BF)

    @pl.when(m == 1)
    def _():
        row_ref[...] = jnp.concatenate([o_ref[k] for k in range(ways)], axis=1)


def mix(sc, parts, weight, tokens, right, left, gain):
    owned, width = tokens.shape
    ways, _, local = parts.shape
    whole = lambda *dims: pl.BlockSpec(dims, lambda m, sc: (0,) * len(dims))
    return pl.pallas_call(
        mix_kernel,
        grid_spec=pltpu.PrefetchScalarGridSpec(
            num_scalar_prefetch=1,
            grid=(2,),
            in_specs=[
                pl.BlockSpec((ways, owned, local), lambda m, sc: (0, (sc[0] & 1) ^ 1 ^ m, 0)),
                whole(*weight.shape),
                whole(owned, width),
                whole(owned, width),
                whole(owned, width),
                whole(1, width),
            ],
            out_specs=[
                pl.BlockSpec((1, owned, width), lambda m, sc: (m, 0, 0)),
                pl.BlockSpec((1, owned, width), lambda m, sc: (m, 0, 0)),
                whole(owned, ways * local),
            ],
        ),
        out_shape=[
            shape((2, owned, width), F32),
            shape((2, owned, width), BF),
            shape((owned, ways * local), BF),
        ],
        compiler_params=params(60),
        cost_estimate=cost(1, 1),
    )(sc, parts, weight, tokens, right, left, gain.reshape(1, width))


def feed_kernel(
    sc_ref, ho_ref, hs_ref, co_ref, cs_ref, gu_own, d_own, w0, w1, w2, w3,
    a_ref, dg_ref, du_ref, sib_dh, own_dh, sib_y, own_y, w_s, a_s, dg_s, du_s, sem,
):
    r = pl.program_id(0)
    steps = pl.num_programs(0)
    place, odd = sc_ref[1], sc_ref[2]
    taken = [w0, w1, w2, w3]
    span = a_ref.shape[1]
    into = [pl.ds(k * span, span) for k in range(len(taken))]

    def fetch(at):
        for k, w in enumerate(taken):

            @pl.when((at == k) & (odd == 0))
            def _():
                part = pl.ds(pl.multiple_of((place ^ k) * span, span), span)
                pltpu.make_async_copy(
                    gu_own.at[:, :, part], w_s.at[pl.ds(0, 2), :, into[k]], sem.at[0, k]
                ).start()
                pltpu.make_async_copy(
                    d_own.at[:, part], w_s.at[2, :, into[k]], sem.at[1, k]
                ).start()

            @pl.when((at == k) & (odd == 1))
            def _():
                pltpu.make_async_copy(
                    w.at[pl.ds(0, 2)], w_s.at[pl.ds(0, 2), :, into[k]], sem.at[0, k]
                ).start()
                pltpu.make_async_copy(w.at[2], w_s.at[2, :, into[k]], sem.at[1, k]).start()

    @pl.when(r == 0)
    def _():
        fetch(0)

    @pl.when(r + 1 < steps)
    def _():
        fetch(r + 1)

    here = pl.ds(pl.multiple_of(r * span, span), span)
    pltpu.make_async_copy(
        w0.at[pl.ds(0, 2)], w_s.at[pl.ds(0, 2), :, here], sem.at[0, r]
    ).wait()
    pltpu.make_async_copy(w0.at[2], w_s.at[2, :, here], sem.at[1, r]).wait()
    h = jnp.concatenate([hs_ref[0], ho_ref[0]], axis=0)
    ct = jnp.concatenate([cs_ref[0], co_ref[0]], axis=0)
    gate = dot(h, w_s[0, :, here])
    up = dot(h, w_s[1, :, here])
    da = dot(ct, w_s[2, :, here])
    sig = jax.nn.sigmoid(gate)
    act = gate * sig
    a = (act * up).astype(BF)
    dgate = (da * up * sig * (1.0 + gate * (1.0 - sig))).astype(BF)
    dup = (da * act).astype(BF)
    for ref, whole, value in ((a_ref, a_s, a), (dg_ref, dg_s, dgate), (du_ref, du_s, dup)):
        ref[...] = value
        whole[:, here] = value

    @pl.when(r == steps - 1)
    def _():
        half = sib_dh.shape[0]
        for k, (dh_ref, y_ref) in enumerate(((sib_dh, sib_y), (own_dh, own_y))):
            rows = pl.ds(k * half, half)
            dh_ref[...] = (dot(dg_s[rows], w_s[0], NT) + dot(du_s[rows], w_s[1], NT)).astype(BF)
            y_ref[...] = dot(a_s[rows], w_s[2], NT).astype(BF)


def feed(m, sc, h_own, h_sib, ct_own, ct_sib, gu_own, d_own, taken):
    _, owned, width = h_own.shape
    units = d_own.shape[1]
    span = units // 4
    rows = pl.BlockSpec((1, owned, width), lambda r, sc: (m, 0, 0))
    out = pl.BlockSpec((2 * owned, span), lambda r, sc: (0, sc[1] ^ r))
    whole = pl.BlockSpec((owned, width), lambda r, sc: (0, 0))
    return pl.pallas_call(
        feed_kernel,
        grid_spec=pltpu.PrefetchScalarGridSpec(
            num_scalar_prefetch=1,
            grid=(4,),
            in_specs=[rows] * 4 + [ANY] * 6,
            out_specs=[out, out, out] + [whole] * 4,
            scratch_shapes=[pltpu.VMEM((3, width, units), BF)]
            + [pltpu.VMEM((2 * owned, units), BF)] * 3
            + [pltpu.SemaphoreType.DMA((2, 4))],
        ),
        out_shape=[shape((2 * owned, units), BF)] * 3 + [shape((owned, width), BF)] * 4,
        compiler_params=params(60),
        cost_estimate=cost(36 * owned * width * units, 22 * MIB, 2 * owned * units),
    )(sc, h_own, h_sib, ct_own, ct_sib, gu_own, d_own, *taken)


def feed_grad_kernel(
    sc_ref, ho0, hs0, co0, cs0, ho1, hs1, co1, cs1, a0, dg0, du0, a1, dg1, du1, out_ref
):
    part = ho0.shape[2]
    both = lambda x, y: jnp.concatenate([x[...], y[...]], axis=0)
    rows = lambda own, sib: jnp.concatenate([sib[0], own[0], sib[1], own[1]], axis=0)
    h = jnp.concatenate([rows(ho0, hs0), rows(ho1, hs1)], axis=1)
    ct = jnp.concatenate([rows(co0, cs0), rows(co1, cs1)], axis=1)
    for n, (left, right) in enumerate(
        ((h, both(dg0, dg1)), (h, both(du0, du1)), (ct, both(a0, a1)))
    ):
        grad = dot(left, right, TN).astype(BF)
        for k in range(2):
            out_ref[k, n] = grad[k * part : (k + 1) * part]


def feed_grad(blocks, half, sc, h_own, h_sib, ct_own, ct_sib, first, second):
    _, owned, width = h_own.shape
    units = first[0].shape[1] // 2
    part = width // 4
    cut = 2
    lanes = lambda r: pl.BlockSpec((2, owned, part), lambda n, sc: (0, 0, sc[1] ^ r))
    right = pl.BlockSpec((2 * owned, units // cut), lambda n, sc: (0, half * cut + n))
    return pl.pallas_call(
        feed_grad_kernel,
        grid_spec=pltpu.PrefetchScalarGridSpec(
            num_scalar_prefetch=1,
            grid=(cut,),
            in_specs=[lanes(blocks[0])] * 4 + [lanes(blocks[1])] * 4 + [right] * 6,
            out_specs=pl.BlockSpec((2, 3, part, units // cut), lambda n, sc: (0, 0, 0, n)),
        ),
        out_shape=shape((2, 3, part, units), BF),
        compiler_params=params(60),
        cost_estimate=cost(48 * owned * part * units, 14 * MIB),
    )(sc, *([h_own, h_sib, ct_own, ct_sib] * 2), *first, *second)


def norm_back(dn, v, gain):
    r = lax.rsqrt(jnp.mean(v * v, axis=-1, keepdims=True) + EPSILON)
    scaled = gain * dn
    gain_grad = jnp.sum(dn * (v * r), axis=0, keepdims=True)
    return r * scaled - v * (r * r * r) * jnp.mean(scaled * v, axis=-1, keepdims=True), gain_grad


def turn_back_kernel(
    sc_ref, a_ref, b_ref, z_ref, x2_ref, ct_ref, g_ref, w_ref, dx_ref, db_ref, gain_ref, do_ref
):
    dn = a_ref[...].astype(F32) + b_ref[...].astype(F32) + z_ref[...].astype(F32)
    dv, gain_grad = norm_back(dn, x2_ref[0], g_ref[...])
    gain_ref[...] = gain_grad
    dx = ct_ref[...].astype(F32) + dv
    dx_ref[...] = dx
    low = dx.astype(BF)
    db_ref[...] = low
    j = sc_ref[0]
    for d in range(do_ref.shape[0]):
        do_ref[j ^ d] = dot(low, shard(w_ref, d), NT).astype(BF)


def turn_back(sc, mine, core, tp, x2, cotangent, gain, weight):
    owned, width = cotangent.shape
    ways, local = weight.shape[1], weight.shape[0] * weight.shape[2]
    whole = lambda *dims: pl.BlockSpec(dims, lambda n, sc: (0,) * len(dims))
    own = pl.BlockSpec((1, owned, width), lambda n, sc: (1, 0, 0))
    return pl.pallas_call(
        turn_back_kernel,
        grid_spec=pltpu.PrefetchScalarGridSpec(
            num_scalar_prefetch=1,
            grid=(1,),
            in_specs=[
                whole(owned, width),
                whole(owned, width),
                whole(owned, width),
                own,
                whole(owned, width),
                whole(1, width),
                whole(*weight.shape),
            ],
            out_specs=[
                whole(owned, width),
                whole(owned, width),
                whole(1, width),
                whole(ways, owned, local),
            ],
        ),
        out_shape=[
            shape((owned, width), F32),
            shape((owned, width), BF),
            shape((1, width), F32),
            shape((ways, owned, local), BF),
        ],
        compiler_params=params(60),
        cost_estimate=cost(2 * owned * width * ways * local, 12 * MIB),
    )(sc, mine, core, tp, x2, cotangent, gain.reshape(1, width), weight)


def pair_grad_kernel(kvheads, own_ref, back_ref, c_ref, s_ref, out_ref):
    total = own_ref[...] + back_ref[...].astype(F32)
    cosine, sine = c_ref[...], s_ref[...]
    parts = []
    for n in range(kvheads):
        a = total[:, n * HEAD_DIM : n * HEAD_DIM + HALF]
        b = total[:, n * HEAD_DIM + HALF : (n + 1) * HEAD_DIM]
        parts += [a * cosine + b * sine, b * cosine - a * sine]
    parts.append(total[:, kvheads * HEAD_DIM :])
    out_ref[...] = jnp.concatenate(parts, axis=1).astype(BF)


def pair_grad(own, back, cosine, sine, kvheads):
    rows, wide = own.shape
    row = lambda n: pl.BlockSpec((TILE, n), lambda t: (t, 0))
    return pl.pallas_call(
        lambda *refs: pair_grad_kernel(kvheads, *refs),
        grid=(rows // TILE,),
        in_specs=[row(wide), row(wide), row(HALF), row(HALF)],
        out_specs=row(wide),
        out_shape=shape((rows, wide), BF),
        compiler_params=params(60),
        cost_estimate=cost(MIB, 4 * MIB),
    )(own, back, cosine, sine)


def finish_kernel(
    sc_ref, q_ref, k_ref, w_ref, v_ref, x_ref, g_ref, dx_ref, out_ref, gain_ref, acc
):
    d = pl.program_id(0)
    even = sc_ref[2] == 0
    mine = jnp.where(even, q_ref[0], k_ref[0])
    other = jnp.where(even, k_ref[0], q_ref[0])
    term = dot(mine, shard(w_ref, 0)) + dot(other, shard(v_ref, 0))

    @pl.when(d == 0)
    def _():
        acc[...] = term

    @pl.when(d > 0)
    def _():
        acc[...] += term

    @pl.when(d == pl.num_programs(0) - 1)
    def _():
        dv, gain_grad = norm_back(acc[...], x_ref[...].astype(F32), g_ref[...])
        out_ref[...] = dx_ref[...] + dv
        gain_ref[...] = gain_grad


def finish(sc, query_parts, pair_parts, weight, others, tokens, gain, dx):
    owned, width = tokens.shape
    pieces, ways, part, _ = weight.shape
    local = query_parts.shape[2]
    whole = lambda *dims: pl.BlockSpec(dims, lambda d, sc: (0,) * len(dims))
    one = pl.BlockSpec((1, owned, local), lambda d, sc: (d, 0, 0))
    half = pl.BlockSpec((pieces, 1, part, width), lambda d, sc: (0, d, 0, 0))
    return pl.pallas_call(
        finish_kernel,
        grid_spec=pltpu.PrefetchScalarGridSpec(
            num_scalar_prefetch=1,
            grid=(ways,),
            in_specs=[
                one, one, half, half, whole(owned, width), whole(1, width), whole(owned, width)
            ],
            out_specs=[whole(owned, width), whole(1, width)],
            scratch_shapes=[pltpu.VMEM((owned, width), F32)],
        ),
        out_shape=[shape((owned, width), F32), shape((1, width), F32)],
        compiler_params=params(60),
        cost_estimate=cost(1, 1),
    )(sc, query_parts, pair_parts, weight, others, tokens, gain.reshape(1, width), dx)


def tie(*values):
    return lax.optimization_barrier(values)


def hop(bit, group):
    return lambda s, t: (s ^ (bit * group), t)


def exchanged(pieces, group):
    groups = [[r + k * group for k in range(4)] for r in range(group)]
    return lax.all_to_all(
        pieces, "seq", split_axis=0, concat_axis=0, axis_index_groups=groups, tiled=True
    )


def swapped(pieces):
    return lax.all_to_all(pieces, "tp", split_axis=0, concat_axis=0, tiled=True)


def take(a, index, axis=0):
    return lax.dynamic_index_in_dim(a, index, axis, keepdims=False)


def middle_scatter(a, axis, size, group):
    middle = group // 2
    if middle == 1:
        return a
    groups = [
        [g * group + 2 * m + c for m in range(middle)] for g in range(size // group) for c in (0, 1)
    ]
    return lax.psum_scatter(
        a, "seq", scatter_dimension=axis, tiled=True, axis_index_groups=groups
    )


def gain_sum(part):
    devices = lax.axis_size("seq") * lax.axis_size("tp")
    parts = lax.all_to_all(
        part.reshape(devices, -1), AXES, split_axis=0, concat_axis=0, tiled=True
    )
    return jnp.sum(parts, axis=0)


def body(
    tokens, lengths, first_gain, w_query, w_keyval, w_output, second_gain, w_gateup, w_down,
    cotangent,
):
    size, ways = lax.axis_size("seq"), lax.axis_size("tp")
    owned, width = tokens.shape
    rows = owned * ways
    local = w_query.shape[1]
    qheads = local // HEAD_DIM
    kvheads = w_keyval.shape[2] // HEAD_DIM
    units = w_down.shape[0]
    span = units // 4
    group = size // 4
    i, j = lax.axis_index("seq"), lax.axis_index("tp")
    odd = i & 1
    place = i // group
    sc = jnp.stack([j, place, odd]).astype(jnp.int32)
    sibling = lambda s, t: (s ^ 1, t)
    partner = lambda s, t: (s, t ^ 1)

    near = lambda a: lax.dynamic_slice_in_dim(a, place * span, span, a.ndim - 1)
    far = lambda s, t: (s, t ^ 2) if s & 1 else None
    hop_odd = lambda bit: lambda s, t: (s ^ (bit * group), t) if s & 1 else None
    up = lambda a, k: send(a, lambda s, t: (s, t + 1) if t >= k else None)
    down = lambda a, k: send(a, lambda s, t: (s, t - 1) if t < ways - k else None)
    pieces = 8
    eights = [list(range(k, k + pieces)) for k in range(0, size, pieces)]

    def own_piece(w):
        part = w.shape[0] // pieces
        return lax.dynamic_slice_in_dim(w, (i % pieces) * part, part, 0)

    def gathered(parts):
        return lax.all_gather(parts, "seq", axis=0, axis_index_groups=eights)

    r1, l1 = up(tokens, 0), down(tokens, 0)
    output_mine = own_piece(w_output)
    o1, o2, o3 = (send(output_mine, lambda s, t: (s, t ^ d)) for d in (1, 2, 3))
    gateup_own = jnp.transpose(w_gateup, (1, 0, 2))
    down_own = jnp.transpose(w_down)
    r1, l1, gateup_own, down_own, w_query, w_keyval = tie(
        r1, l1, gateup_own, down_own, w_query, w_keyval
    )
    r2, l2 = up(r1, 1), down(l1, 1)
    piece = jnp.concatenate([near(gateup_own), near(down_own)[None]], axis=0)
    weight_one = jnp.concatenate(
        [spread_halves(w_query), spread_halves(w_keyval[:, 0]), w_keyval[:, 1]], axis=1
    )
    r2, l2, weight_one, piece, lengths, o1, o2, o3 = tie(
        r2, l2, weight_one, piece, lengths, o1, o2, o3
    )
    output_all = gathered(jnp.stack([output_mine, o1, o2, o3]))
    r3, l3 = up(r2, 2), down(l2, 2)
    w0 = send(piece, far)
    start_id = i * rows
    query_ids = start_id + jnp.arange(rows, dtype=jnp.int32)
    begins = doc_places(lengths, query_ids)
    cosine, sine = rotation_tables(query_ids - begins)
    lo = jnp.maximum(query_ids - (WINDOW - 1), begins) - (start_id - rows)
    lo = lo.reshape(1, rows)
    lane_cos, lane_sin = lane_tables(cosine, sine)
    turned_cos, turned_sin = jnp.transpose(cosine), jnp.transpose(sine)
    flat = jnp.concatenate(
        [jnp.transpose(w_query), jnp.transpose(w_keyval, (1, 2, 0)).reshape(-1, width)], axis=0
    )
    part = flat.shape[0] // 8
    flat_mine = lax.dynamic_slice_in_dim(flat, (4 * odd + place) * part, part, 0)
    r3, l3, lane_cos, lane_sin, turned_cos, turned_sin, lo, flat_mine = tie(
        r3, l3, lane_cos, lane_sin, turned_cos, turned_sin, lo, flat_mine
    )
    inputs_one, queries, pair_here = project(
        sc, [tokens, r1, r2, r3, l1, l2, l3], first_gain, weight_one, lane_cos, lane_sin,
        qheads, kvheads,
    )
    pair_before = send(pair_here, lambda s, t: (s + 1, t))
    pair_here, ct_late = tie(pair_here, cotangent)
    ct_partner = send(ct_late, partner)
    heads_out, logs = attend(queries, pair_before, pair_here, lo, kvheads)

    heads_out, w0 = tie(heads_out, w0)
    head_parts = swapped(heads_out.reshape(ways, 2 * owned, local))
    w1, w2, w3 = (send(w0, hop_odd(bit)) for bit in (1, 2, 3))
    head_parts, flat_mine = tie(head_parts, flat_mine)
    flat_parts = swapped(jnp.broadcast_to(flat_mine[None], (ways, *flat_mine.shape)))
    x2, h_own, heads_rows = mix(sc, head_parts, output_all, tokens, r1, l1, second_gain)
    ct_own = jnp.stack([ct_partner, cotangent])
    h_own, w1, w2, w3, ct_own = tie(h_own, w1, w2, w3, ct_own)
    h_sib = send(h_own, sibling)
    ct_sib = send(ct_own, sibling)
    h_sib, ct_sib, flat_parts = tie(h_sib, ct_sib, flat_parts)
    fours = [[r + k * group for k in range(4)] for r in range(group)]
    weight_half = lax.all_gather(flat_parts, "seq", axis=0, axis_index_groups=fours)
    fed = lambda m, h: feed(
        m, sc, h, h_sib, ct_own, ct_sib, gateup_own, down_own, (w0, w1, w2, w3)
    )
    add = lambda a, b: a.astype(F32) + b.astype(F32)
    a0, dg0, du0, sib_dh0, own_dh0, sib_y0, own_y0 = fed(0, h_own)
    core0 = send(sib_dh0, sibling)
    dh_part = add(own_dh0, core0).astype(BF)
    dh_part, h_next = tie(dh_part, h_own)
    dh_z = send(dh_part, partner)
    a1, dg1, du1, sib_dh1, own_dh1, sib_y1, own_y1 = fed(1, h_next)
    sib_dh1, dh_z = tie(sib_dh1, dh_z)
    core1 = send(sib_dh1, sibling)
    graded = lambda blocks, half, h: feed_grad(
        blocks, half, sc, h, h_sib, ct_own, ct_sib, (a0, dg0, du0), (a1, dg1, du1)
    )
    first_away, core1 = tie(graded((1, 3), 0, h_own), core1)
    first_came = send(first_away, hop(1, group))
    dx2, low, second_part, heads_grad = turn_back(
        sc, own_dh1, core1, dh_z, x2, cotangent, second_gain, output_all
    )
    grad_rows = swapped(heads_grad).reshape(rows, local)

    h_late, heads_rows, low, sib_y0, sib_y1 = tie(h_own, heads_rows, low, sib_y0, sib_y1)
    second_came = send(graded((2, 3), 1, h_late), hop(2, group))
    first_kept = graded((0, 2), 0, h_late)
    second_kept = graded((0, 1), 1, h_late)
    share = width // size
    low_parts = low.reshape(owned, size // 2, 2, share)
    low_mine = take(low_parts, odd, 2).reshape(owned, -1)
    low_came = send(take(low_parts, 1 - odd, 2).reshape(owned, -1), sibling)
    heads_sib = send(heads_rows, sibling)
    core_y = send(jnp.stack([sib_y0, sib_y1]), sibling)
    grad_rows, first_kept, second_kept, core_y, low_came, heads_sib = tie(
        grad_rows, first_kept, second_kept, core_y, low_came, heads_sib
    )
    y_z = send(add(own_y0, core_y[0]).astype(BF), partner)
    dq, dpair_before, dpair_here = attend_back(
        queries, pair_before, pair_here, lo, heads_out, logs, grad_rows,
        (turned_cos, turned_sin), kvheads,
    )
    dq, dpair_before, first_came, y_z = tie(dq, dpair_before, first_came, y_z)
    returned = send(dpair_before, lambda s, t: (s - 1, t))
    query_parts = swapped(dq.reshape(ways, owned, local))
    first_next = add(first_kept[1], first_came[1]).astype(BF)
    returned, first_next, second_came, weight_half = tie(
        returned, first_next, second_came, weight_half
    )
    first_back = send(first_next, hop(2, group))
    second_back = send(add(second_kept[1], second_came[1]).astype(BF), hop(1, group))
    weight_other = send(weight_half, sibling)
    dpair = pair_grad(dpair_here, returned, cosine, sine, kvheads)
    dpair, query_parts = tie(dpair, query_parts)
    pair_parts = swapped(dpair.reshape(ways, owned, local))

    dpair, low_mine = tie(dpair, low_mine)
    out_grad = dot(
        jnp.concatenate([low_mine, low_came], axis=0),
        jnp.concatenate([heads_rows, heads_sib], axis=0),
        TN,
    ).astype(BF)

    out_grad, first_back, second_back = tie(out_grad, first_back, second_back)
    block = jnp.concatenate(
        [
            add(first_kept[0], first_came[0]) + first_back.astype(F32),
            add(second_kept[0], second_came[0]) + second_back.astype(F32),
        ],
        axis=2,
    )
    block = middle_scatter(block, 1, size, group)
    low_block = block.astype(BF)
    cut = lambda k: lax.dynamic_slice_in_dim(low_block, k * share, share, 1)
    crossed_out, second_out = cut(1 - odd), low_block[:, share:]
    grads = jnp.concatenate([dq, dpair], axis=1)
    full = dot(inputs_one, grads, TN).astype(BF).reshape(4, -1, 2, share, 2 * local)
    full_came = send(take(full, 1 - odd, 2), sibling)
    pair_parts, full_came, crossed_out, second_out, out_grad = tie(
        pair_parts, full_came, crossed_out, second_out, out_grad
    )
    out_parts = exchanged(out_grad.reshape(4, -1, ways * local), group)
    crossed = send(crossed_out, lambda s, t: (s ^ 1, t ^ 2) if s & 1 else (s ^ 1, t))
    second = send(second_out, far)
    tokens_grad, first_part = finish(
        sc, query_parts, pair_parts, weight_half, weight_other, tokens, first_gain, dx2
    )
    first_part, full_came, own_y1 = tie(first_part, full_came, own_y1)
    one_low = add(take(full, odd, 2), full_came).astype(BF)
    one_came = [send(take(one_low, place ^ r), hop(r, group)) for r in (1, 2, 3)]
    first_part, out_parts = tie(first_part, out_parts)
    devices = size * ways
    parts = jnp.concatenate(
        [first_part.reshape(devices, -1), second_part.reshape(devices, -1)], axis=1
    )
    gains = jnp.sum(
        lax.all_to_all(parts, AXES, split_axis=0, concat_axis=0, tiled=True), axis=0
    )
    own = width // devices

    out_block = middle_scatter(jnp.sum(out_parts.astype(F32), axis=0), 0, size, group)
    out_low = out_block.astype(BF)
    columns = lambda k: lax.dynamic_slice_in_dim(out_low, k * local, local, 1)
    out_came = [send(columns(j ^ d), lambda s, t: (s, t ^ d)) for d in (1, 2, 3)]
    total = lambda first, rest: sum((a.astype(F32) for a in rest), first.astype(F32))
    output_grad = jnp.transpose(
        total(lax.dynamic_slice_in_dim(out_block, j * local, local, 1), out_came)
    )
    one_block = total(take(one_low, place), one_came)
    one_block = middle_scatter(one_block.reshape(-1, 2 * local), 0, size, group)
    query_grad = one_block[:, :local]
    keyval_grad = one_block[:, local:].reshape(share, 2, -1)
    gains, crossed, second = tie(gains, crossed, second)
    block = jnp.where(odd == 0, block[:, :share], second.astype(F32)) + crossed.astype(F32)
    gateup_grad = jnp.transpose(block[:2], (1, 0, 2))
    down_grad = jnp.transpose(block[2])
    result = (x2[1] + (add(own_y1, core_y[1]) + y_z.astype(F32))).astype(BF)
    return (
        result, tokens_grad, gains[:own], query_grad, keyval_grad, output_grad, gains[own:],
        gateup_grad, down_grad,
    )


def solution(mesh):
    return jax.shard_map(
        body,
        mesh=mesh,
        in_specs=(
            P(AXES, None), P(), P(), P(None, "tp"), P(None, None, "tp"), P("tp", None), P(),
            P(None, None, "tp"), P("tp", None), P(AXES, None),
        ),
        out_specs=(
            P(AXES, None), P(AXES, None), P(AXES), P("seq", "tp"), P("seq", None, "tp"),
            P("tp", "seq"), P(AXES), P("seq", None, "tp"), P("tp", "seq"),
        ),
        check_vma=False,
    )
```

```python
import jax
import jax.numpy as jnp
from jax import lax
from jax.experimental import pallas as pl
from jax.experimental.pallas import tpu as pltpu
from jax.sharding import PartitionSpec as P

HEAD_DIM = 96
HALF = HEAD_DIM // 2
LANES = 128
WINDOW = 1024
TILE = 256
EPSILON = 1e-05
THETA = 100000.0
SCALE = HEAD_DIM ** (-0.5)
LOG2E = 1.4426950408889634
SCALE2 = SCALE * LOG2E
BF = jnp.bfloat16
F32 = jnp.float32
NT = (((1,), (1,)), ((), ()))
NN = (((1,), (0,)), ((), ()))
TN = (((0,), (0,)), ((), ()))
MIB = 1 << 20
AXES = ("seq", "tp")
ANY = pl.BlockSpec(memory_space=pl.ANY)


def dot(a, b, dims=NN):
    return lax.dot_general(a, b, dims, preferred_element_type=F32)


def shape(dims, dtype):
    return jax.ShapeDtypeStruct(dims, dtype)


def cost(flops, moved, exps=0):
    return pl.CostEstimate(flops=flops // 16, bytes_accessed=moved // 16, transcendentals=0)


def params(mib):
    return pltpu.CompilerParams(vmem_limit_bytes=mib * MIB)


def send(a, to):
    size, ways = lax.axis_size("seq"), lax.axis_size("tp")
    pairs = []
    for s in range(size):
        for t in range(ways):
            there = to(s, t)
            if there is not None and 0 <= there[0] < size and 0 <= there[1] < ways:
                pairs.append((s * ways + t, there[0] * ways + there[1]))
    return lax.ppermute(a, AXES, pairs)


def doc_places(lengths, token_ids):
    bounds = jnp.cumsum(lengths)
    passed = token_ids[:, None] >= bounds[None, :]
    return jnp.sum(jnp.where(passed, lengths[None, :], 0), axis=1)


def spread_halves(w):
    n = w.shape[0]
    parts = w.reshape(n, -1, 2, HALF)
    parts = jnp.pad(parts, ((0, 0), (0, 0), (0, 0), (0, LANES // 2 - HALF)))
    return parts.reshape(n, -1)


def rotation_tables(places):
    freqs = THETA ** (-2.0 * jnp.arange(HALF, dtype=F32) / HEAD_DIM)
    angles = places.astype(F32)[:, None] * freqs[None, :]
    return jnp.cos(angles), jnp.sin(angles)


def lane_tables(cosine, sine):
    fill = ((0, 0), (0, LANES // 2 - HALF))
    cosine, sine = jnp.pad(cosine, fill), jnp.pad(sine, fill)
    return (
        jnp.concatenate([cosine, cosine], axis=1),
        jnp.concatenate([-sine, sine], axis=1),
    )


def project_kernel(
    sizes, sc_ref, own, r1, r2, r3, l1, l2, l3, g_ref, w_ref, c_ref, s_ref,
    h_ref, q_ref, kv_ref, x_s, sem,
):
    qheads, kvheads, ways = sizes
    o = pl.program_id(0)
    j = sc_ref[0]
    sources = {0: own, -1: r1, -2: r2, -3: r3, 1: l1, 2: l2, 3: l3}

    def fetch(at, slot):
        for d, ref in sources.items():

            @pl.when(at - j == d)
            def _():
                pltpu.make_async_copy(ref, x_s.at[slot], sem.at[slot]).start()

    @pl.when(o == 0)
    def _():
        fetch(0, 0)

    slot = lax.rem(o, 2)

    @pl.when(o + 1 < ways)
    def _():
        fetch(o + 1, 1 - slot)

    pltpu.make_async_copy(own, x_s.at[slot], sem.at[slot]).wait()
    x = x_s[slot].astype(F32)
    scale = lax.rsqrt(jnp.mean(x * x, axis=-1, keepdims=True) + EPSILON)
    h = (x * scale * g_ref[...]).astype(BF)
    h_ref[...] = h
    flat = dot(h, w_ref[...])
    cosine, sine = c_ref[...], s_ref[...]

    def turned(n):
        u = flat[:, n * LANES : (n + 1) * LANES]
        u = u * cosine + pltpu.roll(u, LANES // 2, 1) * sine
        return jnp.concatenate([u[:, :HALF], u[:, LANES // 2 : LANES // 2 + HALF]], axis=1)

    fill = jnp.zeros((x.shape[0], LANES - HEAD_DIM), F32)
    for n in range(qheads):
        q_ref[:, n * LANES : (n + 1) * LANES] = jnp.concatenate([turned(n), fill], axis=1).astype(
            BF
        )
    keys = [turned(qheads + n) for n in range(kvheads)]
    values = [flat[:, (qheads + kvheads) * LANES :]]
    kv_ref[...] = jnp.concatenate(keys + values, axis=1).astype(BF)


def project(sc, shards, gain, weight, cosine, sine, qheads, kvheads):
    owned, width = shards[0].shape
    ways = 4
    rows = owned * ways
    wide = weight.shape[1]
    kvwide = 2 * kvheads * HEAD_DIM
    row = lambda n: pl.BlockSpec((owned, n), lambda o, sc: (o, 0))
    whole = lambda m, n: pl.BlockSpec((m, n), lambda o, sc: (0, 0))
    return pl.pallas_call(
        lambda *refs: project_kernel((qheads, kvheads, ways), *refs),
        grid_spec=pltpu.PrefetchScalarGridSpec(
            num_scalar_prefetch=1,
            grid=(ways,),
            in_specs=[ANY] * 7 + [whole(1, width), whole(width, wide), row(LANES), row(LANES)],
            out_specs=[row(width), row(qheads * LANES), row(kvwide)],
            scratch_shapes=[pltpu.VMEM((2, owned, width), BF), pltpu.SemaphoreType.DMA((2,))],
        ),
        out_shape=[
            shape((rows, width), BF),
            shape((rows, qheads * LANES), BF),
            shape((rows, kvwide), BF),
        ],
        compiler_params=params(60),
        cost_estimate=cost(2 * rows * width * wide, 4 * rows * width),
    )(sc, *shards, gain.reshape(1, width), weight, cosine, sine)


def masked(raw, first_key, lo, diagonal, query_ids):
    keys = first_key + lax.broadcasted_iota(jnp.int32, raw.shape, 0)
    ok = keys >= lo
    if diagonal:
        ok = ok & (keys <= query_ids)
    return jnp.where(ok, raw, -1e30)


def load_pairs(kp_ref, ko_ref, k_s, v_s, head, kvheads):
    rows = ko_ref.shape[0]

    @pl.when(head == 0)
    def _():
        k_s[...] = jnp.zeros_like(k_s)
        v_s[...] = jnp.zeros_like(v_s)

    for n in range(kvheads):

        @pl.when(head == n)
        def _():
            for place, ref in ((0, kp_ref), (rows, ko_ref)):
                at = n * HEAD_DIM
                k_s[place : place + rows, :HEAD_DIM] = ref[:, at : at + HEAD_DIM]
                at = (kvheads + n) * HEAD_DIM
                v_s[place : place + rows, :HEAD_DIM] = ref[:, at : at + HEAD_DIM]


def tile_parts(q_ref, lo_ref, rows, t):
    q = jnp.concatenate([q_ref[:, :LANES], q_ref[:, LANES:]], axis=0)
    lo = jnp.concatenate([lo_ref[...], lo_ref[...]], axis=1)
    ids = rows + t * TILE + lax.broadcasted_iota(jnp.int32, (1, TILE), 1)
    return q, lo, jnp.concatenate([ids, ids], axis=1)


def attend_kernel(kvheads, q_ref, kp_ref, ko_ref, lo_ref, o_ref, l_ref, k_s, v_s):
    head, t = pl.program_id(0), pl.program_id(1)
    rows = ko_ref.shape[0]
    chunks = WINDOW // TILE + 1

    @pl.when(t == 0)
    def _():
        load_pairs(kp_ref, ko_ref, k_s, v_s, head, kvheads)

    q, lo, ids = tile_parts(q_ref, lo_ref, rows, t)
    scores = []
    for c in range(chunks):
        first = pl.multiple_of((t + c) * TILE, TILE)
        raw = dot(k_s[pl.ds(first, TILE)], q, NT)
        scores.append(masked(raw, first, lo, c == chunks - 1, ids))
    top = scores[0].max(axis=0, keepdims=True)
    for s in scores[1:]:
        top = jnp.maximum(top, s.max(axis=0, keepdims=True))
    top = top * SCALE2
    total = jnp.zeros_like(top)
    mixed = jnp.zeros((LANES, 2 * TILE), F32)
    for c in range(chunks):
        first = pl.multiple_of((t + c) * TILE, TILE)
        p = jnp.exp2(scores[c] * SCALE2 - top)
        total = total + jnp.sum(p, axis=0, keepdims=True)
        mixed = mixed + dot(v_s[pl.ds(first, TILE)], p.astype(BF), TN)
    l_ref[0, 0] = top + jnp.log2(total)
    out = jnp.transpose(mixed / total).astype(BF)
    here = pl.ds(pl.multiple_of(lax.rem(t, 2) * TILE, TILE), TILE)
    for n in range(kvheads):

        @pl.when(head == n)
        def _():
            for g in range(2):
                at = (2 * n + g) * HEAD_DIM
                for copy in range(2):
                    o_ref[lax.div(t, 2), copy, here, at : at + HEAD_DIM] = out[
                        g * TILE : (g + 1) * TILE, :HEAD_DIM
                    ]


def attend(queries, pair_before, pair_here, lo, kvheads):
    rows = queries.shape[0]
    tiles = rows // TILE
    whole = pl.BlockSpec((rows, 2 * kvheads * HEAD_DIM), lambda h, t: (0, 0))
    return pl.pallas_call(
        lambda *refs: attend_kernel(kvheads, *refs),
        grid=(kvheads, tiles),
        in_specs=[
            pl.BlockSpec((TILE, 2 * LANES), lambda h, t: (t, h)),
            whole,
            whole,
            pl.BlockSpec((1, TILE), lambda h, t: (0, t)),
        ],
        out_specs=[
            pl.BlockSpec(
                (tiles // 2, 2, 2 * TILE, 2 * kvheads * HEAD_DIM), lambda h, t: (0, 0, 0, 0)
            ),
            pl.BlockSpec((1, 1, 1, 2 * TILE), lambda h, t: (h, t, 0, 0)),
        ],
        out_shape=[
            shape((tiles // 2, 2, 2 * TILE, 2 * kvheads * HEAD_DIM), BF),
            shape((kvheads, tiles, 1, 2 * TILE), F32),
        ],
        scratch_shapes=[pltpu.VMEM((2 * rows, LANES), BF), pltpu.VMEM((2 * rows, LANES), BF)],
        compiler_params=params(60),
        cost_estimate=cost(6400 * MIB, 5 * MIB, 5 * MIB),
    )(queries, pair_before, pair_here, lo)


def attend_back_kernel(
    kvheads, q_ref, kp_ref, ko_ref, lo_ref, o_ref, l_ref, do_ref, c_ref, s_ref,
    dq_ref, dp_ref, dkv_ref, k_s, v_s, dk_s, dv_s,
):
    head, t = pl.program_id(0), pl.program_id(1)
    rows = ko_ref.shape[0]
    chunks = WINDOW // TILE + 1

    @pl.when(t == 0)
    def _():
        load_pairs(kp_ref, ko_ref, k_s, v_s, head, kvheads)
        dk_s[...] = jnp.zeros_like(dk_s)
        dv_s[...] = jnp.zeros_like(dv_s)

    def heads_of(both):
        pair = both[:, : 2 * HEAD_DIM]
        for n in range(1, kvheads):
            pair = jnp.where(
                head == n, both[:, 2 * n * HEAD_DIM : 2 * (n + 1) * HEAD_DIM], pair
            )
        fill = jnp.zeros((TILE, LANES - HEAD_DIM), BF)
        first = jnp.concatenate([pair[:, :HEAD_DIM], fill], axis=1)
        second = jnp.concatenate([pair[:, HEAD_DIM:], fill], axis=1)
        return jnp.concatenate([first, second], axis=0)

    q, lo, ids = tile_parts(q_ref, lo_ref, rows, t)
    grad = heads_of(do_ref[...])
    prod = grad.astype(F32) * heads_of(o_ref[0, 0]).astype(F32)
    center = jnp.sum(jnp.transpose(prod), axis=0, keepdims=True)
    logs = l_ref[0, 0]
    dq = jnp.zeros((LANES, 2 * TILE), F32)
    for c in range(chunks):
        first = pl.multiple_of((t + c) * TILE, TILE)
        here = pl.ds(first, TILE)
        keys = k_s[here]
        raw = masked(dot(keys, q, NT), first, lo, c == chunks - 1, ids)
        p = jnp.exp2(raw * SCALE2 - logs)
        dp = dot(v_s[here], grad, NT)
        ds = (p * (dp - center)).astype(BF)
        dv_s[here] += dot(p.astype(BF), grad)
        dk_s[here] += dot(ds, q)
        dq = dq + dot(keys, ds, TN)
    cosine = jnp.concatenate([c_ref[...], c_ref[...]], axis=1)
    sine = jnp.concatenate([s_ref[...], s_ref[...]], axis=1)
    a, b = dq[:HALF] * SCALE, dq[HALF:HEAD_DIM] * SCALE
    fill = jnp.zeros((LANES - HEAD_DIM, 2 * TILE), F32)
    dq = jnp.concatenate([a * cosine + b * sine, b * cosine - a * sine, fill], axis=0)
    dq = jnp.transpose(dq).astype(BF)
    mine = pl.ds(pl.multiple_of(t * TILE, TILE), TILE)
    last = t == pl.num_programs(1) - 1
    for n in range(kvheads):

        @pl.when(head == n)
        def _():
            for g in range(2):
                at = (2 * n + g) * HEAD_DIM
                dq_ref[mine, at : at + HEAD_DIM] = dq[g * TILE : (g + 1) * TILE, :HEAD_DIM]

        @pl.when((head == n) & last)
        def _():
            at = n * HEAD_DIM
            dp_ref[:, at : at + HEAD_DIM] = (dk_s[:rows, :HEAD_DIM] * SCALE).astype(BF)
            dkv_ref[:, at : at + HEAD_DIM] = dk_s[rows:, :HEAD_DIM] * SCALE
            at = (kvheads + n) * HEAD_DIM
            dp_ref[:, at : at + HEAD_DIM] = dv_s[:rows, :HEAD_DIM].astype(BF)
            dkv_ref[:, at : at + HEAD_DIM] = dv_s[rows:, :HEAD_DIM]


def attend_back(queries, pair_before, pair_here, lo, heads_out, logs, grads, tables, kvheads):
    rows = queries.shape[0]
    tiles = rows // TILE
    wide = 2 * kvheads * HEAD_DIM
    whole = pl.BlockSpec((rows, wide), lambda h, t: (0, 0))
    table = pl.BlockSpec((HALF, TILE), lambda h, t: (0, t))
    return pl.pallas_call(
        lambda *refs: attend_back_kernel(kvheads, *refs),
        grid=(kvheads, tiles),
        in_specs=[
            pl.BlockSpec((TILE, 2 * LANES), lambda h, t: (t, h)),
            whole,
            whole,
            pl.BlockSpec((1, TILE), lambda h, t: (0, t)),
            pl.BlockSpec((1, 1, TILE, wide), lambda h, t: (lax.div(t, 2), 0, lax.rem(t, 2), 0)),
            pl.BlockSpec((1, 1, 1, 2 * TILE), lambda h, t: (h, t, 0, 0)),
            pl.BlockSpec((TILE, wide), lambda h, t: (t, 0)),
            table,
            table,
        ],
        out_specs=[whole, whole, whole],
        scratch_shapes=[
            pltpu.VMEM((2 * rows, LANES), BF),
            pltpu.VMEM((2 * rows, LANES), BF),
            pltpu.VMEM((2 * rows, LANES), F32),
            pltpu.VMEM((2 * rows, LANES), F32),
        ],
        out_shape=[shape((rows, wide), BF), shape((rows, wide), BF), shape((rows, wide), F32)],
        compiler_params=params(60),
        cost_estimate=cost(16000 * MIB, 8 * MIB, 5 * MIB),
    )(queries, pair_before, pair_here, lo, heads_out, logs, grads, *tables)


def shard(w_ref, k):
    pieces, _, part, width = w_ref.shape
    return w_ref[:, pl.ds(k, 1)].reshape(pieces * part, width)


def mix_kernel(
    sc_ref, o_ref, w_ref, x_ref, xr_ref, xl_ref, g_ref, x2_ref, h2_ref, row_ref
):
    m = pl.program_id(0)
    j = sc_ref[0]
    ways = o_ref.shape[0]
    acc = dot(o_ref[0], shard(w_ref, j))
    for k in range(1, ways):
        acc = acc + dot(o_ref[k], shard(w_ref, j ^ k))
    other = jnp.where((j & 1) == 1, xr_ref[...], xl_ref[...])
    x2 = jnp.where(m == 1, x_ref[...], other).astype(F32) + acc
    scale = lax.rsqrt(jnp.mean(x2 * x2, axis=-1, keepdims=True) + EPSILON)
    h2_ref[0] = (x2 * scale * g_ref[...]).astype(BF)

    @pl.when(m == 1)
    def _():
        x2_ref[...] = x2
        row_ref[...] = jnp.concatenate([o_ref[k] for k in range(ways)], axis=1)


def mix(sc, parts, weight, tokens, right, left, gain):
    owned, width = tokens.shape
    ways, _, local = parts.shape
    whole = lambda *dims: pl.BlockSpec(dims, lambda m, sc: (0,) * len(dims))
    return pl.pallas_call(
        mix_kernel,
        grid_spec=pltpu.PrefetchScalarGridSpec(
            num_scalar_prefetch=1,
            grid=(2,),
            in_specs=[
                pl.BlockSpec((ways, owned, local), lambda m, sc: (0, (sc[0] & 1) ^ 1 ^ m, 0)),
                whole(*weight.shape),
                whole(owned, width),
                whole(owned, width),
                whole(owned, width),
                whole(1, width),
            ],
            out_specs=[
                whole(owned, width),
                pl.BlockSpec((1, owned, width), lambda m, sc: (m, 0, 0)),
                whole(owned, ways * local),
            ],
        ),
        out_shape=[
            shape((owned, width), F32),
            shape((2, owned, width), BF),
            shape((owned, ways * local), BF),
        ],
        compiler_params=params(60),
        cost_estimate=cost(1, 1),
    )(sc, parts, weight, tokens, right, left, gain.reshape(1, width))


def feed_kernel(
    sc_ref, ho_ref, hs_ref, co_ref, cs_ref, gu_own, d_own, w0, w1, w2, w3,
    a_ref, dg_ref, du_ref, sib_dh, own_dh, sib_y, own_y, w_s, a_s, dg_s, du_s, sem,
):
    r = pl.program_id(0)
    steps = pl.num_programs(0)
    place, odd = sc_ref[1], sc_ref[2]
    taken = [w0, w1, w2, w3]
    span = a_ref.shape[1]
    into = [pl.ds(k * span, span) for k in range(len(taken))]

    def fetch(at):
        for k, w in enumerate(taken):

            @pl.when((at == k) & (odd == 0))
            def _():
                part = pl.ds(pl.multiple_of((place ^ k) * span, span), span)
                pltpu.make_async_copy(
                    gu_own.at[:, :, part], w_s.at[pl.ds(0, 2), :, into[k]], sem.at[0, k]
                ).start()
                pltpu.make_async_copy(
                    d_own.at[:, part], w_s.at[2, :, into[k]], sem.at[1, k]
                ).start()

            @pl.when((at == k) & (odd == 1))
            def _():
                pltpu.make_async_copy(
                    w.at[pl.ds(0, 2)], w_s.at[pl.ds(0, 2), :, into[k]], sem.at[0, k]
                ).start()
                pltpu.make_async_copy(w.at[2], w_s.at[2, :, into[k]], sem.at[1, k]).start()

    @pl.when(r == 0)
    def _():
        fetch(0)

    @pl.when(r + 1 < steps)
    def _():
        fetch(r + 1)

    here = pl.ds(pl.multiple_of(r * span, span), span)
    pltpu.make_async_copy(
        w0.at[pl.ds(0, 2)], w_s.at[pl.ds(0, 2), :, here], sem.at[0, r]
    ).wait()
    pltpu.make_async_copy(w0.at[2], w_s.at[2, :, here], sem.at[1, r]).wait()
    h = jnp.concatenate([hs_ref[0], ho_ref[0]], axis=0)
    ct = jnp.concatenate([cs_ref[0], co_ref[0]], axis=0)
    gate = dot(h, w_s[0, :, here])
    up = dot(h, w_s[1, :, here])
    da = dot(ct, w_s[2, :, here])
    sig = jax.nn.sigmoid(gate)
    act = gate * sig
    a = (act * up).astype(BF)
    dgate = (da * up * sig * (1.0 + gate * (1.0 - sig))).astype(BF)
    dup = (da * act).astype(BF)
    for ref, whole, value in ((a_ref, a_s, a), (dg_ref, dg_s, dgate), (du_ref, du_s, dup)):
        ref[...] = value
        whole[:, here] = value

    @pl.when(r == steps - 1)
    def _():
        half = sib_dh.shape[0]
        for k, (dh_ref, y_ref) in enumerate(((sib_dh, sib_y), (own_dh, own_y))):
            rows = pl.ds(k * half, half)
            dh_ref[...] = (dot(dg_s[rows], w_s[0], NT) + dot(du_s[rows], w_s[1], NT)).astype(BF)
            y_ref[...] = dot(a_s[rows], w_s[2], NT).astype(BF)


def feed(m, sc, h_own, h_sib, ct_own, ct_sib, gu_own, d_own, taken):
    _, owned, width = h_own.shape
    units = d_own.shape[1]
    span = units // 4
    rows = pl.BlockSpec((1, owned, width), lambda r, sc: (m, 0, 0))
    out = pl.BlockSpec((2 * owned, span), lambda r, sc: (0, sc[1] ^ r))
    whole = pl.BlockSpec((owned, width), lambda r, sc: (0, 0))
    return pl.pallas_call(
        feed_kernel,
        grid_spec=pltpu.PrefetchScalarGridSpec(
            num_scalar_prefetch=1,
            grid=(4,),
            in_specs=[rows] * 4 + [ANY] * 6,
            out_specs=[out, out, out] + [whole] * 4,
            scratch_shapes=[pltpu.VMEM((3, width, units), BF)]
            + [pltpu.VMEM((2 * owned, units), BF)] * 3
            + [pltpu.SemaphoreType.DMA((2, 4))],
        ),
        out_shape=[shape((2 * owned, units), BF)] * 3 + [shape((owned, width), BF)] * 4,
        compiler_params=params(60),
        cost_estimate=cost(36 * owned * width * units, 22 * MIB, 2 * owned * units),
    )(sc, h_own, h_sib, ct_own, ct_sib, gu_own, d_own, *taken)


def feed_grad_kernel(
    sc_ref, ho0, hs0, co0, cs0, ho1, hs1, co1, cs1, a0, dg0, du0, a1, dg1, du1, out_ref
):
    part = ho0.shape[2]
    both = lambda x, y: jnp.concatenate([x[...], y[...]], axis=0)
    rows = lambda own, sib: jnp.concatenate([sib[0], own[0], sib[1], own[1]], axis=0)
    h = jnp.concatenate([rows(ho0, hs0), rows(ho1, hs1)], axis=1)
    ct = jnp.concatenate([rows(co0, cs0), rows(co1, cs1)], axis=1)
    for n, (left, right) in enumerate(
        ((h, both(dg0, dg1)), (h, both(du0, du1)), (ct, both(a0, a1)))
    ):
        grad = dot(left, right, TN).astype(BF)
        for k in range(2):
            out_ref[k, n] = grad[k * part : (k + 1) * part]


def feed_grad(blocks, half, sc, h_own, h_sib, ct_own, ct_sib, first, second):
    _, owned, width = h_own.shape
    units = first[0].shape[1] // 2
    part = width // 4
    cut = 2
    lanes = lambda r: pl.BlockSpec((2, owned, part), lambda n, sc: (0, 0, sc[1] ^ r))
    right = pl.BlockSpec((2 * owned, units // cut), lambda n, sc: (0, half * cut + n))
    return pl.pallas_call(
        feed_grad_kernel,
        grid_spec=pltpu.PrefetchScalarGridSpec(
            num_scalar_prefetch=1,
            grid=(cut,),
            in_specs=[lanes(blocks[0])] * 4 + [lanes(blocks[1])] * 4 + [right] * 6,
            out_specs=pl.BlockSpec((2, 3, part, units // cut), lambda n, sc: (0, 0, 0, n)),
        ),
        out_shape=shape((2, 3, part, units), BF),
        compiler_params=params(60),
        cost_estimate=cost(48 * owned * part * units, 14 * MIB),
    )(sc, *([h_own, h_sib, ct_own, ct_sib] * 2), *first, *second)


def norm_back(dn, v, gain):
    r = lax.rsqrt(jnp.mean(v * v, axis=-1, keepdims=True) + EPSILON)
    scaled = gain * dn
    gain_grad = jnp.sum(dn * (v * r), axis=0, keepdims=True)
    return r * scaled - v * (r * r * r) * jnp.mean(scaled * v, axis=-1, keepdims=True), gain_grad


def turn_back_kernel(
    sc_ref, a_ref, b_ref, z_ref, x2_ref, ct_ref, g_ref, w_ref, dx_ref, db_ref, gain_ref, do_ref
):
    dn = a_ref[...].astype(F32) + b_ref[...].astype(F32) + z_ref[...].astype(F32)
    dv, gain_grad = norm_back(dn, x2_ref[...], g_ref[...])
    gain_ref[...] = gain_grad
    dx = ct_ref[...].astype(F32) + dv
    dx_ref[...] = dx
    low = dx.astype(BF)
    db_ref[...] = low
    j = sc_ref[0]
    for d in range(do_ref.shape[0]):
        do_ref[j ^ d] = dot(low, shard(w_ref, d), NT).astype(BF)


def turn_back(sc, mine, core, tp, x2, cotangent, gain, weight):
    owned, width = cotangent.shape
    ways, local = weight.shape[1], weight.shape[0] * weight.shape[2]
    whole = lambda *dims: pl.BlockSpec(dims, lambda n, sc: (0,) * len(dims))
    return pl.pallas_call(
        turn_back_kernel,
        grid_spec=pltpu.PrefetchScalarGridSpec(
            num_scalar_prefetch=1,
            grid=(1,),
            in_specs=[
                whole(owned, width),
                whole(owned, width),
                whole(owned, width),
                whole(owned, width),
                whole(owned, width),
                whole(1, width),
                whole(*weight.shape),
            ],
            out_specs=[
                whole(owned, width),
                whole(owned, width),
                whole(1, width),
                whole(ways, owned, local),
            ],
        ),
        out_shape=[
            shape((owned, width), F32),
            shape((owned, width), BF),
            shape((1, width), F32),
            shape((ways, owned, local), BF),
        ],
        compiler_params=params(60),
        cost_estimate=cost(2 * owned * width * ways * local, 12 * MIB),
    )(sc, mine, core, tp, x2, cotangent, gain.reshape(1, width), weight)


def pair_grad_kernel(kvheads, own_ref, back_ref, c_ref, s_ref, out_ref):
    total = own_ref[...] + back_ref[...].astype(F32)
    cosine, sine = c_ref[...], s_ref[...]
    parts = []
    for n in range(kvheads):
        a = total[:, n * HEAD_DIM : n * HEAD_DIM + HALF]
        b = total[:, n * HEAD_DIM + HALF : (n + 1) * HEAD_DIM]
        parts += [a * cosine + b * sine, b * cosine - a * sine]
    parts.append(total[:, kvheads * HEAD_DIM :])
    out_ref[...] = jnp.concatenate(parts, axis=1).astype(BF)


def pair_grad(own, back, cosine, sine, kvheads):
    rows, wide = own.shape
    row = lambda n: pl.BlockSpec((TILE, n), lambda t: (t, 0))
    return pl.pallas_call(
        lambda *refs: pair_grad_kernel(kvheads, *refs),
        grid=(rows // TILE,),
        in_specs=[row(wide), row(wide), row(HALF), row(HALF)],
        out_specs=row(wide),
        out_shape=shape((rows, wide), BF),
        compiler_params=params(60),
        cost_estimate=cost(MIB, 4 * MIB),
    )(own, back, cosine, sine)


def finish_kernel(
    sc_ref, q_ref, k_ref, w_ref, v_ref, x_ref, g_ref, dx_ref, out_ref, gain_ref, acc
):
    d = pl.program_id(0)
    even = sc_ref[2] == 0
    mine = jnp.where(even, q_ref[0], k_ref[0])
    other = jnp.where(even, k_ref[0], q_ref[0])
    term = dot(mine, shard(w_ref, 0)) + dot(other, shard(v_ref, 0))

    @pl.when(d == 0)
    def _():
        acc[...] = term

    @pl.when(d > 0)
    def _():
        acc[...] += term

    @pl.when(d == pl.num_programs(0) - 1)
    def _():
        dv, gain_grad = norm_back(acc[...], x_ref[...].astype(F32), g_ref[...])
        out_ref[...] = dx_ref[...] + dv
        gain_ref[...] = gain_grad


def finish(sc, query_parts, pair_parts, weight, others, tokens, gain, dx):
    owned, width = tokens.shape
    pieces, ways, part, _ = weight.shape
    local = query_parts.shape[2]
    whole = lambda *dims: pl.BlockSpec(dims, lambda d, sc: (0,) * len(dims))
    one = pl.BlockSpec((1, owned, local), lambda d, sc: (d, 0, 0))
    half = pl.BlockSpec((pieces, 1, part, width), lambda d, sc: (0, d, 0, 0))
    return pl.pallas_call(
        finish_kernel,
        grid_spec=pltpu.PrefetchScalarGridSpec(
            num_scalar_prefetch=1,
            grid=(ways,),
            in_specs=[
                one, one, half, half, whole(owned, width), whole(1, width), whole(owned, width)
            ],
            out_specs=[whole(owned, width), whole(1, width)],
            scratch_shapes=[pltpu.VMEM((owned, width), F32)],
        ),
        out_shape=[shape((owned, width), F32), shape((1, width), F32)],
        compiler_params=params(60),
        cost_estimate=cost(1, 1),
    )(sc, query_parts, pair_parts, weight, others, tokens, gain.reshape(1, width), dx)


def tie(*values):
    return lax.optimization_barrier(values)


def hop(bit, group):
    return lambda s, t: (s ^ (bit * group), t)


def exchanged(pieces, group):
    groups = [[r + k * group for k in range(4)] for r in range(group)]
    return lax.all_to_all(
        pieces, "seq", split_axis=0, concat_axis=0, axis_index_groups=groups, tiled=True
    )


def swapped(pieces):
    return lax.all_to_all(pieces, "tp", split_axis=0, concat_axis=0, tiled=True)


def take(a, index, axis=0):
    return lax.dynamic_index_in_dim(a, index, axis, keepdims=False)


def middle_scatter(a, axis, size, group):
    middle = group // 2
    if middle == 1:
        return a
    groups = [
        [g * group + 2 * m + c for m in range(middle)] for g in range(size // group) for c in (0, 1)
    ]
    return lax.psum_scatter(
        a, "seq", scatter_dimension=axis, tiled=True, axis_index_groups=groups
    )


def gain_sum(part):
    devices = lax.axis_size("seq") * lax.axis_size("tp")
    parts = lax.all_to_all(
        part.reshape(devices, -1), AXES, split_axis=0, concat_axis=0, tiled=True
    )
    return jnp.sum(parts, axis=0)


def body(
    tokens, lengths, first_gain, w_query, w_keyval, w_output, second_gain, w_gateup, w_down,
    cotangent,
):
    size, ways = lax.axis_size("seq"), lax.axis_size("tp")
    owned, width = tokens.shape
    rows = owned * ways
    local = w_query.shape[1]
    qheads = local // HEAD_DIM
    kvheads = w_keyval.shape[2] // HEAD_DIM
    units = w_down.shape[0]
    span = units // 4
    group = size // 4
    i, j = lax.axis_index("seq"), lax.axis_index("tp")
    odd = i & 1
    place = i // group
    sc = jnp.stack([j, place, odd]).astype(jnp.int32)
    sibling = lambda s, t: (s ^ 1, t)
    partner = lambda s, t: (s, t ^ 1)

    near = lambda a: lax.dynamic_slice_in_dim(a, place * span, span, a.ndim - 1)
    far = lambda s, t: (s, t ^ 2) if s & 1 else None
    hop_odd = lambda bit: lambda s, t: (s ^ (bit * group), t) if s & 1 else None
    up = lambda a, k: send(a, lambda s, t: (s, t + 1) if t >= k else None)
    down = lambda a, k: send(a, lambda s, t: (s, t - 1) if t < ways - k else None)
    pieces = 8
    eights = [list(range(k, k + pieces)) for k in range(0, size, pieces)]

    def own_piece(w):
        part = w.shape[0] // pieces
        return lax.dynamic_slice_in_dim(w, (i % pieces) * part, part, 0)

    def gathered(parts):
        return lax.all_gather(parts, "seq", axis=0, axis_index_groups=eights)

    r1, l1 = up(tokens, 0), down(tokens, 0)
    output_mine = own_piece(w_output)
    o1, o2, o3 = (send(output_mine, lambda s, t: (s, t ^ d)) for d in (1, 2, 3))
    gateup_own = jnp.transpose(w_gateup, (1, 0, 2))
    down_own = jnp.transpose(w_down)
    r1, l1, gateup_own, down_own, w_query, w_keyval = tie(
        r1, l1, gateup_own, down_own, w_query, w_keyval
    )
    r2, l2 = up(r1, 1), down(l1, 1)
    piece = jnp.concatenate([near(gateup_own), near(down_own)[None]], axis=0)
    weight_one = jnp.concatenate(
        [spread_halves(w_query), spread_halves(w_keyval[:, 0]), w_keyval[:, 1]], axis=1
    )
    r2, l2, weight_one, piece, lengths, o1, o2, o3 = tie(
        r2, l2, weight_one, piece, lengths, o1, o2, o3
    )
    output_all = gathered(jnp.stack([output_mine, o1, o2, o3]))
    r3, l3 = up(r2, 2), down(l2, 2)
    w0 = send(piece, far)
    start_id = i * rows
    query_ids = start_id + jnp.arange(rows, dtype=jnp.int32)
    begins = doc_places(lengths, query_ids)
    cosine, sine = rotation_tables(query_ids - begins)
    lo = jnp.maximum(query_ids - (WINDOW - 1), begins) - (start_id - rows)
    lo = lo.reshape(1, rows)
    lane_cos, lane_sin = lane_tables(cosine, sine)
    turned_cos, turned_sin = jnp.transpose(cosine), jnp.transpose(sine)
    flat = jnp.concatenate(
        [jnp.transpose(w_query), jnp.transpose(w_keyval, (1, 2, 0)).reshape(-1, width)], axis=0
    )
    part = flat.shape[0] // 8
    flat_mine = lax.dynamic_slice_in_dim(flat, (4 * odd + place) * part, part, 0)
    r3, l3, lane_cos, lane_sin, turned_cos, turned_sin, lo, flat_mine = tie(
        r3, l3, lane_cos, lane_sin, turned_cos, turned_sin, lo, flat_mine
    )
    inputs_one, queries, pair_here = project(
        sc, [tokens, r1, r2, r3, l1, l2, l3], first_gain, weight_one, lane_cos, lane_sin,
        qheads, kvheads,
    )
    pair_before = send(pair_here, lambda s, t: (s + 1, t))
    pair_here, ct_late = tie(pair_here, cotangent)
    ct_partner = send(ct_late, partner)
    heads_out, logs = attend(queries, pair_before, pair_here, lo, kvheads)

    heads_out, w0 = tie(heads_out, w0)
    head_parts = swapped(heads_out.reshape(ways, 2 * owned, local))
    w1, w2, w3 = (send(w0, hop_odd(bit)) for bit in (1, 2, 3))
    head_parts, flat_mine = tie(head_parts, flat_mine)
    flat_parts = swapped(jnp.broadcast_to(flat_mine[None], (ways, *flat_mine.shape)))
    x2, h_own, heads_rows = mix(sc, head_parts, output_all, tokens, r1, l1, second_gain)
    ct_own = jnp.stack([ct_partner, cotangent])
    h_own, w1, w2, w3, ct_own = tie(h_own, w1, w2, w3, ct_own)
    h_sib = send(h_own, sibling)
    ct_sib = send(ct_own, sibling)
    h_sib, ct_sib, flat_parts = tie(h_sib, ct_sib, flat_parts)
    fours = [[r + k * group for k in range(4)] for r in range(group)]
    weight_half = lax.all_gather(flat_parts, "seq", axis=0, axis_index_groups=fours)
    fed = lambda m, h: feed(
        m, sc, h, h_sib, ct_own, ct_sib, gateup_own, down_own, (w0, w1, w2, w3)
    )
    add = lambda a, b: a.astype(F32) + b.astype(F32)
    a0, dg0, du0, sib_dh0, own_dh0, sib_y0, own_y0 = fed(0, h_own)
    core0 = send(sib_dh0, sibling)
    dh_part = add(own_dh0, core0).astype(BF)
    dh_part, h_next = tie(dh_part, h_own)
    dh_z = send(dh_part, partner)
    a1, dg1, du1, sib_dh1, own_dh1, sib_y1, own_y1 = fed(1, h_next)
    sib_dh1, dh_z = tie(sib_dh1, dh_z)
    core1 = send(sib_dh1, sibling)
    graded = lambda blocks, half, h: feed_grad(
        blocks, half, sc, h, h_sib, ct_own, ct_sib, (a0, dg0, du0), (a1, dg1, du1)
    )
    first_away, core1 = tie(graded((1, 3), 0, h_own), core1)
    first_came = send(first_away, hop(1, group))
    dx2, low, second_part, heads_grad = turn_back(
        sc, own_dh1, core1, dh_z, x2, cotangent, second_gain, output_all
    )
    grad_rows = swapped(heads_grad).reshape(rows, local)

    h_late, heads_rows, low, sib_y0, sib_y1 = tie(h_own, heads_rows, low, sib_y0, sib_y1)
    second_came = send(graded((2, 3), 1, h_late), hop(2, group))
    first_kept = graded((0, 2), 0, h_late)
    second_kept = graded((0, 1), 1, h_late)
    share = width // size
    low_parts = low.reshape(owned, size // 2, 2, share)
    low_mine = take(low_parts, odd, 2).reshape(owned, -1)
    low_came = send(take(low_parts, 1 - odd, 2).reshape(owned, -1), sibling)
    heads_sib = send(heads_rows, sibling)
    core_y = send(jnp.stack([sib_y0, sib_y1]), sibling)
    grad_rows, first_kept, second_kept, core_y, low_came, heads_sib = tie(
        grad_rows, first_kept, second_kept, core_y, low_came, heads_sib
    )
    y_z = send(add(own_y0, core_y[0]).astype(BF), partner)
    dq, dpair_before, dpair_here = attend_back(
        queries, pair_before, pair_here, lo, heads_out, logs, grad_rows,
        (turned_cos, turned_sin), kvheads,
    )
    dq, dpair_before, first_came, y_z = tie(dq, dpair_before, first_came, y_z)
    returned = send(dpair_before, lambda s, t: (s - 1, t))
    query_parts = swapped(dq.reshape(ways, owned, local))
    first_next = add(first_kept[1], first_came[1]).astype(BF)
    returned, first_next, second_came, weight_half = tie(
        returned, first_next, second_came, weight_half
    )
    first_back = send(first_next, hop(2, group))
    second_back = send(add(second_kept[1], second_came[1]).astype(BF), hop(1, group))
    weight_other = send(weight_half, sibling)
    dpair = pair_grad(dpair_here, returned, cosine, sine, kvheads)
    dpair, query_parts = tie(dpair, query_parts)
    pair_parts = swapped(dpair.reshape(ways, owned, local))

    dpair, low_mine = tie(dpair, low_mine)
    out_grad = dot(
        jnp.concatenate([low_mine, low_came], axis=0),
        jnp.concatenate([heads_rows, heads_sib], axis=0),
        TN,
    ).astype(BF)

    out_grad, first_back, second_back = tie(out_grad, first_back, second_back)
    block = jnp.concatenate(
        [
            add(first_kept[0], first_came[0]) + first_back.astype(F32),
            add(second_kept[0], second_came[0]) + second_back.astype(F32),
        ],
        axis=2,
    )
    block = middle_scatter(block, 1, size, group)
    low_block = block.astype(BF)
    cut = lambda k: lax.dynamic_slice_in_dim(low_block, k * share, share, 1)
    crossed_out, second_out = cut(1 - odd), low_block[:, share:]
    grads = jnp.concatenate([dq, dpair], axis=1)
    full = dot(inputs_one, grads, TN).astype(BF).reshape(4, -1, 2, share, 2 * local)
    full_came = send(take(full, 1 - odd, 2), sibling)
    pair_parts, full_came, crossed_out, second_out, out_grad = tie(
        pair_parts, full_came, crossed_out, second_out, out_grad
    )
    out_parts = exchanged(out_grad.reshape(4, -1, ways * local), group)
    crossed = send(crossed_out, lambda s, t: (s ^ 1, t ^ 2) if s & 1 else (s ^ 1, t))
    second = send(second_out, far)
    tokens_grad, first_part = finish(
        sc, query_parts, pair_parts, weight_half, weight_other, tokens, first_gain, dx2
    )
    first_part, full_came, own_y1 = tie(first_part, full_came, own_y1)
    one_low = add(take(full, odd, 2), full_came).astype(BF)
    one_came = [send(take(one_low, place ^ r), hop(r, group)) for r in (1, 2, 3)]
    first_part, out_parts = tie(first_part, out_parts)
    devices = size * ways
    parts = jnp.concatenate(
        [first_part.reshape(devices, -1), second_part.reshape(devices, -1)], axis=1
    )
    gains = jnp.sum(
        lax.all_to_all(parts, AXES, split_axis=0, concat_axis=0, tiled=True), axis=0
    )
    own = width // devices

    out_block = middle_scatter(jnp.sum(out_parts.astype(F32), axis=0), 0, size, group)
    out_low = out_block.astype(BF)
    columns = lambda k: lax.dynamic_slice_in_dim(out_low, k * local, local, 1)
    out_came = [send(columns(j ^ d), lambda s, t: (s, t ^ d)) for d in (1, 2, 3)]
    total = lambda first, rest: sum((a.astype(F32) for a in rest), first.astype(F32))
    output_grad = jnp.transpose(
        total(lax.dynamic_slice_in_dim(out_block, j * local, local, 1), out_came)
    )
    one_block = total(take(one_low, place), one_came)
    one_block = middle_scatter(one_block.reshape(-1, 2 * local), 0, size, group)
    query_grad = one_block[:, :local]
    keyval_grad = one_block[:, local:].reshape(share, 2, -1)
    gains, crossed, second = tie(gains, crossed, second)
    block = jnp.where(odd == 0, block[:, :share], second.astype(F32)) + crossed.astype(F32)
    gateup_grad = jnp.transpose(block[:2], (1, 0, 2))
    down_grad = jnp.transpose(block[2])
    result = (x2 + (add(own_y1, core_y[1]) + y_z.astype(F32))).astype(BF)
    return (
        result, tokens_grad, gains[:own], query_grad, keyval_grad, output_grad, gains[own:],
        gateup_grad, down_grad,
    )


def solution(mesh):
    return jax.shard_map(
        body,
        mesh=mesh,
        in_specs=(
            P(AXES, None), P(), P(), P(None, "tp"), P(None, None, "tp"), P("tp", None), P(),
            P(None, None, "tp"), P("tp", None), P(AXES, None),
        ),
        out_specs=(
            P(AXES, None), P(AXES, None), P(AXES), P("seq", "tp"), P("seq", None, "tp"),
            P("tp", "seq"), P(AXES), P("seq", None, "tp"), P("tp", "seq"),
        ),
        check_vma=False,
    )
```
